32 devices in a mesh: dp: 16 (over z, y, x), tensor: 2 (over core).
Axes of the slice: x: 2, y: 2, z: 4, core: 2. Of those that a mesh axis runs over, the one named last changes fastest.
Arguments:
- tokens: bfloat16 [6144, 2048], P(('dp', 'tensor')), may hold values from -6 to 6
- segments: int32 [6144], P('dp'), may hold values from 0 to 31, never falling along the last dimension, each value on 1 to 384 neighbouring positions
- decay: float32 [8], P('tensor'), may hold values from 0.0005 to 0.03
- norm1_gain: float32 [2048], replicated, may hold values from 0.5 to 1.5
- w_query: bfloat16 [2048, 2048], P('dp', 'tensor'), may hold values from -0.110485435 to 0.110485435
- w_key: bfloat16 [2048, 2048], P('dp', 'tensor'), may hold values from -0.15467961 to 0.15467961
- w_value: bfloat16 [2048, 4096], P('dp', 'tensor'), may hold values from -0.125 to 0.125
- w_swish: bfloat16 [2048, 4096], P('dp', 'tensor'), may hold values from -0.125 to 0.125
- w_out: bfloat16 [4096, 2048], P('tensor', 'dp'), may hold values from -0.09375 to 0.09375
- norm2_gain: float32 [2048], replicated, may hold values from 0.5 to 1.5
- w_up: bfloat16 [2048, 4096], P('dp', 'tensor'), may hold values from -0.125 to 0.125
- w_gate: bfloat16 [2048, 4096], P('dp', 'tensor'), may hold values from -0.125 to 0.125
- w_down: bfloat16 [4096, 2048], P('tensor', 'dp'), may hold values from -0.09375 to 0.09375
- cotangent: bfloat16 [6144, 2048], P(('dp', 'tensor')), may hold values from -6 to 6
Outputs:
- mixed: bfloat16 [6144, 2048], P(('dp', 'tensor'))
- grad_tokens: float32 [6144, 2048], P(('dp', 'tensor'))
- grad_norm1: float32 [2048], replicated
- grad_query: float32 [2048, 2048], P('dp', 'tensor')
- grad_key: float32 [2048, 2048], P('dp', 'tensor')
- grad_value: float32 [2048, 4096], P('dp', 'tensor')
- grad_swish: float32 [2048, 4096], P('dp', 'tensor')
- grad_out: float32 [4096, 2048], P('tensor', 'dp')
- grad_norm2: float32 [2048], replicated
- grad_up: float32 [2048, 4096], P('dp', 'tensor')
- grad_gate: float32 [2048, 4096], P('dp', 'tensor')
- grad_down: float32 [4096, 2048], P('tensor', 'dp')
The draws below stay inside these ranges and needn't reach their ends.
Inputs may be any that keep to these rules, and one draw needn't show every extreme that they name: `segments`: segment numbers never fall along the tokens; a document has 1 to 384 tokens, and one has exactly 384.
All inputs are finite; a program needn't handle non-finite values.
Results may differ from the reference program's by a relative error of at most 0.015.
Values may be sent and summed in bfloat16 or wider, within the bound.
No kernel may reach another device: no remote copies, remote signals or barrier semaphores. Data moves between devices by JAX's collectives and lax.ppermute only.
A program may use at most 320 MiB of HBM per device.

```python
import math
import jax
import jax.numpy as jnp
import numpy as np
from jax import lax

D = 2048
HEADS = 8
KEY = 256
VALUE = 512
FF = 4096
SEQ = 384
QD = 2048
VD = 4096
TOKENS = 6144


def shared_projection(key):
    base = jnp.clip(jax.random.normal(jax.random.fold_in(key, 11), (D, QD), jnp.float32), -5.0, 5.0)
    noise = jnp.clip(jax.random.normal(jax.random.fold_in(key, 12), (D, QD), jnp.float32), -5.0, 5.0)
    return (base, noise)


def draw_w_query(key, part):
    base, noise = shared_projection(key)
    return (base * (1.0 / jnp.sqrt(jnp.float32(D)))).astype(jnp.bfloat16)


def draw_w_key(key, part):
    base, noise = shared_projection(key)
    return ((0.8 * base + 0.6 * noise) * (1.0 / jnp.sqrt(jnp.float32(D)))).astype(jnp.bfloat16)


def block_levels(stream_key, shape, cuts, smallest, high):
    level, own = 1.0, jax.random.fold_in(stream_key, 6)
    for dim, shards_of in cuts:
        heights = jnp.exp(jax.random.uniform(jax.random.fold_in(own, dim), (shards_of,), jnp.float32, smallest / len(cuts), high / len(cuts)))
        level = level * jnp.repeat(heights, shape[dim] // shards_of).reshape([-1 if axis == dim else 1 for axis in range(len(shape))])
    return level


def length_profile(amount, total, most, skew):
    weights = [(1 << 20) // math.isqrt(rank ** skew) + 1 for rank in range(2, amount + 1)]
    surplus, holding = total - most - (amount - 1), [1] * (amount - 1)
    while surplus > 0:
        movable = [i for i in range(amount - 1) if holding[i] < most]
        mass, remaining = sum([weights[i] for i in movable]), surplus
        for i in movable:
            more = min(most - holding[i], max(1, remaining * weights[i] // mass), surplus)
            holding[i] = holding[i] + more
            surplus = surplus - more
    return np.array([most] + holding)


def uneven(stream_key, count, total, limit, slope):
    if count == 2:
        one = jax.random.randint(stream_key, (), max(1, total - limit), min(limit, total - 1) + 1)
        return jnp.stack([one, total - one])
    lengths = jnp.asarray(length_profile(count, total, limit, slope), jnp.int32)
    twos = (count - 1) // 2
    giver, taker = lengths[1:1 + 2 * twos:2], lengths[2:2 + 2 * twos:2]
    room = jnp.minimum(giver - 1, limit - taker)
    shifted = jax.random.randint(jax.random.fold_in(stream_key, 1), (twos,), 0, 1 << 20) % (room + 1)
    lengths = lengths.at[1:1 + 2 * twos:2].set(giver - shifted).at[2:2 + 2 * twos:2].set(taker + shifted)
    return lengths[jax.random.permutation(jax.random.fold_in(stream_key, 2), count)]


def gaussian(stream_key, shape, width, bound, shards=(), kind=jnp.bfloat16):
    level = block_levels(stream_key, shape, shards, -0.22, 0.18) if shards else 1.0
    values = jax.random.normal(stream_key, shape, jnp.float32) * width * level
    return jnp.minimum(jnp.maximum(values, -bound), bound).astype(kind)


def setup_inputs(seed: int = 0) -> dict:
    arg_keys = jax.random.split(jax.random.key(seed), 15)
    tokens = gaussian(arg_keys[0], (TOKENS, D), 1.0, 6.0, ((0, 32),))
    segments = jnp.searchsorted(jnp.cumsum(uneven(arg_keys[1], 2 * TOKENS // SEQ, TOKENS, SEQ, 1)), jnp.arange(TOKENS), side="right").astype(jnp.int32)
    decay = jnp.clip(jnp.exp(math.log(0.03) - 4.0943445 * jax.random.uniform(arg_keys[2], (HEADS,), jnp.float32) ** block_levels(arg_keys[2], (HEADS,), ((0, 2),), -0.2, 0.2)), 0.0005, 0.03)
    norm1_gain = jnp.clip(1.0 + 0.1 * jax.random.normal(arg_keys[3], (D,), jnp.float32), 0.5, 1.5)
    w_query = draw_w_query(jax.random.fold_in(arg_keys[14], 71), 0)
    w_key = draw_w_key(jax.random.fold_in(arg_keys[14], 71), 0)
    w_value = gaussian(arg_keys[6], (D, VD), D ** -0.5, 0.125, ((0, 16), (1, 2)))
    w_swish = gaussian(arg_keys[7], (D, VD), D ** -0.5, 0.125, ((0, 16), (1, 2)))
    w_out = gaussian(arg_keys[8], (VD, D), VD ** -0.5, 0.09375, ((0, 2), (1, 16)))
    norm2_gain = jnp.clip(1.0 + 0.1 * jax.random.normal(arg_keys[9], (D,), jnp.float32), 0.5, 1.5)
    w_up = gaussian(arg_keys[10], (D, FF), D ** -0.5, 0.125, ((0, 16), (1, 2)))
    w_gate = gaussian(arg_keys[11], (D, FF), D ** -0.5, 0.125, ((0, 16), (1, 2)))
    w_down = gaussian(arg_keys[12], (FF, D), FF ** -0.5, 0.09375, ((0, 2), (1, 16)))
    cotangent = gaussian(arg_keys[13], (TOKENS, D), 1.0, 6.0, ((0, 32),))
    return {"tokens": tokens, "segments": segments, "decay": decay, "norm1_gain": norm1_gain, "w_query": w_query, "w_key": w_key, "w_value": w_value, "w_swish": w_swish, "w_out": w_out, "norm2_gain": norm2_gain, "w_up": w_up, "w_gate": w_gate, "w_down": w_down, "cotangent": cotangent}


@jax.custom_vjp
def low(v):
    return lax.optimization_barrier(v.astype(jnp.bfloat16)).astype(jnp.float32)

@jax.custom_vjp
def low_back(v):
    return v

def low_keep(v):
    return (low(v), None)

def low_pass(kept, grad):
    return (grad,)

def back_keep(v):
    return (v, None)

def back_low(kept, grad):
    return (low(grad),)
low.defvjp(low_keep, low_pass)
low_back.defvjp(back_keep, back_low)
epsilon = 1e-05

def matmul(left, right):
    return jnp.dot(left, right, precision=lax.Precision.HIGHEST)

def normalize(values):
    centred = values - lax.optimization_barrier(jnp.mean(values, axis=-1, keepdims=True))
    variance = lax.optimization_barrier(jnp.mean(centred * centred, axis=-1, keepdims=True))
    return centred * lax.rsqrt(variance + epsilon)

def both_ways(value):
    return low(low_back(value))

def sequence_layer(rows, segment_ids, rates, first_norm_gain, w_query, w_key, w_value, w_swish, w_out, gain_two, w_up, w_gate, w_down):
    length = rows.shape[0]
    normed = low(normalize(rows) * first_norm_gain)
    query_rows = both_ways(matmul(normed, w_query)).reshape(length, HEADS, KEY)
    key_rows = both_ways(matmul(normed, w_key)).reshape(length, HEADS, KEY)
    values = both_ways(matmul(normed, w_value)).reshape(length, HEADS, VALUE)
    swish_in = low_back(matmul(normed, w_swish))
    position = jnp.arange(length, dtype=jnp.int32)
    offset = position[:, None] - position[None, :]
    allowed = (offset >= 0) & (segment_ids[:, None] == segment_ids[None, :])
    distance = jnp.maximum(offset, 0).astype(jnp.float32)
    decay_mask = jnp.where(allowed[None], jnp.exp(-rates[:, None, None] * distance[None]), 0.0)
    unmasked_scores = low_back(jnp.einsum('pqk,aqk->qpa', query_rows, key_rows, precision=lax.Precision.HIGHEST))
    scores = low(unmasked_scores * decay_mask)
    retained = low_back(jnp.einsum('hnm,mhe->nhe', scores, values, precision=lax.Precision.HIGHEST))
    gated = low((jax.nn.silu(swish_in).reshape(length, HEADS, VALUE) * normalize(retained)).reshape(length, HEADS * VALUE))
    middle = rows + low_back(matmul(gated, w_out))
    normed_two = low(normalize(middle) * gain_two)
    up_rows = low_back(matmul(normed_two, w_up))
    gate_rows = low_back(matmul(normed_two, w_gate))
    hidden = low(jax.nn.gelu(gate_rows) * up_rows)
    return middle + low_back(matmul(hidden, w_down))

def reference(tokens, segments, decay, norm1_gain, w_query, w_key, w_value, w_swish, w_out, norm2_gain, w_up, w_gate, w_down, cotangent):
    seq_count = tokens.shape[0] // SEQ
    weights = tuple((matrix.astype(jnp.float32) for matrix in (norm1_gain, w_query, w_key, w_value, w_swish, w_out, norm2_gain, w_up, w_gate, w_down)))
    seg_blocks = segments.reshape(seq_count, SEQ)

    def whole(rows, first_norm_gain, m_query, m_key, m_value, m_swish, m_out, gain_two, m_up, m_gate, m_down):

        def one_sequence(sequence_item):
            return jax.checkpoint(sequence_layer)(sequence_item[0], sequence_item[1], decay, first_norm_gain, m_query, m_key, m_value, m_swish, m_out, gain_two, m_up, m_gate, m_down)
        result = lax.map(one_sequence, (rows.reshape(seq_count, SEQ, D), seg_blocks))
        return result.reshape(seq_count * SEQ, D)
    mixed, pullback = jax.vjp(whole, tokens.astype(jnp.float32), *weights)
    grads = pullback(cotangent.astype(jnp.float32))
    return (mixed.astype(jnp.bfloat16), grads[0], grads[1], grads[2], grads[3], grads[4], grads[5], grads[6], grads[7], grads[8], grads[9], grads[10])
```

```python
import jax
import jax.numpy as jnp
from jax import lax
from jax.sharding import Mesh, PartitionSpec as P

epsilon = 1e-05
bf16 = jnp.bfloat16
f32 = jnp.float32
SPREAD = ("zh", "zl", "y", "x")
GROUP = ("zl", "x")


def normalize(values):
    centred = values - jnp.mean(values, axis=-1, keepdims=True)
    variance = jnp.mean(centred * centred, axis=-1, keepdims=True)
    return centred * lax.rsqrt(variance + epsilon)


def layer_norm(rows, gain):
    return normalize(rows) * gain


def product(left, right):
    return jnp.dot(left, right, preferred_element_type=f32)


def left_product(left, right):
    return lax.dot_general(left, right, (((0,), (0,)), ((), ())), preferred_element_type=f32)


def right_product(left, right):
    return lax.dot_general(left, right, (((1,), (1,)), ((), ())), preferred_element_type=f32)


def gate_piece(swish_in, retained):
    shaped = jax.nn.silu(swish_in).reshape(retained.shape) * normalize(retained)
    return shaped.reshape(swish_in.shape)


def gelu_piece(gate_rows, up_rows):
    return jax.nn.gelu(gate_rows) * up_rows


def swap(a, axis):
    return lax.ppermute(a, axis, [(0, 1), (1, 0)])


def both(own, axis, dim):
    if lax.axis_size(axis) != 2:
        return lax.all_gather(own, axis, axis=dim)
    return ordered(own, swap(own, axis), axis, dim)


def ordered(own, other, axis, dim):
    first = lax.axis_index(axis) == 0
    return jnp.stack([jnp.where(first, own, other), jnp.where(first, other, own)], dim)


def gather_weight(piece):
    piece = piece.reshape((2, 2) + piece.shape[1:])
    if lax.axis_size("zh") == 2:
        far = swap(piece, "zh")
        near_y = swap(piece, "y")
        far_y = swap(far, "y")
        own = ordered(piece, near_y, "y", 1)
        other = ordered(far, far_y, "y", 1)
        whole = ordered(own, other, "zh", 0)
    else:
        whole = both(lax.all_gather(piece, "zh"), "y", 2)
    return whole


def gather_rows_split(w):
    rows, cols = w.shape
    n = cols // 4
    parts = w.reshape(rows, 4, n).transpose(1, 0, 2)
    piece = lax.all_to_all(parts, GROUP, 0, 0, tiled=True)
    return gather_weight(piece).reshape(-1, n)


def gather_columns_split(w):
    rows, cols = w.shape
    n = rows // 4
    piece = lax.all_to_all(w.reshape(4, n, cols), GROUP, 0, 0, tiled=True)
    whole = gather_weight(piece)
    return whole.transpose(4, 0, 1, 2, 3, 5).reshape(n, -1)


def take(a, index, dim):
    return lax.dynamic_index_in_dim(a, index, dim, keepdims=False)


def scatter_weight(g):
    y = lax.axis_index("y")
    got = swap(take(g, 1 - y, 2), "y")
    g = (take(g, y, 2).astype(f32) + got.astype(f32)).astype(bf16)
    if lax.axis_size("zh") == 2:
        zh = lax.axis_index("zh")
        got = swap(take(g, 1 - zh, 0), "zh")
        g = (take(g, zh, 0).astype(f32) + got.astype(f32)).astype(bf16)
    else:
        g = lax.psum_scatter(g, "zh", scatter_dimension=0)
    g = g.reshape((4,) + g.shape[2:])
    return lax.all_to_all(g, GROUP, 0, 0, tiled=True)


def mesh_sizes():
    return tuple(lax.axis_size(a) for a in SPREAD)


def scatter_rows_split(g):
    n = g.shape[1]
    parts = scatter_weight(g.astype(bf16).reshape(mesh_sizes() + (-1, n)))
    return parts.transpose(1, 0, 2).reshape(-1, 4 * n).astype(f32)


def scatter_columns_split(g):
    n = g.shape[0]
    g = g.astype(bf16).reshape((n,) + mesh_sizes() + (-1,)).transpose(1, 2, 3, 4, 0, 5)
    parts = scatter_weight(g)
    return parts.reshape(4 * n, -1).astype(f32)


def gather_tokens(a):
    half = a.shape[1] // 2
    ax = swap(a, "x")
    az = swap(a, "zl")
    ad = jnp.concatenate([swap(az[:, :half], "x"), swap(ax[:, half:], "zl")], 1)
    pieces = [a, ax, az, ad]
    return jnp.stack([jnp.stack([p, swap(p, "tensor")]) for p in pieces])


def scatter_tokens(p):
    half = p.shape[3] // 2
    p = p.astype(bf16)
    s = []
    for r in (3, 2, 1, 0):
        s.append(p[r, 0].astype(f32) + swap(p[r, 1], "tensor").astype(f32))
    diag, zmate, xmate, own = s
    diag = diag.astype(bf16)
    through_x = swap(diag[:, :half], "x").astype(f32)
    through_z = swap(diag[:, half:], "zl").astype(f32)
    zmate = jnp.concatenate([zmate[:, :half] + through_x, zmate[:, half:]], 1).astype(bf16)
    xmate = jnp.concatenate([xmate[:, :half], xmate[:, half:] + through_z], 1).astype(bf16)
    return own + swap(xmate, "x").astype(f32) + swap(zmate, "zl").astype(f32)


def sum_everywhere(a):
    for axis in ("tensor",) + SPREAD:
        if lax.axis_size(axis) == 2:
            a = a + swap(a, axis)
        else:
            a = lax.psum(a, axis)
    return a


def local(
    tokens,
    segments,
    decay,
    norm1_gain,
    w_query,
    w_key,
    w_value,
    w_swish,
    w_out,
    norm2_gain,
    w_up,
    w_gate,
    w_down,
    cotangent,
):
    quarter = 2 * lax.axis_index("zl") + lax.axis_index("x")
    core = lax.axis_index("tensor")
    length = segments.shape[0]
    rows_each = tokens.shape[0]
    key_size = w_query.shape[1] // 4
    value_size = w_value.shape[1] // 4
    rate = take(decay, quarter, 0)

    rows_q, rows_v = w_query.shape[0], w_value.shape[0]
    w_qk = jnp.concatenate(
        [w_query.reshape(rows_q, 4, key_size), w_key.reshape(rows_q, 4, key_size)], 2
    ).reshape(rows_q, 8 * key_size)
    full_qk = gather_rows_split(w_qk)
    full_value = gather_rows_split(w_value)
    full_swish = gather_rows_split(w_swish)
    full_out = gather_columns_split(w_out)
    full_up = gather_rows_split(w_up)
    full_gate = gather_rows_split(w_gate)
    full_down = gather_columns_split(w_down)

    seg_x = jnp.stack([segments, swap(segments, "x")])
    segs = jnp.concatenate([seg_x, swap(seg_x, "zl")])
    segs = jnp.where(core == 0, segs, jnp.roll(segs, length // 2, 1))
    position = (jnp.arange(length, dtype=jnp.int32) + core * rows_each) % length

    rows_local = tokens.astype(f32)
    normed_local = layer_norm(rows_local, norm1_gain).astype(bf16)
    model = normed_local.shape[1]
    normed = gather_tokens(normed_local).reshape(-1, model)
    count = normed.shape[0]

    qk = product(normed, full_qk).astype(bf16)
    query_rows = qk[:, :key_size].reshape(4, length, key_size)
    key_rows = qk[:, key_size:].reshape(4, length, key_size)
    values = product(normed, full_value).astype(bf16).reshape(4, length, value_size)
    swish_in = product(normed, full_swish).reshape(4, length, value_size)
    offset = position[:, None] - position[None, :]
    allowed = (offset >= 0)[None] & (segs[:, :, None] == segs[:, None, :])
    distance = jnp.maximum(offset, 0).astype(f32)
    decay_mask = jnp.where(allowed, jnp.exp(-rate * distance)[None], 0.0)
    unmasked_scores = jnp.einsum("snd,smd->snm", query_rows, key_rows, preferred_element_type=f32)
    scores = (unmasked_scores * decay_mask).astype(bf16)
    retained = jnp.einsum("snm,sme->sne", scores, values, preferred_element_type=f32)
    gated = gate_piece(swish_in, retained).astype(bf16).reshape(count, value_size)
    branch = product(gated, full_out).reshape(4, 2, rows_each, model)
    middle = rows_local + scatter_tokens(branch)
    normed_two_local = layer_norm(middle, norm2_gain).astype(bf16)
    normed_two = gather_tokens(normed_two_local).reshape(count, model)
    grad_rows = gather_tokens(cotangent).reshape(count, model)
    up_rows = product(normed_two, full_up)
    gate_rows = product(normed_two, full_gate)
    grad_hidden = right_product(grad_rows, full_down)
    hidden = gelu_piece(gate_rows, up_rows).astype(bf16)
    _, gelu_pull = jax.vjp(gelu_piece, gate_rows, up_rows)
    grad_gate_rows, grad_up_rows = gelu_pull(grad_hidden)
    grad_gate_rows = grad_gate_rows.astype(bf16)
    grad_up_rows = grad_up_rows.astype(bf16)
    back_two = right_product(grad_up_rows, full_up) + right_product(grad_gate_rows, full_gate)
    back_two_local = scatter_tokens(back_two.reshape(4, 2, rows_each, model))
    _, norm_two_pull = jax.vjp(layer_norm, middle, norm2_gain)
    grad_mid_norm, grad_norm2_local = norm_two_pull(back_two_local)
    grad_middle = cotangent.astype(f32) + grad_mid_norm
    grad_branch = gather_tokens(grad_middle.astype(bf16)).reshape(count, model)

    feed = product(hidden, full_down).reshape(4, 2, rows_each, model)
    mixed = (middle + scatter_tokens(feed)).astype(bf16)
    grad_down = scatter_columns_split(left_product(hidden, grad_rows))
    grad_up = scatter_rows_split(left_product(normed_two, grad_up_rows))
    grad_gate = scatter_rows_split(left_product(normed_two, grad_gate_rows))

    grad_gated = right_product(grad_branch, full_out).reshape(4, length, value_size)
    _, gate_pull = jax.vjp(gate_piece, swish_in, retained)
    grad_swish_in, grad_retained = gate_pull(grad_gated)
    grad_swish_in = grad_swish_in.astype(bf16).reshape(count, value_size)
    grad_retained = grad_retained.astype(bf16)
    grad_scores = jnp.einsum("sne,sme->snm", grad_retained, values, preferred_element_type=f32)
    grad_values = jnp.einsum("snm,sne->sme", scores, grad_retained, preferred_element_type=f32)
    grad_values = grad_values.astype(bf16).reshape(count, value_size)
    grad_raw = (grad_scores * decay_mask).astype(bf16)
    grad_queries = jnp.einsum("snm,smd->snd", grad_raw, key_rows, preferred_element_type=f32)
    grad_keys = jnp.einsum("snm,snd->smd", grad_raw, query_rows, preferred_element_type=f32)
    grad_qk = jnp.concatenate([grad_queries, grad_keys], 2).astype(bf16)
    grad_qk = grad_qk.reshape(count, 2 * key_size)
    back_one = right_product(grad_qk, full_qk)
    back_one = back_one + right_product(grad_values, full_value)
    back_one = back_one + right_product(grad_swish_in, full_swish)
    back_one_local = scatter_tokens(back_one.reshape(4, 2, rows_each, model))

    grad_out = scatter_columns_split(left_product(gated, grad_branch))
    grad_swish = scatter_rows_split(left_product(normed, grad_swish_in))
    grad_value = scatter_rows_split(left_product(normed, grad_values))
    grad_qk = scatter_rows_split(left_product(normed, grad_qk))
    grad_qk = grad_qk.reshape(rows_q, 4, 2, key_size)
    grad_query = grad_qk[:, :, 0].reshape(rows_q, 4 * key_size)
    grad_key = grad_qk[:, :, 1].reshape(rows_q, 4 * key_size)

    _, norm_one_pull = jax.vjp(layer_norm, rows_local, norm1_gain)
    grad_tok_norm, grad_norm1_local = norm_one_pull(back_one_local)
    grad_tokens = grad_middle + grad_tok_norm
    grad_norm1 = sum_everywhere(grad_norm1_local)
    grad_norm2 = sum_everywhere(grad_norm2_local)
    return (
        mixed,
        grad_tokens,
        grad_norm1,
        grad_query,
        grad_key,
        grad_value,
        grad_swish,
        grad_out,
        grad_norm2,
        grad_up,
        grad_gate,
        grad_down,
    )


def solution(mesh):
    dp, tensor = mesh.shape["dp"], mesh.shape["tensor"]
    grid = Mesh(mesh.devices.reshape(dp // 8, 2, 2, 2, tensor), SPREAD + ("tensor",))
    rows = P(SPREAD + ("tensor",), None)
    rows_split = P(SPREAD, "tensor")
    columns_split = P("tensor", SPREAD)
    return jax.shard_map(
        local,
        mesh=grid,
        in_specs=(
            rows,
            P(SPREAD),
            P("tensor"),
            P(),
            rows_split,
            rows_split,
            rows_split,
            rows_split,
            columns_split,
            P(),
            rows_split,
            rows_split,
            columns_split,
            rows,
        ),
        out_specs=(
            rows,
            rows,
            P(),
            rows_split,
            rows_split,
            rows_split,
            rows_split,
            columns_split,
            P(),
            rows_split,
            rows_split,
            columns_split,
        ),
        check_vma=False,
    )
```

```python
import functools
import jax
import jax.numpy as jnp
from jax import lax
from jax.experimental import pallas as pl
from jax.experimental.pallas import tpu as pltpu
from jax.sharding import Mesh, PartitionSpec as P

epsilon = 1e-05
bf16 = jnp.bfloat16
f32 = jnp.float32
SPREAD = ("zh", "zl", "y", "x")
GROUP = ("zl", "x")


def normalize(values):
    centred = values - jnp.mean(values, axis=-1, keepdims=True)
    variance = jnp.mean(centred * centred, axis=-1, keepdims=True)
    return centred * lax.rsqrt(variance + epsilon)


def layer_norm(rows, gain):
    return normalize(rows) * gain


def dot(left, right, dims):
    return lax.dot_general(left, right, (dims, ((), ())), preferred_element_type=f32)


NN = ((1,), (0,))
NT = ((1,), (1,))
TN = ((0,), (0,))


def swap(a, axis, label="move"):
    with jax.named_scope(label):
        return lax.ppermute(a, axis, [(0, 1), (1, 0)])


def after(value, *others):
    return lax.optimization_barrier((value,) + others)[0]


def ordered(own, other, axis, dim):
    first = lax.axis_index(axis) == 0
    return jnp.stack([jnp.where(first, own, other), jnp.where(first, other, own)], dim)


def by_quarter(w):
    rows, cols = w.shape
    return w.reshape(rows, 4, cols // 4).transpose(1, 0, 2)


def group_exchange(parts):
    return lax.all_to_all(parts, GROUP, 0, 0, tiled=True)


def far_half(piece, label):
    if lax.axis_size("zh") == 2:
        return swap(piece, "zh", label)
    return lax.all_gather(piece, "zh")


def whole_weight(piece, near_y, far, far_y, column, width):
    if lax.axis_size("zh") == 2:
        return [(piece, column), (near_y, column), (far, 0), (far_y, 0)], width
    shape = far.shape[:1] + (2, 2) + far.shape[2:]
    whole = ordered(far.reshape(shape), far_y.reshape(shape), "y", 2)
    return [(whole.reshape(16, -1, width), 0)], width


def take(a, index, dim):
    return lax.dynamic_index_in_dim(a, index, dim, keepdims=False)


def add(a, b):
    return (a.astype(f32) + b.astype(f32)).astype(bf16)


def scatter_y(keep, got):
    n = got.shape[-1]
    if lax.axis_size("zh") == 2:
        return add(keep[:2], got[:2]), add(keep[2:], got[2:])
    flip = lambda g: jnp.flip(g.reshape(2, 2, 1, -1, n), 0)
    g = jnp.concatenate([flip(keep), flip(got)], 2).reshape(lax.axis_size("zh"), 2, 2, 2, -1, n)
    y = lax.axis_index("y")
    return add(take(g, y, 2), swap(take(g, 1 - y, 2), "y")), None


def send_y(send):
    return swap(send, "y", "y_grad") if lax.axis_size("zh") == 2 else send


def scatter_zh(send, keep, label):
    if lax.axis_size("zh") == 2:
        g = add(keep, swap(send, "zh", label))
    else:
        g = lax.psum_scatter(send, "zh", scatter_dimension=0)
    return g.reshape(4, -1, g.shape[-1])


class Clock:
    def __init__(self):
        self.now = ()

    def done(self, *values):
        self.now = values

    def at(self, value):
        return after(value, *self.now)


class Gather:
    def __init__(self, clock, a, label):
        self.a, self.label, self.half = clock.at(a), label, a.shape[0] // 2
        self.x = swap(self.a, "x", label + "_x")
        self.z = swap(self.a, "zl", label + "_z")
        self.first = (self.x, self.z)

    def finish(self, clock):
        half, label = self.half, self.label
        ax, az = clock.at(self.x), clock.at(self.z)
        top = swap(az[:half], "x", label + "_dx")
        bottom = swap(ax[half:], "zl", label + "_dz")
        out = []
        for p in ((self.a,), (ax,), (az,), (top, bottom)):
            out += list(p) + [swap(q, "tensor", label + "_c") for q in p]
        return out


class Scatter:
    def __init__(self, send_rest, send_diag, keep, label):
        self.label, self.keep = label, keep
        self.diag = add(keep[3], swap(send_diag, "tensor", label + "_cd"))
        self.rest = swap(send_rest, "tensor", label + "_cr")

    def relay(self, clock):
        half = self.diag.shape[0] // 2
        diag = clock.at(self.diag)
        self.through_x = swap(diag[:half], "x", self.label + "_dx")
        self.through_z = swap(diag[half:], "zl", self.label + "_dz")
        self.second = (self.through_x, self.through_z, self.rest)

    def send(self, clock):
        through_x, through_z, rest = (clock.at(v).astype(f32) for v in self.second)
        half = through_x.shape[0]
        self.own, xmate, zmate = (self.keep[r].astype(f32) + rest[r] for r in range(3))
        zmate = jnp.concatenate([zmate[:half] + through_x, zmate[half:]]).astype(bf16)
        xmate = jnp.concatenate([xmate[:half], xmate[half:] + through_z]).astype(bf16)
        self.x = swap(xmate, "x", self.label + "_x")
        self.z = swap(zmate, "zl", self.label + "_z")
        self.last = (self.x, self.z)

    def finish(self):
        return self.own + self.x.astype(f32) + self.z.astype(f32)


VMEM_LIMIT = 60 * 2**20
PIECES = (
    (0, 0, 0, 1),
    (0, 1, 0, 1),
    (1, 2, 0, 1),
    (1, 3, 0, 1),
    (2, 4, 0, 1),
    (2, 5, 0, 1),
    (3, 6, 0, 2),
    (3, 6, 1, 2),
    (3, 7, 0, 2),
    (3, 7, 1, 2),
)
ANY = pl.BlockSpec(memory_space=pl.ANY)
SMEM = pl.BlockSpec(memory_space=pltpu.SMEM)


class Loader:
    def __init__(self, sems):
        self.sems, self.used = sems, 0

    def copy(self, src, dst):
        self.used += 1
        return pltpu.make_async_copy(src, dst, self.sems.at[self.used - 1])

    def tokens(self, refs, held):
        rows = held.shape[1]
        chips = [[], [], [], []]
        for ref, (chip, slot, part, parts) in zip(refs, PIECES):
            size = rows // parts
            chips[chip].append(self.copy(ref, held.at[slot, pl.ds(part * size, size)]))
        return chips

    def weight(self, refs, columns, held, coord):
        if len(refs) == 1:
            return [self.copy(refs[0], held)]
        copies, n = [], held.shape[2]
        for i, (ref, column) in enumerate(zip(refs, columns)):
            zh, y = coord[0] ^ (i // 2), coord[1] ^ (i % 2)
            for zl in range(2):
                row = ((zh * 2 + zl) * 2 + y) * 2
                block = ref.at[pl.ds(2 * zl, 2), :, pl.ds(column, n)]
                copies.append(self.copy(block, held.at[pl.ds(row, 2)]))
        return copies


def start(*copies):
    for c in copies:
        c.start()


def wait(*copies):
    for c in copies:
        c.wait()


def at_chip(r, chips):
    for i, copies in enumerate(chips):
        pl.when(r == i)(functools.partial(wait, *copies))


def rows_of(held, r):
    pair = held[pl.ds(2 * r, 2)]
    return pair.reshape(2 * pair.shape[1], pair.shape[2])


def flat(w):
    value = w[...]
    return value.reshape(value.shape[0] * value.shape[1], value.shape[2])


def by_chip(shape):
    return pl.BlockSpec((1,) + shape, lambda r: (r,) + (0,) * len(shape))


def chip_kernel(body, operands, specs, outs, out_specs, scratch, copies, flops):
    moved = sum(a.size * a.dtype.itemsize for a in operands) + sum(
        o.size * jnp.dtype(o.dtype).itemsize for o in outs
    )
    return pl.pallas_call(
        body,
        grid=(4,),
        in_specs=specs,
        out_specs=out_specs,
        out_shape=outs,
        scratch_shapes=scratch + [pltpu.SemaphoreType.DMA((copies,))],
        compiler_params=pltpu.CompilerParams(
            dimension_semantics=("arbitrary",), vmem_limit_bytes=VMEM_LIMIT
        ),
        cost_estimate=pl.CostEstimate(flops=flops, bytes_accessed=moved, transcendentals=0),
    )(*operands)


def held_tokens(pieces):
    return pltpu.VMEM((8,) + pieces[0].shape, bf16)


def held_weight(w):
    rows = sum(p.shape[0] * p.shape[1] for p, _ in w[0])
    return pltpu.VMEM((16, rows // 16, w[1]), bf16)


def arrays(*weights):
    return [p for w in weights for p, _ in w[0]]


def columns_of(w):
    return tuple(c for _, c in w[0])


def struct(shape, dtype):
    return jax.ShapeDtypeStruct(shape, dtype)


def column_loop(total, step, f):
    for j in range(0, total, step):
        f(j, step)


def partial_rows(grads, held, r, keep, store):
    rows = keep.shape[1]
    depth = held.shape[0] * held.shape[1]
    blocks = 4
    for j in range(0, held.shape[0], blocks):
        w = held[j : j + blocks].reshape(blocks * held.shape[1], held.shape[2])
        c = j * held.shape[1]
        out = dot(grads, w, NT).astype(bf16)
        keep[0, :, c : c + blocks * held.shape[1]] = out[:rows]
        store[r, :, c : c + blocks * held.shape[1]] = out[rows:]


def send_copies(load, store, rest, diag):
    return [load.copy(store.at[i], rest.at[i]) for i in range(3)] + [load.copy(store.at[3], diag)]


def at_chip_start(r, copies):
    for i, c in enumerate(copies):
        pl.when(r == i)(c.start)

    @pl.when(r == 3)
    def _():
        wait(*copies)


def partial_outs(rows, model):
    outs = [
        struct((3, rows, model), bf16),
        struct((rows, model), bf16),
        struct((4, rows, model), bf16),
    ]
    return outs, [ANY, ANY, by_chip((rows, model))]


def attend_body(c_qk, c_v, coord, mask, *refs):
    acts, refs = refs[:10], refs[10:]
    wqk, refs = refs[: len(c_qk)], refs[len(c_qk) :]
    wv, refs = refs[: len(c_v)], refs[len(c_v) :]
    q_out, k_out, v_out, score_out, hat_out, scale_out, held, held_qk, held_v, sems = refs
    load, r = Loader(sems), pl.program_id(0)
    w1 = load.weight(wqk, c_qk, held_qk, coord)
    chips = load.tokens(acts, held)
    w2 = load.weight(wv, c_v, held_v, coord)

    @pl.when(r == 0)
    def _():
        start(*w1, *chips[0], *w2, *chips[1], *chips[2], *chips[3])
        wait(*w1)

    at_chip(r, chips)
    x = rows_of(held, r)
    qk = dot(x, flat(held_qk), NN).astype(bf16)
    size = qk.shape[1] // 2
    q, k = qk[:, :size], qk[:, size:]
    q_out[0], k_out[0] = q, k
    scores = (dot(q, k, NT) * mask[0]).astype(bf16)
    score_out[0] = scores

    @pl.when(r == 0)
    def _():
        wait(*w2)

    v = dot(x, flat(held_v), NN).astype(bf16)
    v_out[0] = v
    hat_out[0] = dot(scores, v, NN)
    rows, step = hat_out.shape[1], 32

    def chunk(i, carry):
        at = pl.ds(pl.multiple_of(i * step, step), step)
        part = hat_out[0, at, :]
        part = part - jnp.mean(part, axis=-1, keepdims=True)
        scale = lax.rsqrt(jnp.mean(part * part, axis=-1, keepdims=True) + epsilon)
        hat_out[0, at, :] = part * scale
        scale_out[0, at, :] = jnp.broadcast_to(scale, (step, 128))
        return carry

    lax.fori_loop(0, rows // step, chunk, 0)


def attend(coord, mask, acts, wqk, wv, key_size):
    length, n = mask.shape[1], wv[1]
    model = acts[0].shape[1]
    outs = [
        struct((4, length, key_size), bf16),
        struct((4, length, key_size), bf16),
        struct((4, length, n), bf16),
        struct((4, length, length), bf16),
        struct((4, length, n), f32),
        struct((4, length, 128), f32),
    ]
    return chip_kernel(
        functools.partial(attend_body, columns_of(wqk), columns_of(wv)),
        [coord, mask, *acts, *arrays(wqk, wv)],
        [SMEM, by_chip((length, length))] + [ANY] * (10 + len(arrays(wqk, wv))),
        outs,
        [by_chip(o.shape[1:]) for o in outs],
        [held_tokens(acts), held_weight(wqk), held_weight(wv)],
        30,
        16 * length * model * n,
    )


def branch_body(c_s, c_o, coord, hat, *refs):
    acts, refs = refs[:10], refs[10:]
    ws, refs = refs[: len(c_s)], refs[len(c_s) :]
    wo, refs = refs[: len(c_o)], refs[len(c_o) :]
    s_out, gated_out, rest, diag, keep, held, held_s, held_o, store, sems = refs
    load, r = Loader(sems), pl.program_id(0)
    w1 = load.weight(ws, c_s, held_s, coord)
    chips = load.tokens(acts, held)
    w2 = load.weight(wo, c_o, held_o, coord)
    sends = send_copies(load, store, rest, diag)

    @pl.when(r == 0)
    def _():
        start(*w1, *chips[0], *w2, *chips[1], *chips[2], *chips[3])
        wait(*w1)

    at_chip(r, chips)
    s_out[0] = dot(rows_of(held, r), flat(held_s), NN)
    rows, step = s_out.shape[1], 32

    def chunk(i, carry):
        at = pl.ds(pl.multiple_of(i * step, step), step)
        s = s_out[0, at, :]
        gated_out[0, at, :] = (s / (1.0 + jnp.exp(-s)) * hat[0, at, :]).astype(bf16)
        return carry

    lax.fori_loop(0, rows // step, chunk, 0)

    @pl.when(r == 0)
    def _():
        wait(*w2)

    partial_rows(gated_out[0], held_o, r, keep, store)
    at_chip_start(r, sends)


def branch(coord, hat, acts, ws, wo):
    length, n = hat.shape[1:]
    rows, model = acts[0].shape
    outs, out_specs = partial_outs(rows, model)
    outs = [struct((4, length, n), f32), struct((4, length, n), bf16)] + outs
    return chip_kernel(
        functools.partial(branch_body, columns_of(ws), columns_of(wo)),
        [coord, hat, *acts, *arrays(ws, wo)],
        [SMEM, by_chip((length, n))] + [ANY] * (10 + len(arrays(ws, wo))),
        outs,
        [by_chip((length, n)), by_chip((length, n))] + out_specs,
        [held_tokens(acts), held_weight(ws), held_weight(wo), pltpu.VMEM((4, rows, model), bf16)],
        40,
        16 * length * model * n,
    )


def feed_body(c_ug, c_d, coord, *refs):
    acts, cots, refs = refs[:10], refs[10:20], refs[20:]
    wug, refs = refs[: len(c_ug)], refs[len(c_ug) :]
    wd, refs = refs[: len(c_d)], refs[len(c_d) :]
    hidden_out, up_out, gate_out, rest, diag, keep = refs[:6]
    held, held_c, held_ug, held_d, store, ug, gh, sems = refs[6:]
    load, r = Loader(sems), pl.program_id(0)
    w1 = load.weight(wug, c_ug, held_ug, coord)
    chips = load.tokens(acts, held)
    w2 = load.weight(wd, c_d, held_d, coord)
    chips_c = load.tokens(cots, held_c)
    sends = send_copies(load, store, rest, diag)

    @pl.when(r == 0)
    def _():
        start(*w2, *chips_c[0], *w1, *chips[0])
        for i in range(1, 4):
            start(*chips_c[i], *chips[i])
        wait(*w2)

    at_chip(r, chips_c)
    gh[...] = dot(rows_of(held_c, r), flat(held_d), NN)

    @pl.when(r == 0)
    def _():
        wait(*w1)

    at_chip(r, chips)
    ug[...] = dot(rows_of(held, r), flat(held_ug), NN)
    rows, n = gh.shape
    step = 16

    def chunk(i, carry):
        at = pl.ds(pl.multiple_of(i * step, step), step)
        up, g, e = ug[at, :n], ug[at, n:], gh[at, :]
        c = 0.7978845608028654
        square = g * g
        t = jnp.tanh(c * g * (1.0 + 0.044715 * square))
        half = 0.5 * (1.0 + t)
        gelu = g * half
        slope = half + (0.5 * c) * g * (1.0 - t * t) * (1.0 + (3 * 0.044715) * square)
        hidden_out[0, at, :] = (gelu * up).astype(bf16)
        up_out[0, at, :] = (e * gelu).astype(bf16)
        gate_out[0, at, :] = (e * up * slope).astype(bf16)
        return carry

    lax.fori_loop(0, rows // step, chunk, 0)
    grads = jnp.concatenate([up_out[0], gate_out[0]], 1)
    partial_rows(grads, held_ug, r, keep, store)
    at_chip_start(r, sends)


def feed_forward(coord, acts, cots, wug, wd):
    rows, model = acts[0].shape
    n = wd[1]
    outs, out_specs = partial_outs(rows, model)
    outs = [struct((4, 2 * rows, n), bf16)] * 3 + outs
    return chip_kernel(
        functools.partial(feed_body, columns_of(wug), columns_of(wd)),
        [coord, *acts, *cots, *arrays(wug, wd)],
        [SMEM] + [ANY] * (20 + len(arrays(wug, wd))),
        outs,
        [by_chip((2 * rows, n))] * 3 + out_specs,
        [
            held_tokens(acts),
            held_tokens(cots),
            held_weight(wug),
            held_weight(wd),
            pltpu.VMEM((4, rows, model), bf16),
            pltpu.VMEM((2 * rows, 2 * n), f32),
            pltpu.VMEM((2 * rows, n), f32),
        ],
        50,
        80 * rows * model * n,
    )


def back_body(columns, coord, *refs):
    count = len(columns)
    weights = []
    grads, refs = refs[:count], refs[count:]
    for c in columns:
        weights.append(refs[: len(c)])
        refs = refs[len(c) :]
    rest, diag, keep, refs = refs[0], refs[1], refs[2], refs[3:]
    helds, store, sems = refs[:count], refs[-2], refs[-1]
    load, r = Loader(sems), pl.program_id(0)
    copies = [load.weight(w, c, h, coord) for w, c, h in zip(weights, columns, helds)]
    sends = send_copies(load, store, rest, diag)

    @pl.when(r == 0)
    def _():
        for c in copies:
            start(*c)
        for c in copies:
            wait(*c)

    if count == 1:
        partial_rows(grads[0][0], helds[0], r, keep, store)
    else:
        rows = keep.shape[1]
        blocks = 4
        for j in range(0, 16, blocks):
            size = helds[0].shape[1] * blocks
            parts = [
                dot(g[0], h[j : j + blocks].reshape(size, h.shape[2]), NT) for g, h in zip(grads, helds)
            ]
            out = sum(parts[1:], parts[0]).astype(bf16)
            c = j * helds[0].shape[1]
            keep[0, :, c : c + size] = out[:rows]
            store[r, :, c : c + size] = out[rows:]
    at_chip_start(r, sends)


def back(coord, grads, weights):
    length = grads[0].shape[1]
    rows = length // 2
    model = sum(p.shape[0] * p.shape[1] for p in arrays(weights[0]))
    outs, out_specs = partial_outs(rows, model)
    return chip_kernel(
        functools.partial(back_body, tuple(columns_of(w) for w in weights)),
        [coord, *grads, *arrays(*weights)],
        [SMEM] + [by_chip(g.shape[1:]) for g in grads] + [ANY] * len(arrays(*weights)),
        outs,
        out_specs,
        [held_weight(w) for w in weights]
        + [pltpu.VMEM((4, rows, model), bf16)],
        40,
        8 * length * model * sum(g.shape[2] for g in grads),
    )


def attend_back_body(c_o, coord, mask, s, hat, scale, scores, q, k, v, *refs):
    acts, refs = refs[:10], refs[10:]
    wo, refs = refs[: len(c_o)], refs[len(c_o) :]
    gqk_out, gv_out, gs_out, held, held_o, dg, gr, sems = refs
    load, r = Loader(sems), pl.program_id(0)
    w1 = load.weight(wo, c_o, held_o, coord)
    chips = load.tokens(acts, held)

    @pl.when(r == 0)
    def _():
        start(*w1, *chips[0], *chips[1], *chips[2], *chips[3])
        wait(*w1)

    at_chip(r, chips)
    dg[...] = dot(rows_of(held, r), flat(held_o), NN)
    rows, step = dg.shape[0], 16

    def chunk(i, carry):
        at = pl.ds(pl.multiple_of(i * step, step), step)
        e, x, v_s = dg[at, :], hat[0, at, :], s[0, at, :]
        gate = 1.0 / (1.0 + jnp.exp(-v_s))
        silu = v_s * gate
        gs_out[0, at, :] = (e * x * (gate + silu * (1.0 - gate))).astype(bf16)
        f = e * silu
        f = f - jnp.mean(f, axis=-1, keepdims=True) - x * jnp.mean(f * x, axis=-1, keepdims=True)
        gr[at, :] = (f * scale[0, at, :1]).astype(bf16)
        return carry

    lax.fori_loop(0, rows // step, chunk, 0)
    grad_retained = gr[...]
    gv_out[0] = dot(scores[0], grad_retained, TN).astype(bf16)
    raw = (dot(grad_retained, v[0], NT) * mask[0]).astype(bf16)
    size = q.shape[2]
    gqk_out[0, :, :size] = dot(raw, k[0], NN).astype(bf16)
    gqk_out[0, :, size:] = dot(raw, q[0], TN).astype(bf16)


def attend_back(coord, mask, s, hat, scale, scores, q, k, v, acts, wo):
    length, n = s.shape[1:]
    model = acts[0].shape[1]
    blocks = [mask, s, hat, scale, scores, q, k, v]
    outs = [struct((4, length, 2 * q.shape[2]), bf16)] + [struct((4, length, n), bf16)] * 2
    return chip_kernel(
        functools.partial(attend_back_body, columns_of(wo)),
        [coord, *blocks, *acts, *arrays(wo)],
        [SMEM] + [by_chip(b.shape[1:]) for b in blocks] + [ANY] * (10 + len(arrays(wo))),
        outs,
        [by_chip(o.shape[1:]) for o in outs],
        [
            held_tokens(acts),
            held_weight(wo),
            pltpu.VMEM((length, n), f32),
            pltpu.VMEM((length, n), bf16),
        ],
        20,
        12 * length * model * n,
    )


def weight_grad_body(count, coord, *refs):
    grads, acts, refs = refs[:count], refs[count : count + 10], refs[count + 10 :]
    outs, held, sems = refs[: 2 * count], refs[2 * count], refs[-1]
    load, i = Loader(sems), pl.program_id(0)
    chips = load.tokens(acts, held)

    @pl.when(i == 0)
    def _():
        for c in chips:
            start(*c)
        for c in chips:
            wait(*c)

    width = held.shape[2] // 8
    y = coord[1] ^ jnp.where(i < 4, 1, 0)
    j = i % 4
    zh = coord[0] ^ jnp.where(j < 2, 1, 0)
    column = ((zh * 2 + j % 2) * 2 + y) * width
    x = held[:, :, pl.ds(pl.multiple_of(column, width), width)]
    x = x.reshape(x.shape[0] * x.shape[1], width).T
    for n in range(count):
        g = grads[n][...]
        out = dot(x, g.reshape(g.shape[0] * g.shape[1], g.shape[2]), NN).astype(bf16)
        pl.when(i < 4)(functools.partial(store_block, outs[2 * n], out))
        pl.when(i >= 4)(functools.partial(store_block, outs[2 * n + 1], out))


def store_block(ref, value):
    ref[0] = value


def weight_grads(coord, acts, grads):
    rows, model = acts[0].shape
    outs, out_specs = [], []
    for g in grads:
        shape = (4, model // 8, g.shape[2])
        outs += [struct(shape, bf16)] * 2
        out_specs += [
            pl.BlockSpec((1,) + shape[1:], lambda i: (jnp.minimum(i, 3), 0, 0)),
            pl.BlockSpec((1,) + shape[1:], lambda i: (jnp.maximum(i - 4, 0), 0, 0)),
        ]
    width = sum(g.shape[2] for g in grads)
    moved = sum(a.size * 2 for a in acts) + sum(g.size * 2 for g in grads) + 2 * model * width
    got = pl.pallas_call(
        functools.partial(weight_grad_body, len(grads)),
        grid=(8,),
        in_specs=[SMEM] + [pl.BlockSpec(memory_space=pltpu.VMEM)] * len(grads) + [ANY] * 10,
        out_specs=out_specs,
        out_shape=outs,
        scratch_shapes=[held_tokens(acts), pltpu.SemaphoreType.DMA((10,))],
        compiler_params=pltpu.CompilerParams(
            dimension_semantics=("arbitrary",), vmem_limit_bytes=VMEM_LIMIT
        ),
        cost_estimate=pl.CostEstimate(
            flops=16 * rows * model * width, bytes_accessed=moved, transcendentals=0
        ),
    )(coord, *grads, *acts)
    return [(got[2 * i], got[2 * i + 1]) for i in range(len(grads))]


def sum_everywhere(a):
    for axis in ("tensor",) + SPREAD:
        if lax.axis_size(axis) == 2:
            a = a + swap(a, axis)
        else:
            a = lax.psum(a, axis)
    return a


def local(
    tokens,
    segments,
    decay,
    norm1_gain,
    w_query,
    w_key,
    w_value,
    w_swish,
    w_out,
    norm2_gain,
    w_up,
    w_gate,
    w_down,
    cotangent,
):
    quarter = 2 * lax.axis_index("zl") + lax.axis_index("x")
    core = lax.axis_index("tensor")
    length = segments.shape[0]
    rows_each = tokens.shape[0]
    key_size = w_query.shape[1] // 4
    value_size = w_value.shape[1] // 4
    rate = take(decay, quarter, 0)

    rows_q, width = w_query.shape[0], value_size
    if lax.axis_size("zh") == 2:
        coord = jnp.stack([lax.axis_index("zh"), lax.axis_index("y")]).astype(jnp.int32)
    else:
        coord = jnp.zeros((2,), jnp.int32)

    clock = Clock()
    at = clock.at
    rows_local = tokens.astype(f32)
    normed_local = layer_norm(rows_local, norm1_gain).astype(bf16)

    piece_qk = group_exchange(jnp.concatenate([by_quarter(w_query), by_quarter(w_key)], 2))
    parts = jnp.concatenate([by_quarter(w_value), by_quarter(w_swish), by_quarter(w_out.T)], 2)
    clock.done(piece_qk)
    far_qk, near_qk = far_half(piece_qk, "zh_qk"), swap(piece_qk, "y", "ny_qk")
    piece_r = group_exchange(at(parts))

    def third(piece, k, count=1):
        return piece[:, :, k * width : (k + count) * width]

    clock.done(far_qk, near_qk, piece_r)
    far_y_qk = swap(at(far_qk), "y", "fy_qk")
    far_value = far_half(at(third(piece_r, 0)), "zh_value")
    near_r = swap(at(piece_r), "y", "ny_r")
    gather = Gather(clock, normed_local, "normed")
    segments = at(segments)
    seg_x = jnp.stack([segments, swap(segments, "x")])
    segs = jnp.concatenate([seg_x, swap(seg_x, "zl")])
    segs = jnp.where(core == 0, segs, jnp.roll(segs, length // 2, 1))
    position = (jnp.arange(length, dtype=jnp.int32) + core * rows_each) % length
    offset = position[:, None] - position[None, :]
    allowed = (offset >= 0)[None] & (segs[:, :, None] == segs[:, None, :])
    distance = jnp.maximum(offset, 0).astype(f32)
    decay_mask = jnp.where(allowed, jnp.exp(-rate * distance)[None], 0.0)

    clock.done(far_value, far_y_qk, *gather.first)
    far_swish = far_half(at(third(piece_r, 1)), "zh_swish")
    far_y_value = swap(at(far_value), "y", "fy_value")
    normed = gather.finish(clock)
    parts = jnp.concatenate([by_quarter(w_up), by_quarter(w_gate), by_quarter(w_down.T)], 2)
    piece_f = group_exchange(at(parts))

    clock.done(far_swish, far_y_value, piece_f, near_r, *normed)
    far_out = far_half(at(third(piece_r, 2)), "zh_out")
    far_y_swish = swap(at(far_swish), "y", "fy_swish")
    gather = Gather(clock, cotangent, "cot")
    near_f = swap(at(piece_f), "y", "ny_f")
    full_qk = whole_weight(piece_qk, near_qk, far_qk, far_y_qk, 0, width)
    full_value = whole_weight(piece_r, near_r, far_value, far_y_value, 0, width)
    query, key, values, scores, hat, scale = attend(
        at(coord), decay_mask, normed, full_qk, full_value, key_size
    )

    clock.done(query, far_out, far_y_swish, *gather.first)
    far_upgate = far_half(at(third(piece_f, 0, 2)), "zh_upgate")
    far_y_out = swap(at(far_out), "y", "fy_out")
    grad_rows = gather.finish(clock)
    full_swish = whole_weight(piece_r, near_r, far_swish, far_y_swish, width, width)
    full_out = whole_weight(piece_r, near_r, far_out, far_y_out, 2 * width, width)
    clock.done(far_y_out, *grad_rows)
    swish_in, gated, *partial = branch(at(coord), hat, normed, full_swish, full_out)
    scatter = Scatter(*partial, "branch")
    scatter.relay(clock)
    clock.done(scatter.diag)
    scatter.send(clock)
    middle = rows_local + scatter.finish()

    clock.done(far_upgate, near_f, *scatter.last)
    far_down = far_half(at(third(piece_f, 2)), "zh_down")
    far_y_upgate = swap(at(far_upgate), "y", "fy_upgate")
    gather = Gather(clock, layer_norm(middle, norm2_gain).astype(bf16), "two")
    clock.done(far_down, *gather.first)
    far_y_down = swap(at(far_down), "y", "fy_down")
    normed_two = gather.finish(clock)
    full_upgate = whole_weight(piece_f, near_f, far_upgate, far_y_upgate, 0, 2 * width)
    full_down = whole_weight(piece_f, near_f, far_down, far_y_down, 2 * width, width)
    hidden, grad_up_rows, grad_gate_rows, *partial = feed_forward(
        coord, normed_two, grad_rows, full_upgate, full_down
    )

    scatter = Scatter(*partial, "back_two")
    clock.done(scatter.diag)
    scatter.relay(clock)
    g_up, g_gate = weight_grads(at(coord), normed_two, [grad_up_rows, grad_gate_rows])
    clock.done(*scatter.second, g_up[0])
    scatter.send(clock)
    y_up = send_y(at(g_up[0]))
    (g_down,) = weight_grads(at(coord), grad_rows, [hidden])
    back_two_local = scatter.finish()
    _, norm_two_pull = jax.vjp(layer_norm, middle, norm2_gain)
    grad_mid_norm, grad_norm2_local = norm_two_pull(back_two_local)
    grad_middle = cotangent.astype(f32) + grad_mid_norm
    grad_branch_local = grad_middle.astype(bf16)

    clock.done(y_up, g_down[0], grad_branch_local)
    gather = Gather(clock, grad_branch_local, "gb")
    y_gate = send_y(at(g_gate[0]))
    up = scatter_zh(*scatter_y(g_up[1], at(y_up)), "zh_gup")
    feed = Scatter(*back(at(coord), [hidden], [full_down]), "feed")
    clock.done(y_gate, up, feed.diag, feed.rest, *gather.first)
    grad_branch = gather.finish(clock)
    y_down = send_y(at(g_down[0]))
    gate = scatter_zh(*scatter_y(g_gate[1], at(y_gate)), "zh_ggate")

    clock.done(*grad_branch)
    feed.relay(clock)
    (g_out,) = weight_grads(at(coord), grad_branch, [gated])
    clock.done(g_out[0], gate, y_down, *feed.second)
    feed.send(clock)
    y_out = send_y(at(g_out[0]))
    down = scatter_zh(*scatter_y(g_down[1], at(y_down)), "zh_gdown")
    grad_qk, grad_values, grad_swish_in = attend_back(
        at(coord),
        decay_mask,
        swish_in,
        hat,
        scale,
        scores,
        query,
        key,
        values,
        grad_branch,
        full_out,
    )
    clock.done(grad_qk, down, y_out, *feed.last)
    mixed = (middle + feed.finish()).astype(bf16)
    out = scatter_zh(*scatter_y(g_out[1], at(y_out)), "zh_gout")
    grad_ff = group_exchange(at(jnp.concatenate([up, gate, down], 2)))
    (g_swish,) = weight_grads(at(coord), normed, [grad_swish_in])
    clock.done(g_swish[0])
    y_swish = send_y(at(g_swish[0]))
    g_value, g_qk = weight_grads(at(coord), normed, [grad_values, grad_qk])
    clock.done(g_value[0], out, y_swish, grad_ff)
    y_value = send_y(at(g_value[0]))
    swish = scatter_zh(*scatter_y(g_swish[1], at(y_swish)), "zh_gswish")
    partial = back(
        at(coord), [grad_qk, grad_values, grad_swish_in], [full_qk, full_value, full_swish]
    )
    scatter = Scatter(*partial, "back_one")
    scatter.relay(clock)
    clock.done(y_value, swish, *scatter.second)
    y_qk = send_y(at(g_qk[0]))
    value = scatter_zh(*scatter_y(g_value[1], at(y_value)), "zh_gvalue")
    scatter.send(clock)
    back_one_local = scatter.finish()
    clock.done(y_qk, value, *scatter.last)
    grad_qk = scatter_zh(*scatter_y(g_qk[1], at(y_qk)), "zh_gqk")
    grad_r = group_exchange(at(jnp.concatenate([out, swish, value], 2)))
    grad_qk = group_exchange(after(grad_qk, grad_r))

    def columns(g):
        return g.transpose(1, 0, 2).reshape(rows_q, -1).astype(f32)

    def rows(g):
        return g.transpose(0, 2, 1).reshape(-1, rows_q).astype(f32)

    grad_up, grad_gate = columns(grad_ff[:, :, :width]), columns(grad_ff[:, :, width : 2 * width])
    grad_down = rows(grad_ff[:, :, 2 * width :])
    grad_query, grad_key = columns(grad_qk[:, :, :key_size]), columns(grad_qk[:, :, key_size:])
    grad_out, grad_swish = rows(grad_r[:, :, :width]), columns(grad_r[:, :, width : 2 * width])
    grad_value = columns(grad_r[:, :, 2 * width :])

    _, norm_one_pull = jax.vjp(layer_norm, rows_local, norm1_gain)
    grad_tok_norm, grad_norm1_local = norm_one_pull(back_one_local)
    grad_tokens = grad_middle + grad_tok_norm
    grad_norm1, grad_norm2 = sum_everywhere(jnp.stack([grad_norm1_local, grad_norm2_local]))
    return (
        mixed,
        grad_tokens,
        grad_norm1,
        grad_query,
        grad_key,
        grad_value,
        grad_swish,
        grad_out,
        grad_norm2,
        grad_up,
        grad_gate,
        grad_down,
    )


def solution(mesh):
    dp, tensor = mesh.shape["dp"], mesh.shape["tensor"]
    grid = Mesh(mesh.devices.reshape(dp // 8, 2, 2, 2, tensor), SPREAD + ("tensor",))
    rows = P(SPREAD + ("tensor",), None)
    rows_split = P(SPREAD, "tensor")
    columns_split = P("tensor", SPREAD)
    return jax.shard_map(
        local,
        mesh=grid,
        in_specs=(
            rows,
            P(SPREAD),
            P("tensor"),
            P(),
            rows_split,
            rows_split,
            rows_split,
            rows_split,
            columns_split,
            P(),
            rows_split,
            rows_split,
            columns_split,
            rows,
        ),
        out_specs=(
            rows,
            rows,
            P(),
            rows_split,
            rows_split,
            rows_split,
            rows_split,
            columns_split,
            P(),
            rows_split,
            rows_split,
            columns_split,
        ),
        check_vma=False,
    )
```

```python
import functools
import jax
import jax.numpy as jnp
from jax import lax
from jax.experimental import pallas as pl
from jax.experimental.pallas import tpu as pltpu
from jax.sharding import Mesh, PartitionSpec as P

epsilon = 1e-05
bf16 = jnp.bfloat16
f32 = jnp.float32
SPREAD = ("zh", "zl", "y", "x")
GROUP = ("zl", "x")


def normalize(values):
    centred = values - jnp.mean(values, axis=-1, keepdims=True)
    variance = jnp.mean(centred * centred, axis=-1, keepdims=True)
    return centred * lax.rsqrt(variance + epsilon)


def layer_norm(rows, gain):
    return normalize(rows) * gain


def dot(left, right, dims):
    return lax.dot_general(left, right, (dims, ((), ())), preferred_element_type=f32)


NN = ((1,), (0,))
NT = ((1,), (1,))
TN = ((0,), (0,))


def swap(a, axis, label="move"):
    with jax.named_scope(label):
        return lax.ppermute(a, axis, [(0, 1), (1, 0)])


def after(value, *others):
    return lax.optimization_barrier((value,) + others)[0]


def ordered(own, other, axis, dim):
    first = lax.axis_index(axis) == 0
    return jnp.stack([jnp.where(first, own, other), jnp.where(first, other, own)], dim)


def by_quarter(w):
    rows, cols = w.shape
    return w.reshape(rows, 4, cols // 4).transpose(1, 0, 2)


def beside(*parts):
    return jnp.concatenate(parts, 2)


def group_exchange(parts):
    return lax.all_to_all(parts, GROUP, 0, 0, tiled=True)


def take(a, index, dim):
    return lax.dynamic_index_in_dim(a, index, dim, keepdims=False)


def add(a, b):
    return (a.astype(f32) + b.astype(f32)).astype(bf16)


def scatter_y(keep, got):
    n = got.shape[-1]
    if lax.axis_size("zh") == 2:
        return add(keep[:2], got[:2]), add(keep[2:], got[2:])
    flip = lambda g: jnp.flip(g.reshape(2, 2, 1, -1, n), 0)
    g = jnp.concatenate([flip(keep), flip(got)], 2).reshape(lax.axis_size("zh"), 2, 2, 2, -1, n)
    y = lax.axis_index("y")
    return add(take(g, y, 2), swap(take(g, 1 - y, 2), "y")), None


def send_y(send, label):
    return swap(send, "y", label) if lax.axis_size("zh") == 2 else send


def send_zh(send, label):
    return swap(send, "zh", label) if lax.axis_size("zh") == 2 else send


def scatter_zh(keep, got):
    if lax.axis_size("zh") == 2:
        g = add(keep, got)
    else:
        g = lax.psum_scatter(got, "zh", scatter_dimension=0)
    return g.reshape(4, -1, g.shape[-1])


class WeightGrad:
    def __init__(self, pair, label):
        self.send, self.keep, self.label = *pair, label

    def to_y(self, clock):
        self.y = send_y(clock.at(self.send), "y_" + self.label)

    def to_zh(self, clock):
        send, self.keep = scatter_y(self.keep, clock.at(self.y))
        self.zh = send_zh(send, "zh_g" + self.label)

    def sum(self, clock):
        return scatter_zh(self.keep, clock.at(self.zh))


class Clock:
    def __init__(self):
        self.now = ()

    def done(self, *values):
        self.now = values

    def at(self, value):
        return after(value, *self.now)

    def at_all(self, values):
        return lax.optimization_barrier(tuple(values) + self.now)[: len(values)]


class Plan:
    def __init__(self, count, rows, width, column):
        self.count, self.rows, self.width, self.column = count, rows, width, column


class Weight:
    def __init__(self, arrays, plan):
        self.arrays, self.plan = arrays, plan


class Unit:
    def __init__(self, arrays, rows):
        self.arrays, self.rows = arrays, rows

    def weight(self, column, width):
        return Weight(self.arrays, Plan(len(self.arrays), self.rows, width, column))


class WeightPipe:
    def __init__(self):
        self.last = None

    def step(self, clock, piece, label):
        piece = clock.at(piece)
        if lax.axis_size("zh") != 2:
            whole = gather_weight(piece)
            self.moved = (whole,)
            return Unit([whole], piece.shape[1])
        far, near = swap(piece, "zh", "zh_" + label), swap(piece, "y", "ny_" + label)
        self.moved = (far, near)
        self.carry(clock)
        self.last = Unit([piece, near, far], piece.shape[1])
        self.label = label
        return self.last

    def carry(self, clock):
        if self.last is not None:
            far_y = swap(clock.at(self.last.arrays[2]), "y", "fy_" + self.label)
            self.last.arrays.append(far_y)
            self.moved += (far_y,)

    def finish(self, clock):
        self.moved = ()
        self.carry(clock)
        return self.moved


def gather_weight(piece):
    return lax.all_gather(piece, ("zh", "y"), axis=0)


class Gather:
    def __init__(self, clock, a, label, halves=False):
        self.a, self.label, self.halves = clock.at(a), label, halves
        self.x = swap(self.a, "x", label + "_x")
        self.z = swap(self.a, "zl", label + "_z")
        self.c = swap(self.a, "tensor", label + "_c")
        self.first = (self.x, self.z, self.c)

    def second(self, clock):
        half, label = self.a.shape[0] // 2, self.label
        ax, az = clock.at_all((self.x, self.z))
        if self.halves:
            self.diag = (swap(az[:half], "x", label + "_dx"), swap(ax[half:], "zl", label + "_dz"))
        else:
            self.diag = (swap(az, "x", label + "_dx"),)
        self.pieces = [self.a, self.c]
        self.pieces += [ax, swap(ax, "tensor", label + "_c"), az, swap(az, "tensor", label + "_c")]
        self.held = (*self.pieces, *self.diag)

    def finish(self, clock):
        diag = clock.at_all(self.diag)
        return [*self.pieces, *diag, *(swap(d, "tensor", self.label + "_c") for d in diag)]


class Scatter:
    def __init__(self, send_rest, send_diag, keep, label, clock):
        self.label, self.keep = label, keep
        send_rest, send_diag = clock.at_all((send_rest, send_diag))
        self.diag = add(keep[3], swap(send_diag, "tensor", label + "_cd"))
        self.rest = swap(send_rest, "tensor", label + "_cr")

    def relay(self, clock):
        half = self.diag.shape[0] // 2
        diag = clock.at(self.diag)
        self.through_x = swap(diag[:half], "x", self.label + "_dx")
        self.through_z = swap(diag[half:], "zl", self.label + "_dz")
        self.second = (self.through_x, self.through_z, self.rest)

    def send(self, clock):
        through_x, through_z, rest = (v.astype(f32) for v in clock.at_all(self.second))
        half = through_x.shape[0]
        self.own, xmate, zmate = (self.keep[r].astype(f32) + rest[r] for r in range(3))
        zmate = jnp.concatenate([zmate[:half] + through_x, zmate[half:]]).astype(bf16)
        xmate = jnp.concatenate([xmate[:half], xmate[half:] + through_z]).astype(bf16)
        self.x = swap(xmate, "x", self.label + "_x")
        self.z = swap(zmate, "zl", self.label + "_z")
        self.last = (self.x, self.z)

    def finish(self, clock):
        x, z = clock.at_all(self.last)
        return self.own + x.astype(f32) + z.astype(f32)


VMEM_LIMIT = 60 * 2**20
WHOLE = tuple((i // 2, i, 0, 1) for i in range(8))
HALVES = WHOLE[:6] + tuple((3, slot, part, 2) for slot in (6, 7) for part in (0, 1))
ANY = pl.BlockSpec(memory_space=pl.ANY)
SMEM = pl.BlockSpec(memory_space=pltpu.SMEM)


class Loader:
    def __init__(self, sems):
        self.sems, self.used = sems, 0

    def copy(self, src, dst):
        self.used += 1
        return pltpu.make_async_copy(src, dst, self.sems.at[self.used - 1])

    def tokens(self, refs, held, coord):
        rows = held.shape[1]
        chips = [[], [], [], []]
        if len(refs) == 1:
            for slot in range(8):
                other = 2 * ((slot // 2) ^ coord[2]) + ((slot % 2) ^ coord[3])
                chips[slot // 2].append(self.copy(refs[0].at[other], held.at[slot]))
            return chips
        for ref, (chip, slot, part, parts) in zip(refs, HALVES if len(refs) == 10 else WHOLE):
            size = rows // parts
            chips[chip].append(self.copy(ref, held.at[slot, pl.ds(part * size, size)]))
        return chips

    def weight(self, refs, plan, held, coord):
        copies = []
        columns = pl.ds(plan.column, plan.width)
        if len(refs) == 4:
            for i, ref in enumerate(refs):
                zh, y = coord[0] ^ (i // 2), coord[1] ^ (i % 2)
                for zl in range(2):
                    block = ref.at[pl.ds(2 * zl, 2), :, columns]
                    row = ((zh * 2 + zl) * 2 + y) * 2
                    copies.append(self.copy(block, held.at[pl.ds(row, 2)]))
            return copies
        for i in range(refs[0].shape[0]):
            for zl in range(2):
                block = refs[0].at[i, pl.ds(2 * zl, 2), :, columns]
                row = ((i // 2 * 2 + zl) * 2 + i % 2) * 2
                copies.append(self.copy(block, held.at[pl.ds(row, 2)]))
        return copies


def start(*copies):
    for c in copies:
        c.start()


def wait(*copies):
    for c in copies:
        c.wait()


def at_chip(r, chips):
    for i, copies in enumerate(chips):
        pl.when(r == i)(functools.partial(wait, *copies))


def rows_of(held, r):
    pair = held[pl.ds(2 * r, 2)]
    return pair.reshape(2 * pair.shape[1], pair.shape[2])


def flat(w):
    value = w[...]
    return value.reshape(value.shape[0] * value.shape[1], value.shape[2])


def by_chip(shape):
    return pl.BlockSpec((1,) + shape, lambda r: (r,) + (0,) * len(shape))


def chip_kernel(body, operands, specs, outs, out_specs, scratch, copies, flops):
    moved = sum(a.size * a.dtype.itemsize for a in operands) + sum(
        o.size * jnp.dtype(o.dtype).itemsize for o in outs
    )
    return pl.pallas_call(
        body,
        grid=(4,),
        in_specs=specs,
        out_specs=out_specs,
        out_shape=outs,
        scratch_shapes=scratch + [pltpu.SemaphoreType.DMA((copies,))],
        compiler_params=pltpu.CompilerParams(
            dimension_semantics=("arbitrary",), vmem_limit_bytes=VMEM_LIMIT
        ),
        cost_estimate=pl.CostEstimate(flops=flops, bytes_accessed=moved, transcendentals=0),
    )(*operands)


def held_tokens(pieces):
    return pltpu.VMEM((8,) + pieces[0].shape[-2:], bf16)


def held_weight(w):
    devices = 16 if w.plan.count == 4 else 4 * w.arrays[0].shape[0]
    return pltpu.VMEM((devices, w.plan.rows, w.plan.width), bf16)


def arrays(*weights):
    return [a for w in weights for a in w.arrays]


def copies_of(*weights):
    return sum(8 if w.plan.count == 4 else 2 * w.arrays[0].shape[0] for w in weights)


def struct(shape, dtype):
    return jax.ShapeDtypeStruct(shape, dtype)


def partial_rows(grads, helds, r, keep, store):
    rows, blocks = keep.shape[1], helds[0].shape[0] // 4
    size = blocks * helds[0].shape[1]
    for j in range(4):
        parts = [
            dot(g, h[j * blocks : (j + 1) * blocks].reshape(size, h.shape[2]), NT)
            for g, h in zip(grads, helds)
        ]
        out = sum(parts[1:], parts[0]).astype(bf16)
        keep[0, :, j * size : (j + 1) * size] = out[:rows]
        store[r, :, j * size : (j + 1) * size] = out[rows:]


def send_copies(load, store, rest, diag):
    return [load.copy(store.at[i], rest.at[i]) for i in range(3)] + [load.copy(store.at[3], diag)]


def at_chip_start(r, copies):
    for i, c in enumerate(copies):
        pl.when(r == i)(c.start)

    @pl.when(r == 3)
    def _():
        wait(*copies)


def partial_outs(rows, model):
    outs = [
        struct((3, rows, model), bf16),
        struct((rows, model), bf16),
        struct((4, rows, model), bf16),
    ]
    return outs, [ANY, ANY, by_chip((rows, model))]


def attend_body(tokens, f_qk, f_v, coord, mask, *refs):
    acts, refs = refs[:tokens], refs[tokens:]
    wqk, refs = refs[: f_qk.count], refs[f_qk.count :]
    wv, refs = refs[: f_v.count], refs[f_v.count :]
    q_out, k_out, v_out, score_out, hat_out, scale_out, held, held_qk, held_v, sems = refs
    load, r = Loader(sems), pl.program_id(0)
    w1 = load.weight(wqk, f_qk, held_qk, coord)
    chips = load.tokens(acts, held, coord)
    w2 = load.weight(wv, f_v, held_v, coord)

    @pl.when(r == 0)
    def _():
        start(*w1, *chips[0], *w2, *chips[1], *chips[2], *chips[3])
        wait(*w1)

    at_chip(r, chips)
    x = rows_of(held, r)
    qk = dot(x, flat(held_qk), NN).astype(bf16)
    size = qk.shape[1] // 2
    q, k = qk[:, :size], qk[:, size:]
    q_out[0], k_out[0] = q, k
    scores = (dot(q, k, NT) * mask[0]).astype(bf16)
    score_out[0] = scores

    @pl.when(r == 0)
    def _():
        wait(*w2)

    v = dot(x, flat(held_v), NN).astype(bf16)
    v_out[0] = v
    hat_out[0] = dot(scores, v, NN)
    rows, step = hat_out.shape[1], 32

    def chunk(i, carry):
        at = pl.ds(pl.multiple_of(i * step, step), step)
        part = hat_out[0, at, :]
        part = part - jnp.mean(part, axis=-1, keepdims=True)
        scale = lax.rsqrt(jnp.mean(part * part, axis=-1, keepdims=True) + epsilon)
        hat_out[0, at, :] = part * scale
        scale_out[0, at, :] = jnp.broadcast_to(scale, (step, 128))
        return carry

    lax.fori_loop(0, rows // step, chunk, 0)


def attend(coord, mask, acts, wqk, wv, key_size):
    length, n = mask.shape[1], wv.plan.width
    model = acts[0].shape[-1]
    outs = [
        struct((4, length, key_size), bf16),
        struct((4, length, key_size), bf16),
        struct((4, length, n), bf16),
        struct((4, length, length), bf16),
        struct((4, length, n), f32),
        struct((4, length, 128), f32),
    ]
    return chip_kernel(
        functools.partial(attend_body, len(acts), wqk.plan, wv.plan),
        [coord, mask, *acts, *arrays(wqk, wv)],
        [SMEM, by_chip((length, length))] + [ANY] * (len(acts) + len(arrays(wqk, wv))),
        outs,
        [by_chip(o.shape[1:]) for o in outs],
        [held_tokens(acts), held_weight(wqk), held_weight(wv)],
        10 + copies_of(wqk, wv),
        16 * length * model * n,
    )


def branch_body(tokens, f_s, f_o, coord, hat, *refs):
    acts, refs = refs[:tokens], refs[tokens:]
    ws, refs = refs[: f_s.count], refs[f_s.count :]
    wo, refs = refs[: f_o.count], refs[f_o.count :]
    s_out, gated_out, rest, diag, keep, held, held_s, held_o, store, sems = refs
    load, r = Loader(sems), pl.program_id(0)
    w1 = load.weight(ws, f_s, held_s, coord)
    chips = load.tokens(acts, held, coord)
    w2 = load.weight(wo, f_o, held_o, coord)
    sends = send_copies(load, store, rest, diag)

    @pl.when(r == 0)
    def _():
        start(*w1, *chips[0], *w2, *chips[1], *chips[2], *chips[3])
        wait(*w1)

    at_chip(r, chips)
    s_out[0] = dot(rows_of(held, r), flat(held_s), NN)
    rows, step = s_out.shape[1], 32

    def chunk(i, carry):
        at = pl.ds(pl.multiple_of(i * step, step), step)
        s = s_out[0, at, :]
        gated_out[0, at, :] = (s / (1.0 + jnp.exp(-s)) * hat[0, at, :]).astype(bf16)
        return carry

    lax.fori_loop(0, rows // step, chunk, 0)

    @pl.when(r == 0)
    def _():
        wait(*w2)

    partial_rows([gated_out[0]], [held_o], r, keep, store)
    at_chip_start(r, sends)


def branch(coord, hat, acts, ws, wo):
    length, n = hat.shape[1:]
    rows, model = acts[0].shape[-2:]
    outs, out_specs = partial_outs(rows, model)
    outs = [struct((4, length, n), f32), struct((4, length, n), bf16)] + outs
    return chip_kernel(
        functools.partial(branch_body, len(acts), ws.plan, wo.plan),
        [coord, hat, *acts, *arrays(ws, wo)],
        [SMEM, by_chip((length, n))] + [ANY] * (len(acts) + len(arrays(ws, wo))),
        outs,
        [by_chip((length, n)), by_chip((length, n))] + out_specs,
        [held_tokens(acts), held_weight(ws), held_weight(wo), pltpu.VMEM((4, rows, model), bf16)],
        14 + copies_of(ws, wo),
        16 * length * model * n,
    )


def feed_body(tokens, others, f_u, f_g, f_d, coord, *refs):
    acts, cots, refs = refs[:tokens], refs[tokens : tokens + others], refs[tokens + others :]
    wu, refs = refs[: f_u.count], refs[f_u.count :]
    wg, refs = refs[: f_g.count], refs[f_g.count :]
    wd, refs = refs[: f_d.count], refs[f_d.count :]
    hidden_out, up_out, gate_out, rest, diag, keep = refs[:6]
    held, held_c, held_u, held_g, held_d, store, up, gate, gh, sems = refs[6:]
    load, r = Loader(sems), pl.program_id(0)
    w1 = load.weight(wu, f_u, held_u, coord)
    w2 = load.weight(wg, f_g, held_g, coord)
    w3 = load.weight(wd, f_d, held_d, coord)
    chips = load.tokens(acts, held, coord)
    chips_c = load.tokens(cots, held_c, coord)
    sends = send_copies(load, store, rest, diag)

    @pl.when(r == 0)
    def _():
        start(*w3, *chips_c[0], *w1, *chips[0], *w2)
        for i in range(1, 4):
            start(*chips_c[i], *chips[i])
        wait(*w3)

    at_chip(r, chips_c)
    gh[...] = dot(rows_of(held_c, r), flat(held_d), NN)

    @pl.when(r == 0)
    def _():
        wait(*w1)

    at_chip(r, chips)
    x = rows_of(held, r)
    up[...] = dot(x, flat(held_u), NN)

    @pl.when(r == 0)
    def _():
        wait(*w2)

    gate[...] = dot(x, flat(held_g), NN)
    step = 16

    def chunk(i, carry):
        at = pl.ds(pl.multiple_of(i * step, step), step)
        u, g, e = up[at, :], gate[at, :], gh[at, :]
        c = 0.7978845608028654
        square = g * g
        t = jnp.tanh(c * g * (1.0 + 0.044715 * square))
        half = 0.5 * (1.0 + t)
        gelu = g * half
        slope = half + (0.5 * c) * g * (1.0 - t * t) * (1.0 + (3 * 0.044715) * square)
        hidden_out[0, at, :] = (gelu * u).astype(bf16)
        up_out[0, at, :] = (e * gelu).astype(bf16)
        gate_out[0, at, :] = (e * u * slope).astype(bf16)
        return carry

    lax.fori_loop(0, gh.shape[0] // step, chunk, 0)
    partial_rows([up_out[0], gate_out[0]], [held_u, held_g], r, keep, store)
    at_chip_start(r, sends)


def feed_forward(coord, acts, cots, wu, wg, wd):
    rows, model = acts[0].shape[-2:]
    n = wd.plan.width
    outs, out_specs = partial_outs(rows, model)
    outs = [struct((4, 2 * rows, n), bf16)] * 3 + outs
    return chip_kernel(
        functools.partial(feed_body, len(acts), len(cots), wu.plan, wg.plan, wd.plan),
        [coord, *acts, *cots, *arrays(wu, wg, wd)],
        [SMEM] + [ANY] * (len(acts) + len(cots) + len(arrays(wu, wg, wd))),
        outs,
        [by_chip((2 * rows, n))] * 3 + out_specs,
        [
            held_tokens(acts),
            held_tokens(cots),
            held_weight(wu),
            held_weight(wg),
            held_weight(wd),
            pltpu.VMEM((4, rows, model), bf16),
        ]
        + [pltpu.VMEM((2 * rows, n), f32)] * 3,
        24 + copies_of(wu, wg, wd),
        80 * rows * model * n,
    )


def back_body(plans, whole, coord, *refs):
    count = len(plans)
    weights = []
    grads, refs = refs[:count], refs[count:]
    for plan in plans:
        weights.append(refs[: plan.count])
        refs = refs[plan.count :]
    load, r = Loader(refs[-1]), pl.program_id(0)
    if whole:
        result, helds, keep, store = refs[0], refs[1 : 1 + count], refs[-3], refs[-2]
    else:
        rest, diag, keep, helds, store = *refs[:3], refs[3 : 3 + count], refs[-2]
    copies = [load.weight(w, p, h, coord) for w, p, h in zip(weights, plans, helds)]

    @pl.when(r == 0)
    def _():
        for c in copies:
            start(*c)
        for c in copies:
            wait(*c)

    if not whole:
        sends = send_copies(load, store, rest, diag)
        partial_rows([g[0] for g in grads], helds, r, keep, store)
        at_chip_start(r, sends)
        return
    sends = []
    for i in range(4):
        at = 2 * (i ^ coord[2])
        sends.append(
            (
                load.copy(keep.at[i], result.at[at + coord[3]]),
                load.copy(store.at[i], result.at[at + (1 ^ coord[3])]),
            )
        )
    partial_rows([g[0] for g in grads], helds, r, keep.at[pl.ds(r, 1)], store)
    for i in range(4):
        pl.when(r == i)(functools.partial(start, *sends[i]))

    @pl.when(r == 3)
    def _():
        for c in sends:
            wait(*c)


def back(coord, grads, weights, whole=False):
    length = grads[0].shape[1]
    rows = length // 2
    held = held_weight(weights[0])
    model = held.shape[0] * held.shape[1]
    outs, out_specs = partial_outs(rows, model)
    store = pltpu.VMEM((4, rows, model), bf16)
    if whole:
        outs, out_specs = [struct((8, rows, model), bf16)], [ANY]
    return chip_kernel(
        functools.partial(back_body, tuple(w.plan for w in weights), whole),
        [coord, *grads, *arrays(*weights)],
        [SMEM] + [by_chip(g.shape[1:]) for g in grads] + [ANY] * len(arrays(*weights)),
        outs,
        out_specs,
        [held_weight(w) for w in weights] + [store] * (2 if whole else 1),
        8 + copies_of(*weights),
        8 * length * model * sum(g.shape[2] for g in grads),
    )


def attend_back_body(tokens, f_o, coord, mask, s, hat, scale, scores, q, k, v, *refs):
    acts, refs = refs[:tokens], refs[tokens:]
    wo, refs = refs[: f_o.count], refs[f_o.count :]
    gqk_out, gv_out, gs_out, held, held_o, dg, gr, sems = refs
    load, r = Loader(sems), pl.program_id(0)
    w1 = load.weight(wo, f_o, held_o, coord)
    chips = load.tokens(acts, held, coord)

    @pl.when(r == 0)
    def _():
        start(*w1, *chips[0], *chips[1], *chips[2], *chips[3])
        wait(*w1)

    at_chip(r, chips)
    dg[...] = dot(rows_of(held, r), flat(held_o), NN)
    rows, step = dg.shape[0], 16

    def chunk(i, carry):
        at = pl.ds(pl.multiple_of(i * step, step), step)
        e, x, v_s = dg[at, :], hat[0, at, :], s[0, at, :]
        gate = 1.0 / (1.0 + jnp.exp(-v_s))
        silu = v_s * gate
        gs_out[0, at, :] = (e * x * (gate + silu * (1.0 - gate))).astype(bf16)
        f = e * silu
        f = f - jnp.mean(f, axis=-1, keepdims=True) - x * jnp.mean(f * x, axis=-1, keepdims=True)
        gr[at, :] = (f * scale[0, at, :1]).astype(bf16)
        return carry

    lax.fori_loop(0, rows // step, chunk, 0)
    grad_retained = gr[...]
    gv_out[0] = dot(scores[0], grad_retained, TN).astype(bf16)
    raw = (dot(grad_retained, v[0], NT) * mask[0]).astype(bf16)
    size = q.shape[2]
    gqk_out[0, :, :size] = dot(raw, k[0], NN).astype(bf16)
    gqk_out[0, :, size:] = dot(raw, q[0], TN).astype(bf16)


def attend_back(coord, mask, s, hat, scale, scores, q, k, v, acts, wo):
    length, n = s.shape[1:]
    model = acts[0].shape[-1]
    blocks = [mask, s, hat, scale, scores, q, k, v]
    outs = [struct((4, length, 2 * q.shape[2]), bf16)] + [struct((4, length, n), bf16)] * 2
    return chip_kernel(
        functools.partial(attend_back_body, len(acts), wo.plan),
        [coord, *blocks, *acts, *arrays(wo)],
        [SMEM] + [by_chip(b.shape[1:]) for b in blocks] + [ANY] * (len(acts) + len(arrays(wo))),
        outs,
        [by_chip(o.shape[1:]) for o in outs],
        [
            held_tokens(acts),
            held_weight(wo),
            pltpu.VMEM((length, n), f32),
            pltpu.VMEM((length, n), bf16),
        ],
        10 + copies_of(wo),
        12 * length * model * n,
    )


def weight_grad_body(count, tokens, whole, coord, *refs):
    grads, refs = refs[:count], refs[count:]
    acts, refs = refs[:tokens], refs[tokens:]
    outs, held, sems = refs[:-2], refs[-2], refs[-1]
    load, i = Loader(sems), pl.program_id(0)
    chips = load.tokens(acts, held, coord)

    @pl.when(i == 0)
    def _():
        for c in chips:
            start(*c)
        for c in chips:
            wait(*c)

    width = held.shape[2] // 8
    j = i % 4
    if whole:
        column = ((i // 4 * 2 + i % 2) * 2 + i // 2 % 2) * width
    else:
        y = coord[1] ^ jnp.where(i < 4, 1, 0)
        zh = coord[0] ^ jnp.where(j < 2, 1, 0)
        column = ((zh * 2 + j % 2) * 2 + y) * width
    x = held[:, :, pl.ds(pl.multiple_of(column, width), width)]
    x = x.reshape(x.shape[0] * x.shape[1], width).T
    for n in range(count):
        g = grads[n][...]
        size = g.shape[2]
        out = dot(x, g.reshape(g.shape[0] * g.shape[1], size), NN).astype(bf16)
        if whole:
            outs[0][0, :, n * size : (n + 1) * size] = out
            continue
        pl.when(i < 4)(functools.partial(store_block, outs[2 * n], out))
        pl.when(i >= 4)(functools.partial(store_block, outs[2 * n + 1], out))


def store_block(ref, value):
    ref[0] = value


def weight_grads(coord, acts, grads, whole=False):
    rows, model = acts[0].shape[-2:]
    outs, out_specs = [], []
    width = sum(g.shape[2] for g in grads)
    for g in grads:
        shape = (4, model // 8, g.shape[2])
        outs += [struct(shape, bf16)] * 2
        out_specs += [
            pl.BlockSpec((1,) + shape[1:], lambda i: (jnp.minimum(i, 3), 0, 0)),
            pl.BlockSpec((1,) + shape[1:], lambda i: (jnp.maximum(i - 4, 0), 0, 0)),
        ]
    if whole:
        outs = [struct((8, model // 8, width), bf16)]
        out_specs = [pl.BlockSpec((1, model // 8, width), lambda i: (i, 0, 0))]
    moved = sum(a.size * 2 for a in acts) + sum(g.size * 2 for g in grads) + 2 * model * width
    got = pl.pallas_call(
        functools.partial(weight_grad_body, len(grads), len(acts), whole),
        grid=(8,),
        in_specs=[SMEM] + [pl.BlockSpec(memory_space=pltpu.VMEM)] * len(grads) + [ANY] * len(acts),
        out_specs=out_specs,
        out_shape=outs,
        scratch_shapes=[held_tokens(acts), pltpu.SemaphoreType.DMA((10,))],
        compiler_params=pltpu.CompilerParams(
            dimension_semantics=("arbitrary",), vmem_limit_bytes=VMEM_LIMIT
        ),
        cost_estimate=pl.CostEstimate(
            flops=16 * rows * model * width, bytes_accessed=moved, transcendentals=0
        ),
    )(coord, *grads, *acts)
    if whole:
        return got[0]
    return [(got[2 * i], got[2 * i + 1]) for i in range(len(grads))]


def scatter_whole(g):
    zh, n = lax.axis_size("zh"), g.shape[2]
    if zh == 2:
        g = g.reshape(4, 4, -1, n)
    else:
        g = g.reshape(2, 2, 2, -1, n).transpose(0, 2, 1, 3, 4).reshape(zh, 2, 2, 2, -1, n)
        g = g.transpose(0, 2, 1, 3, 4, 5).reshape(2 * zh, 4, -1, n)
    g = lax.psum_scatter(g, ("zh", "y"), scatter_dimension=0, tiled=True)
    return g.reshape(4, -1, n)


def sum_everywhere(a):
    for axis in ("tensor",) + SPREAD:
        if lax.axis_size(axis) == 2:
            a = a + swap(a, axis)
        else:
            a = lax.psum(a, axis)
    return a


def local(
    tokens,
    segments,
    decay,
    norm1_gain,
    w_query,
    w_key,
    w_value,
    w_swish,
    w_out,
    norm2_gain,
    w_up,
    w_gate,
    w_down,
    cotangent,
):
    rows_q, width = w_query.shape[0], w_value.shape[1] // 4
    quarter = 2 * lax.axis_index("zl") + lax.axis_index("x")
    core = lax.axis_index("tensor")
    length = segments.shape[0]
    rows_each = tokens.shape[0]
    key_size = w_query.shape[1] // 4
    value_size = w_value.shape[1] // 4
    rate = take(decay, quarter, 0)

    ids = [jnp.zeros((), jnp.int32)] * 2
    if lax.axis_size("zh") == 2:
        ids = [lax.axis_index("zh"), lax.axis_index("y")]
    coord = jnp.stack(ids + [quarter, core]).astype(jnp.int32)
    clock, free = Clock(), Clock()
    at = clock.at
    rows_local = tokens.astype(f32)
    everyone = ("zl", "x", "tensor")

    pipe = WeightPipe()
    seg_x, seg_z = swap(segments, "x", "seg"), swap(segments, "zl", "seg")
    with jax.named_scope("seg"):
        seg_d = lax.ppermute(segments, GROUP, [(i, 3 - i) for i in range(4)])
    parts = (by_quarter(w) for w in (w_query, w_key, w_value))
    piece = group_exchange(beside(*parts))
    parts = beside(by_quarter(w_swish), by_quarter(w_out.T))

    clock.done(piece, seg_x, seg_z, seg_d, parts)
    unit_qkv = pipe.step(clock, piece, "qkv")
    piece = group_exchange(at(parts))
    normed_local = layer_norm(rows_local, norm1_gain).astype(bf16)
    normed = [lax.all_gather(at(normed_local), everyone, axis=0)]
    segs = jnp.stack([segments, seg_x, seg_z, seg_d])
    segs = jnp.where(core == 0, segs, jnp.roll(segs, length // 2, 1))
    position = (jnp.arange(length, dtype=jnp.int32) + core * rows_each) % length
    offset = position[:, None] - position[None, :]
    allowed = (offset >= 0)[None] & (segs[:, :, None] == segs[:, None, :])
    distance = jnp.maximum(offset, 0).astype(f32)
    decay_mask = jnp.where(allowed, jnp.exp(-rate * distance)[None], 0.0)
    parts = beside(by_quarter(at(w_up)), by_quarter(at(w_gate)))

    clock.done(piece, parts, decay_mask, *pipe.moved)
    unit_so = pipe.step(clock, piece, "so")
    piece = group_exchange(at(parts))
    parts = by_quarter(at(w_down).T)
    full_qk, full_value = unit_qkv.weight(0, width), unit_qkv.weight(width, width)
    query, key, values, scores, hat, scale = attend(
        at(coord), decay_mask, normed, full_qk, full_value, key_size
    )

    clock.done(query, piece, parts, *pipe.moved)
    unit_ug = pipe.step(clock, piece, "ug")
    piece = group_exchange(at(parts))
    grad_rows = [lax.all_gather(at(cotangent), everyone, axis=0)]
    full_swish, full_out = unit_so.weight(0, width), unit_so.weight(width, width)
    swish_in, gated, *partial = branch(at(coord), hat, normed, full_swish, full_out)
    clock.done(piece, *pipe.moved, *partial)
    unit_d = pipe.step(clock, piece, "d")
    scatter = Scatter(*partial, "branch", clock)
    scatter.relay(free)
    clock.done(*scatter.second)
    scatter.send(clock)
    clock.done(*scatter.last, *pipe.moved)
    middle = rows_local + scatter.finish(clock)
    normed_two_local = layer_norm(middle, norm2_gain).astype(bf16)
    gather = Gather(clock, normed_two_local, "two", True)
    far_y = pipe.finish(clock)
    clock.done(*far_y, *gather.first)
    gather.second(clock)
    clock.done(*gather.held)
    normed_two = gather.finish(clock)
    full_up, full_gate = unit_ug.weight(0, width), unit_ug.weight(width, width)
    full_down = unit_d.weight(0, width)
    hidden, grad_up_rows, grad_gate_rows, *partial = feed_forward(
        at(coord), normed_two, grad_rows, full_up, full_gate, full_down
    )

    scatter = Scatter(*partial, "back_two", free)
    clock.done(scatter.diag)
    scatter.relay(clock)
    g_up, g_gate = weight_grads(at(coord), normed_two, [grad_up_rows, grad_gate_rows])
    g_up, g_gate = WeightGrad(g_up, "up"), WeightGrad(g_gate, "gate")
    clock.done(g_up.send, *scatter.second)
    scatter.send(clock)
    g_up.to_y(clock)
    (g_down,) = weight_grads(at(coord), grad_rows, [hidden])
    g_down = WeightGrad(g_down, "down")
    clock.done(g_down.send, g_up.y, *scatter.last)
    back_two_local = scatter.finish(clock)
    _, norm_two_pull = jax.vjp(layer_norm, middle, norm2_gain)
    grad_mid_norm, grad_norm2_local = norm_two_pull(back_two_local)
    grad_middle = cotangent.astype(f32) + grad_mid_norm
    grad_branch_local = grad_middle.astype(bf16)

    clock.done(grad_branch_local)
    gather = Gather(clock, grad_branch_local, "gb", True)
    g_gate.to_y(clock)
    clock.done(g_gate.y, *gather.first)
    gather.second(clock)
    g_down.to_y(clock)
    (feed,) = back(at(coord), [hidden], [full_down], True)
    clock.done(feed, *gather.held)
    grad_branch = gather.finish(clock)
    feed = lax.psum_scatter(at(feed), everyone, scatter_dimension=0, tiled=True)
    g_up.to_zh(clock)
    grad_qk, grad_values, grad_swish_in = attend_back(
        at(coord),
        decay_mask,
        swish_in,
        hat,
        scale,
        scores,
        query,
        key,
        values,
        grad_branch,
        full_out,
    )
    clock.done(grad_qk, g_up.zh, g_down.y)
    g_gate.to_zh(clock)
    (g_out,) = weight_grads(at(coord), grad_branch, [gated])
    g_out = WeightGrad(g_out, "out")
    clock.done(g_out.send)
    g_out.to_y(clock)
    (g_swish,) = weight_grads(at(coord), normed, [grad_swish_in])
    g_swish = WeightGrad(g_swish, "swish")
    clock.done(g_swish.send, g_gate.zh)
    g_down.to_zh(clock)
    g_swish.to_y(clock)
    g_value, g_qk = weight_grads(at(coord), normed, [grad_values, grad_qk])
    g_value, g_qk = WeightGrad(g_value, "value"), WeightGrad(g_qk, "qk")
    clock.done(g_value.send, g_down.zh, g_out.y)
    g_out.to_zh(clock)
    g_value.to_y(clock)
    partial = back(
        at(coord), [grad_qk, grad_values, grad_swish_in], [full_qk, full_value, full_swish]
    )
    clock.done(g_out.zh, g_swish.y, *partial)
    g_swish.to_zh(clock)
    scatter = Scatter(*partial, "back_one", clock)
    clock.done(scatter.diag)
    scatter.relay(clock)
    grad_ff = group_exchange(beside(g_up.sum(clock), g_gate.sum(clock), g_down.sum(clock)))
    clock.done(g_value.y, *scatter.second)
    g_qk.to_y(clock)
    scatter.send(clock)
    clock.done(g_swish.zh)
    g_value.to_zh(clock)
    clock.done(grad_ff, *scatter.last)
    back_one_local = scatter.finish(clock)
    grad_os = group_exchange(beside(g_out.sum(clock), g_swish.sum(clock)))
    clock.done(g_qk.y, g_value.zh)
    g_qk.to_zh(clock)
    mixed = (middle + feed.reshape(middle.shape).astype(f32)).astype(bf16)
    clock.done(g_qk.zh, grad_os)
    grad_qkv = group_exchange(beside(g_qk.sum(clock), g_value.sum(clock)))

    def columns(g):
        return g.transpose(1, 0, 2).reshape(rows_q, -1).astype(f32)

    def rows(g):
        return g.transpose(0, 2, 1).reshape(-1, rows_q).astype(f32)

    grad_up, grad_gate = columns(grad_ff[:, :, :width]), columns(grad_ff[:, :, width : 2 * width])
    grad_down = rows(grad_ff[:, :, 2 * width :])
    grad_query = columns(grad_qkv[:, :, :key_size])
    grad_key, grad_value = columns(grad_qkv[:, :, key_size:width]), columns(grad_qkv[:, :, width:])
    grad_out, grad_swish = rows(grad_os[:, :, :width]), columns(grad_os[:, :, width:])

    _, norm_one_pull = jax.vjp(layer_norm, rows_local, norm1_gain)
    grad_tok_norm, grad_norm1_local = norm_one_pull(back_one_local)
    grad_tokens = grad_middle + grad_tok_norm
    grad_norm1, grad_norm2 = sum_everywhere(jnp.stack([grad_norm1_local, grad_norm2_local]))
    return (
        mixed,
        grad_tokens,
        grad_norm1,
        grad_query,
        grad_key,
        grad_value,
        grad_swish,
        grad_out,
        grad_norm2,
        grad_up,
        grad_gate,
        grad_down,
    )


def solution(mesh):
    dp, tensor = mesh.shape["dp"], mesh.shape["tensor"]
    grid = Mesh(mesh.devices.reshape(dp // 8, 2, 2, 2, tensor), SPREAD + ("tensor",))
    rows = P(SPREAD + ("tensor",), None)
    rows_split = P(SPREAD, "tensor")
    columns_split = P("tensor", SPREAD)
    return jax.shard_map(
        local,
        mesh=grid,
        in_specs=(
            rows,
            P(SPREAD),
            P("tensor"),
            P(),
            rows_split,
            rows_split,
            rows_split,
            rows_split,
            columns_split,
            P(),
            rows_split,
            rows_split,
            columns_split,
            rows,
        ),
        out_specs=(
            rows,
            rows,
            P(),
            rows_split,
            rows_split,
            rows_split,
            rows_split,
            columns_split,
            P(),
            rows_split,
            rows_split,
            columns_split,
        ),
        check_vma=False,
    )
```

```python
import functools
import jax
import jax.numpy as jnp
from jax import lax
from jax.experimental import pallas as pl
from jax.experimental.pallas import tpu as pltpu
from jax.sharding import Mesh, PartitionSpec as P

epsilon = 1e-05
bf16 = jnp.bfloat16
f32 = jnp.float32
SPREAD = ("zh", "zl", "y", "x")
GROUP = ("zl", "x")


def normalize(values):
    centred = values - jnp.mean(values, axis=-1, keepdims=True)
    variance = jnp.mean(centred * centred, axis=-1, keepdims=True)
    return centred * lax.rsqrt(variance + epsilon)


def layer_norm(rows, gain):
    return normalize(rows) * gain


def dot(left, right, dims):
    return lax.dot_general(left, right, (dims, ((), ())), preferred_element_type=f32)


NN = ((1,), (0,))
NT = ((1,), (1,))
TN = ((0,), (0,))


def swap(a, axis, label="move"):
    with jax.named_scope(label):
        return lax.ppermute(a, axis, [(0, 1), (1, 0)])


def after(value, *others):
    return lax.optimization_barrier((value,) + others)[0]


def ordered(own, other, axis, dim):
    first = lax.axis_index(axis) == 0
    return jnp.stack([jnp.where(first, own, other), jnp.where(first, other, own)], dim)


def by_quarter(w):
    rows, cols = w.shape
    return w.reshape(rows, 4, cols // 4).transpose(1, 0, 2)


def beside(*parts):
    return jnp.concatenate(parts, 2)


def group_exchange(parts):
    return lax.all_to_all(parts, GROUP, 0, 0, tiled=True)


def take(a, index, dim):
    return lax.dynamic_index_in_dim(a, index, dim, keepdims=False)


def add(a, b):
    return (a.astype(f32) + b.astype(f32)).astype(bf16)


def scatter_y(keep, got):
    n = got.shape[-1]
    if lax.axis_size("zh") == 2:
        return add(keep[:2], got[:2]), add(keep[2:], got[2:])
    flip = lambda g: jnp.flip(g.reshape(2, 2, 1, -1, n), 0)
    g = jnp.concatenate([flip(keep), flip(got)], 2).reshape(lax.axis_size("zh"), 2, 2, 2, -1, n)
    y = lax.axis_index("y")
    return add(take(g, y, 2), swap(take(g, 1 - y, 2), "y")), None


def send_y(send, label):
    return swap(send, "y", label) if lax.axis_size("zh") == 2 else send


def send_zh(send, label):
    return swap(send, "zh", label) if lax.axis_size("zh") == 2 else send


def scatter_zh(keep, got):
    if lax.axis_size("zh") == 2:
        g = add(keep, got)
    else:
        g = lax.psum_scatter(got, "zh", scatter_dimension=0)
    return g.reshape(4, -1, g.shape[-1])


class WeightGrad:
    def __init__(self, pair, label):
        self.send, self.keep, self.label = *pair, label

    def to_y(self, clock):
        self.y = send_y(clock.at(self.send), "y_" + self.label)

    def to_zh(self, clock):
        send, self.keep = scatter_y(self.keep, clock.at(self.y))
        self.zh = send_zh(send, "zh_g" + self.label)

    def sum(self, clock):
        return scatter_zh(self.keep, clock.at(self.zh))


class Clock:
    def __init__(self):
        self.now = ()

    def done(self, *values):
        self.now = values

    def at(self, value):
        return after(value, *self.now)

    def at_all(self, values):
        return lax.optimization_barrier(tuple(values) + self.now)[: len(values)]


class Plan:
    def __init__(self, count, rows, width, column):
        self.count, self.rows, self.width, self.column = count, rows, width, column


class Weight:
    def __init__(self, arrays, plan):
        self.arrays, self.plan = arrays, plan


class Unit:
    def __init__(self, arrays, rows):
        self.arrays, self.rows = arrays, rows

    def weight(self, column, width):
        return Weight(self.arrays, Plan(len(self.arrays), self.rows, width, column))


class WeightPipe:
    def __init__(self):
        self.last = None

    def step(self, clock, piece, label):
        piece = clock.at(piece)
        if lax.axis_size("zh") != 2:
            whole = gather_weight(piece)
            self.moved = (whole,)
            return Unit([whole], piece.shape[1])
        far, near = swap(piece, "zh", "zh_" + label), swap(piece, "y", "ny_" + label)
        self.moved = (far, near)
        self.carry(clock)
        self.last = Unit([piece, near, far], piece.shape[1])
        self.label = label
        return self.last

    def carry(self, clock):
        if self.last is not None:
            far_y = swap(clock.at(self.last.arrays[2]), "y", "fy_" + self.label)
            self.last.arrays.append(far_y)
            self.moved += (far_y,)

    def finish(self, clock):
        self.moved = ()
        self.carry(clock)
        return self.moved


def gather_weight(piece):
    return lax.all_gather(piece, ("zh", "y"), axis=0)


class Gather:
    def __init__(self, clock, a, label, halves=False):
        self.a, self.label, self.halves = clock.at(a), label, halves
        self.x = swap(self.a, "x", label + "_x")
        self.z = swap(self.a, "zl", label + "_z")
        self.c = swap(self.a, "tensor", label + "_c")
        self.first = (self.x, self.z, self.c)

    def second(self, clock):
        half, label = self.a.shape[0] // 2, self.label
        ax, az = clock.at_all((self.x, self.z))
        if self.halves:
            self.diag = (swap(az[:half], "x", label + "_dx"), swap(ax[half:], "zl", label + "_dz"))
        else:
            self.diag = (swap(az, "x", label + "_dx"),)
        self.pieces = [self.a, self.c]
        self.pieces += [ax, swap(ax, "tensor", label + "_c"), az, swap(az, "tensor", label + "_c")]
        self.held = (*self.pieces, *self.diag)

    def finish(self, clock):
        diag = clock.at_all(self.diag)
        return [*self.pieces, *diag, *(swap(d, "tensor", self.label + "_c") for d in diag)]


class Scatter:
    def __init__(self, send_rest, send_diag, keep, label, clock):
        self.label, self.keep = label, keep
        send_rest, send_diag = clock.at_all((send_rest, send_diag))
        self.diag = add(keep[3], swap(send_diag, "tensor", label + "_cd"))
        self.rest = swap(send_rest, "tensor", label + "_cr")

    def relay(self, clock):
        half = self.diag.shape[0] // 2
        diag = clock.at(self.diag)
        self.through_x = swap(diag[:half], "x", self.label + "_dx")
        self.through_z = swap(diag[half:], "zl", self.label + "_dz")
        self.second = (self.through_x, self.through_z, self.rest)

    def send(self, clock):
        through_x, through_z, rest = (v.astype(f32) for v in clock.at_all(self.second))
        half = through_x.shape[0]
        self.own, xmate, zmate = (self.keep[r].astype(f32) + rest[r] for r in range(3))
        zmate = jnp.concatenate([zmate[:half] + through_x, zmate[half:]]).astype(bf16)
        xmate = jnp.concatenate([xmate[:half], xmate[half:] + through_z]).astype(bf16)
        self.x = swap(xmate, "x", self.label + "_x")
        self.z = swap(zmate, "zl", self.label + "_z")
        self.last = (self.x, self.z)

    def finish(self, clock):
        x, z = clock.at_all(self.last)
        return self.own + x.astype(f32) + z.astype(f32)


VMEM_LIMIT = 60 * 2**20
WHOLE = tuple((i // 2, i, 0, 1) for i in range(8))
HALVES = WHOLE[:6] + tuple((3, slot, part, 2) for slot in (6, 7) for part in (0, 1))
ANY = pl.BlockSpec(memory_space=pl.ANY)
SMEM = pl.BlockSpec(memory_space=pltpu.SMEM)


class Loader:
    def __init__(self, sems):
        self.sems, self.used = sems, 0

    def copy(self, src, dst):
        self.used += 1
        return pltpu.make_async_copy(src, dst, self.sems.at[self.used - 1])

    def tokens(self, refs, held, coord):
        rows = held.shape[1]
        chips = [[], [], [], []]
        if len(refs) == 1:
            for slot in range(8):
                other = 2 * ((slot // 2) ^ coord[2]) + ((slot % 2) ^ coord[3])
                chips[slot // 2].append(self.copy(refs[0].at[other], held.at[slot]))
            return chips
        for ref, (chip, slot, part, parts) in zip(refs, HALVES if len(refs) == 10 else WHOLE):
            size = rows // parts
            chips[chip].append(self.copy(ref, held.at[slot, pl.ds(part * size, size)]))
        return chips

    def weight(self, refs, plan, held, coord):
        copies = []
        columns = pl.ds(plan.column, plan.width)
        if len(refs) == 4:
            for i, ref in enumerate(refs):
                zh, y = coord[0] ^ (i // 2), coord[1] ^ (i % 2)
                for zl in range(2):
                    block = ref.at[pl.ds(2 * zl, 2), :, columns]
                    row = ((zh * 2 + zl) * 2 + y) * 2
                    copies.append(self.copy(block, held.at[pl.ds(row, 2)]))
            return copies
        for i in range(refs[0].shape[0]):
            for zl in range(2):
                block = refs[0].at[i, pl.ds(2 * zl, 2), :, columns]
                row = ((i // 2 * 2 + zl) * 2 + i % 2) * 2
                copies.append(self.copy(block, held.at[pl.ds(row, 2)]))
        return copies


def start(*copies):
    for c in copies:
        c.start()


def wait(*copies):
    for c in copies:
        c.wait()


def at_chip(r, chips):
    for i, copies in enumerate(chips):
        pl.when(r == i)(functools.partial(wait, *copies))


def rows_of(held, r):
    pair = held[pl.ds(2 * r, 2)]
    return pair.reshape(2 * pair.shape[1], pair.shape[2])


def flat(w):
    value = w[...]
    return value.reshape(value.shape[0] * value.shape[1], value.shape[2])


def by_chip(shape):
    return pl.BlockSpec((1,) + shape, lambda r: (r,) + (0,) * len(shape))


def chip_kernel(body, operands, specs, outs, out_specs, scratch, copies, flops):
    moved = sum(a.size * a.dtype.itemsize for a in operands) + sum(
        o.size * jnp.dtype(o.dtype).itemsize for o in outs
    )
    return pl.pallas_call(
        body,
        grid=(4,),
        in_specs=specs,
        out_specs=out_specs,
        out_shape=outs,
        scratch_shapes=scratch + [pltpu.SemaphoreType.DMA((copies,))],
        compiler_params=pltpu.CompilerParams(
            dimension_semantics=("arbitrary",), vmem_limit_bytes=VMEM_LIMIT
        ),
        cost_estimate=pl.CostEstimate(flops=flops, bytes_accessed=moved, transcendentals=0),
    )(*operands)


def held_tokens(pieces):
    return pltpu.VMEM((8,) + pieces[0].shape[-2:], bf16)


def held_weight(w):
    devices = 16 if w.plan.count == 4 else 4 * w.arrays[0].shape[0]
    return pltpu.VMEM((devices, w.plan.rows, w.plan.width), bf16)


def arrays(*weights):
    return [a for w in weights for a in w.arrays]


def copies_of(*weights):
    return sum(8 if w.plan.count == 4 else 2 * w.arrays[0].shape[0] for w in weights)


def struct(shape, dtype):
    return jax.ShapeDtypeStruct(shape, dtype)


def partial_rows(grads, helds, r, keep, store):
    rows, blocks = keep.shape[1], helds[0].shape[0] // 4
    size = blocks * helds[0].shape[1]
    for j in range(4):
        parts = [
            dot(g, h[j * blocks : (j + 1) * blocks].reshape(size, h.shape[2]), NT)
            for g, h in zip(grads, helds)
        ]
        out = sum(parts[1:], parts[0]).astype(bf16)
        keep[0, :, j * size : (j + 1) * size] = out[:rows]
        store[r, :, j * size : (j + 1) * size] = out[rows:]


def send_copies(load, store, rest, diag):
    return [load.copy(store.at[i], rest.at[i]) for i in range(3)] + [load.copy(store.at[3], diag)]


def at_chip_start(r, copies):
    for i, c in enumerate(copies):
        pl.when(r == i)(c.start)

    @pl.when(r == 3)
    def _():
        wait(*copies)


def partial_outs(rows, model):
    outs = [
        struct((3, rows, model), bf16),
        struct((rows, model), bf16),
        struct((4, rows, model), bf16),
    ]
    return outs, [ANY, ANY, by_chip((rows, model))]


def attend_body(tokens, f_qk, f_v, coord, mask, *refs):
    acts, refs = refs[:tokens], refs[tokens:]
    wqk, refs = refs[: f_qk.count], refs[f_qk.count :]
    wv, refs = refs[: f_v.count], refs[f_v.count :]
    q_out, k_out, v_out, score_out, hat_out, scale_out, held, held_qk, held_v, sems = refs
    load, r = Loader(sems), pl.program_id(0)
    w1 = load.weight(wqk, f_qk, held_qk, coord)
    chips = load.tokens(acts, held, coord)
    w2 = load.weight(wv, f_v, held_v, coord)

    @pl.when(r == 0)
    def _():
        start(*w1, *chips[0], *w2, *chips[1], *chips[2], *chips[3])
        wait(*w1)

    at_chip(r, chips)
    x = rows_of(held, r)
    qk = dot(x, flat(held_qk), NN).astype(bf16)
    size = qk.shape[1] // 2
    q, k = qk[:, :size], qk[:, size:]
    q_out[0], k_out[0] = q, k
    scores = (dot(q, k, NT) * mask[0]).astype(bf16)
    score_out[0] = scores

    @pl.when(r == 0)
    def _():
        wait(*w2)

    v = dot(x, flat(held_v), NN).astype(bf16)
    v_out[0] = v
    hat_out[0] = dot(scores, v, NN)
    rows, step = hat_out.shape[1], 32

    def chunk(i, carry):
        at = pl.ds(pl.multiple_of(i * step, step), step)
        part = hat_out[0, at, :]
        part = part - jnp.mean(part, axis=-1, keepdims=True)
        scale = lax.rsqrt(jnp.mean(part * part, axis=-1, keepdims=True) + epsilon)
        hat_out[0, at, :] = part * scale
        scale_out[0, at, :] = jnp.broadcast_to(scale, (step, 128))
        return carry

    lax.fori_loop(0, rows // step, chunk, 0, unroll=4)


def attend(coord, mask, acts, wqk, wv, key_size):
    length, n = mask.shape[1], wv.plan.width
    model = acts[0].shape[-1]
    outs = [
        struct((4, length, key_size), bf16),
        struct((4, length, key_size), bf16),
        struct((4, length, n), bf16),
        struct((4, length, length), bf16),
        struct((4, length, n), f32),
        struct((4, length, 128), f32),
    ]
    return chip_kernel(
        functools.partial(attend_body, len(acts), wqk.plan, wv.plan),
        [coord, mask, *acts, *arrays(wqk, wv)],
        [SMEM, by_chip((length, length))] + [ANY] * (len(acts) + len(arrays(wqk, wv))),
        outs,
        [by_chip(o.shape[1:]) for o in outs],
        [held_tokens(acts), held_weight(wqk), held_weight(wv)],
        10 + copies_of(wqk, wv),
        16 * length * model * n,
    )


def branch_body(tokens, f_s, f_o, coord, hat, *refs):
    acts, refs = refs[:tokens], refs[tokens:]
    ws, refs = refs[: f_s.count], refs[f_s.count :]
    wo, refs = refs[: f_o.count], refs[f_o.count :]
    s_out, gated_out, rest, diag, keep, held, held_s, held_o, store, sems = refs
    load, r = Loader(sems), pl.program_id(0)
    w1 = load.weight(ws, f_s, held_s, coord)
    chips = load.tokens(acts, held, coord)
    w2 = load.weight(wo, f_o, held_o, coord)
    sends = send_copies(load, store, rest, diag)

    @pl.when(r == 0)
    def _():
        start(*w1, *chips[0], *w2, *chips[1], *chips[2], *chips[3])
        wait(*w1)

    at_chip(r, chips)
    s_out[0] = dot(rows_of(held, r), flat(held_s), NN)
    rows, step = s_out.shape[1], 32

    def chunk(i, carry):
        at = pl.ds(pl.multiple_of(i * step, step), step)
        s = s_out[0, at, :]
        gated_out[0, at, :] = (s / (1.0 + jnp.exp(-s)) * hat[0, at, :]).astype(bf16)
        return carry

    lax.fori_loop(0, rows // step, chunk, 0, unroll=4)

    @pl.when(r == 0)
    def _():
        wait(*w2)

    partial_rows([gated_out[0]], [held_o], r, keep, store)
    at_chip_start(r, sends)


def branch(coord, hat, acts, ws, wo):
    length, n = hat.shape[1:]
    rows, model = acts[0].shape[-2:]
    outs, out_specs = partial_outs(rows, model)
    outs = [struct((4, length, n), f32), struct((4, length, n), bf16)] + outs
    return chip_kernel(
        functools.partial(branch_body, len(acts), ws.plan, wo.plan),
        [coord, hat, *acts, *arrays(ws, wo)],
        [SMEM, by_chip((length, n))] + [ANY] * (len(acts) + len(arrays(ws, wo))),
        outs,
        [by_chip((length, n)), by_chip((length, n))] + out_specs,
        [held_tokens(acts), held_weight(ws), held_weight(wo), pltpu.VMEM((4, rows, model), bf16)],
        14 + copies_of(ws, wo),
        16 * length * model * n,
    )


def feed_body(tokens, others, f_u, f_g, f_d, coord, *refs):
    acts, cots, refs = refs[:tokens], refs[tokens : tokens + others], refs[tokens + others :]
    wu, refs = refs[: f_u.count], refs[f_u.count :]
    wg, refs = refs[: f_g.count], refs[f_g.count :]
    wd, refs = refs[: f_d.count], refs[f_d.count :]
    hidden_out, up_out, gate_out, rest, diag, keep = refs[:6]
    held, held_c, held_u, held_g, held_d, store, up, gate, gh, sems = refs[6:]
    load, r = Loader(sems), pl.program_id(0)
    w1 = load.weight(wu, f_u, held_u, coord)
    w2 = load.weight(wg, f_g, held_g, coord)
    w3 = load.weight(wd, f_d, held_d, coord)
    chips = load.tokens(acts, held, coord)
    chips_c = load.tokens(cots, held_c, coord)
    sends = send_copies(load, store, rest, diag)

    @pl.when(r == 0)
    def _():
        start(*w3, *chips_c[0], *w1, *chips[0], *w2)
        for i in range(1, 4):
            start(*chips_c[i], *chips[i])
        wait(*w3)

    at_chip(r, chips_c)
    gh[...] = dot(rows_of(held_c, r), flat(held_d), NN)

    @pl.when(r == 0)
    def _():
        wait(*w1)

    at_chip(r, chips)
    x = rows_of(held, r)
    up[...] = dot(x, flat(held_u), NN)

    @pl.when(r == 0)
    def _():
        wait(*w2)

    gate[...] = dot(x, flat(held_g), NN)
    step = 16

    def chunk(i, carry):
        at = pl.ds(pl.multiple_of(i * step, step), step)
        u, g, e = up[at, :], gate[at, :], gh[at, :]
        c = 0.7978845608028654
        square = g * g
        t = jnp.tanh(c * g * (1.0 + 0.044715 * square))
        half = 0.5 * (1.0 + t)
        gelu = g * half
        slope = half + (0.5 * c) * g * (1.0 - t * t) * (1.0 + (3 * 0.044715) * square)
        hidden_out[0, at, :] = (gelu * u).astype(bf16)
        up_out[0, at, :] = (e * gelu).astype(bf16)
        gate_out[0, at, :] = (e * u * slope).astype(bf16)
        return carry

    lax.fori_loop(0, gh.shape[0] // step, chunk, 0, unroll=4)
    partial_rows([up_out[0], gate_out[0]], [held_u, held_g], r, keep, store)
    at_chip_start(r, sends)


def feed_forward(coord, acts, cots, wu, wg, wd):
    rows, model = acts[0].shape[-2:]
    n = wd.plan.width
    outs, out_specs = partial_outs(rows, model)
    outs = [struct((4, 2 * rows, n), bf16)] * 3 + outs
    return chip_kernel(
        functools.partial(feed_body, len(acts), len(cots), wu.plan, wg.plan, wd.plan),
        [coord, *acts, *cots, *arrays(wu, wg, wd)],
        [SMEM] + [ANY] * (len(acts) + len(cots) + len(arrays(wu, wg, wd))),
        outs,
        [by_chip((2 * rows, n))] * 3 + out_specs,
        [
            held_tokens(acts),
            held_tokens(cots),
            held_weight(wu),
            held_weight(wg),
            held_weight(wd),
            pltpu.VMEM((4, rows, model), bf16),
        ]
        + [pltpu.VMEM((2 * rows, n), f32)] * 3,
        24 + copies_of(wu, wg, wd),
        80 * rows * model * n,
    )


def back_body(plans, whole, coord, *refs):
    count = len(plans)
    weights = []
    grads, refs = refs[:count], refs[count:]
    for plan in plans:
        weights.append(refs[: plan.count])
        refs = refs[plan.count :]
    load, r = Loader(refs[-1]), pl.program_id(0)
    if whole:
        result, helds, keep, store = refs[0], refs[1 : 1 + count], refs[-3], refs[-2]
    else:
        rest, diag, keep, helds, store = *refs[:3], refs[3 : 3 + count], refs[-2]
    copies = [load.weight(w, p, h, coord) for w, p, h in zip(weights, plans, helds)]

    @pl.when(r == 0)
    def _():
        for c in copies:
            start(*c)
        for c in copies:
            wait(*c)

    if not whole:
        sends = send_copies(load, store, rest, diag)
        partial_rows([g[0] for g in grads], helds, r, keep, store)
        at_chip_start(r, sends)
        return
    sends = []
    for i in range(4):
        at = 2 * (i ^ coord[2])
        sends.append(
            (
                load.copy(keep.at[i], result.at[at + coord[3]]),
                load.copy(store.at[i], result.at[at + (1 ^ coord[3])]),
            )
        )
    partial_rows([g[0] for g in grads], helds, r, keep.at[pl.ds(r, 1)], store)
    for i in range(4):
        pl.when(r == i)(functools.partial(start, *sends[i]))

    @pl.when(r == 3)
    def _():
        for c in sends:
            wait(*c)


def back(coord, grads, weights, whole=False):
    length = grads[0].shape[1]
    rows = length // 2
    held = held_weight(weights[0])
    model = held.shape[0] * held.shape[1]
    outs, out_specs = partial_outs(rows, model)
    store = pltpu.VMEM((4, rows, model), bf16)
    if whole:
        outs, out_specs = [struct((8, rows, model), bf16)], [ANY]
    return chip_kernel(
        functools.partial(back_body, tuple(w.plan for w in weights), whole),
        [coord, *grads, *arrays(*weights)],
        [SMEM] + [by_chip(g.shape[1:]) for g in grads] + [ANY] * len(arrays(*weights)),
        outs,
        out_specs,
        [held_weight(w) for w in weights] + [store] * (2 if whole else 1),
        8 + copies_of(*weights),
        8 * length * model * sum(g.shape[2] for g in grads),
    )


def attend_back_body(tokens, f_o, coord, mask, s, hat, scale, scores, q, k, v, *refs):
    acts, refs = refs[:tokens], refs[tokens:]
    wo, refs = refs[: f_o.count], refs[f_o.count :]
    gqk_out, gv_out, gs_out, held, held_o, dg, gr, sems = refs
    load, r = Loader(sems), pl.program_id(0)
    w1 = load.weight(wo, f_o, held_o, coord)
    chips = load.tokens(acts, held, coord)

    @pl.when(r == 0)
    def _():
        start(*w1, *chips[0], *chips[1], *chips[2], *chips[3])
        wait(*w1)

    at_chip(r, chips)
    dg[...] = dot(rows_of(held, r), flat(held_o), NN)
    rows, step = dg.shape[0], 16

    def chunk(i, carry):
        at = pl.ds(pl.multiple_of(i * step, step), step)
        e, x, v_s = dg[at, :], hat[0, at, :], s[0, at, :]
        gate = 1.0 / (1.0 + jnp.exp(-v_s))
        silu = v_s * gate
        gs_out[0, at, :] = (e * x * (gate + silu * (1.0 - gate))).astype(bf16)
        f = e * silu
        f = f - jnp.mean(f, axis=-1, keepdims=True) - x * jnp.mean(f * x, axis=-1, keepdims=True)
        gr[at, :] = (f * scale[0, at, :1]).astype(bf16)
        return carry

    lax.fori_loop(0, rows // step, chunk, 0, unroll=4)
    grad_retained = gr[...]
    gv_out[0] = dot(scores[0], grad_retained, TN).astype(bf16)
    raw = (dot(grad_retained, v[0], NT) * mask[0]).astype(bf16)
    size = q.shape[2]
    gqk_out[0, :, :size] = dot(raw, k[0], NN).astype(bf16)
    gqk_out[0, :, size:] = dot(raw, q[0], TN).astype(bf16)


def attend_back(coord, mask, s, hat, scale, scores, q, k, v, acts, wo):
    length, n = s.shape[1:]
    model = acts[0].shape[-1]
    blocks = [mask, s, hat, scale, scores, q, k, v]
    outs = [struct((4, length, 2 * q.shape[2]), bf16)] + [struct((4, length, n), bf16)] * 2
    return chip_kernel(
        functools.partial(attend_back_body, len(acts), wo.plan),
        [coord, *blocks, *acts, *arrays(wo)],
        [SMEM] + [by_chip(b.shape[1:]) for b in blocks] + [ANY] * (len(acts) + len(arrays(wo))),
        outs,
        [by_chip(o.shape[1:]) for o in outs],
        [
            held_tokens(acts),
            held_weight(wo),
            pltpu.VMEM((length, n), f32),
            pltpu.VMEM((length, n), bf16),
        ],
        10 + copies_of(wo),
        12 * length * model * n,
    )


def weight_grad_body(count, tokens, whole, coord, *refs):
    grads, refs = refs[:count], refs[count:]
    acts, refs = refs[:tokens], refs[tokens:]
    outs, held, sems = refs[:-2], refs[-2], refs[-1]
    load, i = Loader(sems), pl.program_id(0)
    chips = load.tokens(acts, held, coord)

    @pl.when(i == 0)
    def _():
        for c in chips:
            start(*c)
        for c in chips:
            wait(*c)

    width = held.shape[2] // 8
    j = i % 4
    if whole:
        column = ((i // 4 * 2 + i % 2) * 2 + i // 2 % 2) * width
    else:
        y = coord[1] ^ jnp.where(i < 4, 1, 0)
        zh = coord[0] ^ jnp.where(j < 2, 1, 0)
        column = ((zh * 2 + j % 2) * 2 + y) * width
    x = held[:, :, pl.ds(pl.multiple_of(column, width), width)]
    x = x.reshape(x.shape[0] * x.shape[1], width).T
    for n in range(count):
        g = grads[n][...]
        size = g.shape[2]
        out = dot(x, g.reshape(g.shape[0] * g.shape[1], size), NN).astype(bf16)
        if whole:
            outs[0][0, :, n * size : (n + 1) * size] = out
            continue
        pl.when(i < 4)(functools.partial(store_block, outs[2 * n], out))
        pl.when(i >= 4)(functools.partial(store_block, outs[2 * n + 1], out))


def store_block(ref, value):
    ref[0] = value


def weight_grads(coord, acts, grads, whole=False):
    rows, model = acts[0].shape[-2:]
    outs, out_specs = [], []
    width = sum(g.shape[2] for g in grads)
    for g in grads:
        shape = (4, model // 8, g.shape[2])
        outs += [struct(shape, bf16)] * 2
        out_specs += [
            pl.BlockSpec((1,) + shape[1:], lambda i: (jnp.minimum(i, 3), 0, 0)),
            pl.BlockSpec((1,) + shape[1:], lambda i: (jnp.maximum(i - 4, 0), 0, 0)),
        ]
    if whole:
        outs = [struct((8, model // 8, width), bf16)]
        out_specs = [pl.BlockSpec((1, model // 8, width), lambda i: (i, 0, 0))]
    moved = sum(a.size * 2 for a in acts) + sum(g.size * 2 for g in grads) + 2 * model * width
    got = pl.pallas_call(
        functools.partial(weight_grad_body, len(grads), len(acts), whole),
        grid=(8,),
        in_specs=[SMEM] + [pl.BlockSpec(memory_space=pltpu.VMEM)] * len(grads) + [ANY] * len(acts),
        out_specs=out_specs,
        out_shape=outs,
        scratch_shapes=[held_tokens(acts), pltpu.SemaphoreType.DMA((10,))],
        compiler_params=pltpu.CompilerParams(
            dimension_semantics=("arbitrary",), vmem_limit_bytes=VMEM_LIMIT
        ),
        cost_estimate=pl.CostEstimate(
            flops=16 * rows * model * width, bytes_accessed=moved, transcendentals=0
        ),
    )(coord, *grads, *acts)
    if whole:
        return got[0]
    return [(got[2 * i], got[2 * i + 1]) for i in range(len(grads))]


def place_body(parts, g, *outs):
    column = 0
    for (width, way), out in zip(parts, outs):
        value = g[0, :, column : column + width].astype(f32)
        out[...] = value.T if way == "r" else value
        column += width


def place(g, parts):
    rows = g.shape[1]
    outs, specs = [], []
    for width, way in parts:
        if way == "r":
            outs.append(struct((4 * width, rows), f32))
            specs.append(pl.BlockSpec((width, rows), lambda q: (q, 0)))
        else:
            outs.append(struct((rows, 4 * width), f32))
            specs.append(pl.BlockSpec((rows, width), lambda q: (0, q)))
    return pl.pallas_call(
        functools.partial(place_body, parts),
        grid=(4,),
        in_specs=[by_chip(g.shape[1:])],
        out_specs=specs,
        out_shape=outs,
        compiler_params=pltpu.CompilerParams(dimension_semantics=("arbitrary",)),
        cost_estimate=pl.CostEstimate(flops=0, bytes_accessed=6 * g.size, transcendentals=0),
    )(g)


def scatter_whole(g):
    zh, n = lax.axis_size("zh"), g.shape[2]
    if zh == 2:
        g = g.reshape(4, 4, -1, n)
    else:
        g = g.reshape(2, 2, 2, -1, n).transpose(0, 2, 1, 3, 4).reshape(zh, 2, 2, 2, -1, n)
        g = g.transpose(0, 2, 1, 3, 4, 5).reshape(2 * zh, 4, -1, n)
    g = lax.psum_scatter(g, ("zh", "y"), scatter_dimension=0, tiled=True)
    return g.reshape(4, -1, n)


def sum_everywhere(a):
    for axis in ("tensor",) + SPREAD:
        if lax.axis_size(axis) == 2:
            a = a + swap(a, axis)
        else:
            a = lax.psum(a, axis)
    return a


def local(
    tokens,
    segments,
    decay,
    norm1_gain,
    w_query,
    w_key,
    w_value,
    w_swish,
    w_out,
    norm2_gain,
    w_up,
    w_gate,
    w_down,
    cotangent,
):
    rows_q, width = w_query.shape[0], w_value.shape[1] // 4
    quarter = 2 * lax.axis_index("zl") + lax.axis_index("x")
    core = lax.axis_index("tensor")
    length = segments.shape[0]
    rows_each = tokens.shape[0]
    key_size = w_query.shape[1] // 4
    value_size = w_value.shape[1] // 4
    rate = take(decay, quarter, 0)

    ids = [jnp.zeros((), jnp.int32)] * 2
    if lax.axis_size("zh") == 2:
        ids = [lax.axis_index("zh"), lax.axis_index("y")]
    coord = jnp.stack(ids + [quarter, core]).astype(jnp.int32)
    clock, free = Clock(), Clock()
    at = clock.at
    rows_local = tokens.astype(f32)
    everyone = ("zl", "x", "tensor")

    pipe = WeightPipe()
    seg_x, seg_z = swap(segments, "x", "seg"), swap(segments, "zl", "seg")
    with jax.named_scope("seg"):
        seg_d = lax.ppermute(segments, GROUP, [(i, 3 - i) for i in range(4)])
    parts = (by_quarter(w) for w in (w_query, w_key, w_value))
    piece = group_exchange(beside(*parts))
    grad_rows = [lax.all_gather(cotangent, everyone, axis=0)]
    parts = beside(by_quarter(w_swish), by_quarter(w_out.T))

    clock.done(piece, parts)
    unit_qkv = pipe.step(clock, piece, "qkv")
    piece = group_exchange(at(parts))
    normed_local = layer_norm(rows_local, norm1_gain).astype(bf16)
    normed = [lax.all_gather(at(normed_local), everyone, axis=0)]
    segs = jnp.stack([segments, seg_x, seg_z, seg_d])
    segs = jnp.where(core == 0, segs, jnp.roll(segs, length // 2, 1))
    position = (jnp.arange(length, dtype=jnp.int32) + core * rows_each) % length
    offset = position[:, None] - position[None, :]
    allowed = (offset >= 0)[None] & (segs[:, :, None] == segs[:, None, :])
    distance = jnp.maximum(offset, 0).astype(f32)
    decay_mask = jnp.where(allowed, jnp.exp(-rate * distance)[None], 0.0)
    parts = beside(by_quarter(at(w_up)), by_quarter(at(w_gate)), by_quarter(at(w_down).T))

    clock.done(piece, parts, decay_mask, *pipe.moved)
    unit_so = pipe.step(clock, piece, "so")
    piece = group_exchange(at(parts))
    full_qk, full_value = unit_qkv.weight(0, width), unit_qkv.weight(width, width)
    query, key, values, scores, hat, scale = attend(
        at(coord), decay_mask, normed, full_qk, full_value, key_size
    )

    clock.done(query, piece, *pipe.moved)
    unit_ug = pipe.step(clock, piece[:, :, : 2 * width], "ug")
    full_swish, full_out = unit_so.weight(0, width), unit_so.weight(width, width)
    swish_in, gated, *partial = branch(at(coord), hat, normed, full_swish, full_out)
    clock.done(*pipe.moved, *partial)
    unit_d = pipe.step(clock, piece[:, :, 2 * width :], "d")
    scatter = Scatter(*partial, "branch", clock)
    scatter.relay(free)
    clock.done(*scatter.second)
    scatter.send(clock)
    clock.done(*scatter.last, *pipe.moved)
    middle = rows_local + scatter.finish(clock)
    normed_two_local = layer_norm(middle, norm2_gain).astype(bf16)
    gather = Gather(clock, normed_two_local, "two", True)
    far_y = pipe.finish(clock)
    clock.done(*far_y, *gather.first)
    gather.second(clock)
    clock.done(*gather.held)
    normed_two = gather.finish(clock)
    full_up, full_gate = unit_ug.weight(0, width), unit_ug.weight(width, width)
    full_down = unit_d.weight(0, width)
    hidden, grad_up_rows, grad_gate_rows, *partial = feed_forward(
        at(coord), normed_two, grad_rows, full_up, full_gate, full_down
    )

    scatter = Scatter(*partial, "back_two", free)
    clock.done(scatter.diag)
    scatter.relay(clock)
    (g_down,) = weight_grads(at(coord), grad_rows, [hidden])
    g_down = WeightGrad(g_down, "down")
    clock.done(g_down.send, *scatter.second)
    scatter.send(clock)
    g_down.to_y(clock)
    g_up, g_gate = weight_grads(at(coord), normed_two, [grad_up_rows, grad_gate_rows])
    g_up, g_gate = WeightGrad(g_up, "up"), WeightGrad(g_gate, "gate")
    clock.done(g_up.send, g_down.y, *scatter.last)
    back_two_local = scatter.finish(clock)
    _, norm_two_pull = jax.vjp(layer_norm, middle, norm2_gain)
    grad_mid_norm, grad_norm2_local = norm_two_pull(back_two_local)
    grad_middle = cotangent.astype(f32) + grad_mid_norm
    grad_branch_local = grad_middle.astype(bf16)

    clock.done(grad_branch_local)
    gather = Gather(clock, grad_branch_local, "gb", True)
    g_down.to_zh(clock)
    g_up.to_y(clock)
    clock.done(g_down.zh, g_up.y, *gather.first)
    gather.second(clock)
    g_gate.to_y(clock)
    (feed,) = back(at(coord), [hidden], [full_down], True)
    clock.done(feed, *gather.held)
    grad_branch = gather.finish(clock)
    feed = lax.psum_scatter(at(feed), everyone, scatter_dimension=0, tiled=True)
    g_up.to_zh(clock)
    grad_qk, grad_values, grad_swish_in = attend_back(
        at(coord),
        decay_mask,
        swish_in,
        hat,
        scale,
        scores,
        query,
        key,
        values,
        grad_branch,
        full_out,
    )
    clock.done(grad_qk, g_up.zh, g_gate.y)
    g_gate.to_zh(clock)
    (g_out,) = weight_grads(at(coord), grad_branch, [gated])
    g_out = WeightGrad(g_out, "out")
    clock.done(g_out.send)
    g_out.to_y(clock)
    (g_swish,) = weight_grads(at(coord), normed, [grad_swish_in])
    g_swish = WeightGrad(g_swish, "swish")
    clock.done(g_swish.send, g_gate.zh)
    g_value, g_qk = weight_grads(at(coord), normed, [grad_values, grad_qk])
    g_value, g_qk = WeightGrad(g_value, "value"), WeightGrad(g_qk, "qk")
    clock.done(g_value.send, g_out.y)
    g_out.to_zh(clock)
    g_swish.to_y(clock)
    partial = back(
        at(coord), [grad_qk, grad_values, grad_swish_in], [full_qk, full_value, full_swish]
    )
    clock.done(g_out.zh, g_swish.y, *partial)
    g_swish.to_zh(clock)
    g_value.to_y(clock)
    scatter = Scatter(*partial, "back_one", clock)
    clock.done(scatter.diag)
    scatter.relay(clock)
    clock.done(*scatter.second)
    scatter.send(clock)
    clock.done(g_swish.zh, g_value.y)
    g_value.to_zh(clock)
    g_qk.to_y(clock)
    grad_ff = group_exchange(beside(g_up.sum(clock), g_gate.sum(clock), g_down.sum(clock)))
    clock.done(g_value.zh, g_qk.y)
    g_qk.to_zh(clock)
    clock.done(*scatter.last)
    back_one_local = scatter.finish(clock)
    grad_os = group_exchange(after(beside(g_out.sum(clock), g_swish.sum(clock)), grad_ff))
    grad_up, grad_gate, grad_down = place(at(grad_ff), ((width, "c"), (width, "c"), (width, "r")))
    mixed = (middle + feed.reshape(middle.shape).astype(f32)).astype(bf16)
    _, norm_one_pull = jax.vjp(layer_norm, rows_local, norm1_gain)
    grad_tok_norm, grad_norm1_local = norm_one_pull(back_one_local)
    grad_tokens = grad_middle + grad_tok_norm
    grad_norm1, grad_norm2 = sum_everywhere(
        after(jnp.stack([grad_norm1_local, grad_norm2_local]), g_qk.zh)
    )
    clock.done(g_qk.zh, grad_os, grad_up, mixed, grad_norm1, grad_tokens)
    grad_qkv = group_exchange(beside(g_qk.sum(clock), g_value.sum(clock)))
    grad_out, grad_swish = place(at(grad_os), ((width, "r"), (width, "c")))
    parts = ((key_size, "c"), (key_size, "c"), (width, "c"))
    grad_query, grad_key, grad_value = place(grad_qkv, parts)

    return (
        mixed,
        grad_tokens,
        grad_norm1,
        grad_query,
        grad_key,
        grad_value,
        grad_swish,
        grad_out,
        grad_norm2,
        grad_up,
        grad_gate,
        grad_down,
    )


def solution(mesh):
    dp, tensor = mesh.shape["dp"], mesh.shape["tensor"]
    grid = Mesh(mesh.devices.reshape(dp // 8, 2, 2, 2, tensor), SPREAD + ("tensor",))
    rows = P(SPREAD + ("tensor",), None)
    rows_split = P(SPREAD, "tensor")
    columns_split = P("tensor", SPREAD)
    return jax.shard_map(
        local,
        mesh=grid,
        in_specs=(
            rows,
            P(SPREAD),
            P("tensor"),
            P(),
            rows_split,
            rows_split,
            rows_split,
            rows_split,
            columns_split,
            P(),
            rows_split,
            rows_split,
            columns_split,
            rows,
        ),
        out_specs=(
            rows,
            rows,
            P(),
            rows_split,
            rows_split,
            rows_split,
            rows_split,
            columns_split,
            P(),
            rows_split,
            rows_split,
            columns_split,
        ),
        check_vma=False,
    )
```

```python
import functools
import jax
import jax.numpy as jnp
from jax import lax
from jax.experimental import pallas as pl
from jax.experimental.pallas import tpu as pltpu
from jax.sharding import Mesh, PartitionSpec as P

epsilon = 1e-05
bf16 = jnp.bfloat16
f32 = jnp.float32
SPREAD = ("zh", "zl", "y", "x")
GROUP = ("zl", "x")


def normalize(values):
    centred = values - jnp.mean(values, axis=-1, keepdims=True)
    variance = jnp.mean(centred * centred, axis=-1, keepdims=True)
    return centred * lax.rsqrt(variance + epsilon)


def layer_norm(rows, gain):
    return normalize(rows) * gain


def dot(left, right, dims):
    return lax.dot_general(left, right, (dims, ((), ())), preferred_element_type=f32)


NN = ((1,), (0,))
NT = ((1,), (1,))
TN = ((0,), (0,))


def swap(a, axis, label="move"):
    with jax.named_scope(label):
        return lax.ppermute(a, axis, [(0, 1), (1, 0)])


def after(value, *others):
    return lax.optimization_barrier((value,) + others)[0]


def ordered(own, other, axis, dim):
    first = lax.axis_index(axis) == 0
    return jnp.stack([jnp.where(first, own, other), jnp.where(first, other, own)], dim)


def by_quarter(w):
    rows, cols = w.shape
    return w.reshape(rows, 4, cols // 4).transpose(1, 0, 2)


def beside(*parts):
    return jnp.concatenate(parts, 2)


def group_exchange(parts):
    return lax.all_to_all(parts, GROUP, 0, 0, tiled=True)


def take(a, index, dim):
    return lax.dynamic_index_in_dim(a, index, dim, keepdims=False)


def add(a, b):
    return (a.astype(f32) + b.astype(f32)).astype(bf16)


def scatter_y(keep, got):
    n = got.shape[-1]
    if lax.axis_size("zh") == 2:
        return add(keep[:2], got[:2]), add(keep[2:], got[2:])
    flip = lambda g: jnp.flip(g.reshape(2, 2, 1, -1, n), 0)
    g = jnp.concatenate([flip(keep), flip(got)], 2).reshape(lax.axis_size("zh"), 2, 2, 2, -1, n)
    y = lax.axis_index("y")
    return add(take(g, y, 2), swap(take(g, 1 - y, 2), "y")), None


def send_y(send, label):
    return swap(send, "y", label) if lax.axis_size("zh") == 2 else send


def send_zh(send, label):
    return swap(send, "zh", label) if lax.axis_size("zh") == 2 else send


def scatter_zh(keep, got):
    if lax.axis_size("zh") == 2:
        g = add(keep, got)
    else:
        g = lax.psum_scatter(got, "zh", scatter_dimension=0)
    return g.reshape(4, -1, g.shape[-1])


class WeightGrad:
    def __init__(self, pair, label):
        self.send, self.keep, self.label = *pair, label

    def to_y(self, clock):
        self.y = send_y(clock.at(self.send), "y_" + self.label)

    def to_zh(self, clock):
        send, self.keep = scatter_y(self.keep, clock.at(self.y))
        self.zh = send_zh(send, "zh_g" + self.label)

    def sum(self, clock):
        return scatter_zh(self.keep, clock.at(self.zh))


class Clock:
    def __init__(self):
        self.now = ()

    def done(self, *values):
        self.now = values

    def at(self, value):
        return after(value, *self.now)

    def at_all(self, values):
        return lax.optimization_barrier(tuple(values) + self.now)[: len(values)]


class Plan:
    def __init__(self, count, rows, width, column):
        self.count, self.rows, self.width, self.column = count, rows, width, column


class Weight:
    def __init__(self, arrays, plan):
        self.arrays, self.plan = arrays, plan


class Unit:
    def __init__(self, arrays, rows):
        self.arrays, self.rows = arrays, rows

    def weight(self, column, width):
        return Weight(self.arrays, Plan(len(self.arrays), self.rows, width, column))


class WeightPipe:
    def __init__(self):
        self.last = None

    def step(self, clock, piece, label):
        piece = clock.at(piece)
        if lax.axis_size("zh") != 2:
            whole = gather_weight(piece)
            self.moved = (whole,)
            return Unit([whole], piece.shape[1])
        far, near = swap(piece, "zh", "zh_" + label), swap(piece, "y", "ny_" + label)
        self.moved = (far, near)
        self.carry(clock)
        self.last = Unit([piece, near, far], piece.shape[1])
        self.label = label
        return self.last

    def carry(self, clock):
        if self.last is not None:
            far_y = swap(clock.at(self.last.arrays[2]), "y", "fy_" + self.label)
            self.last.arrays.append(far_y)
            self.moved += (far_y,)

    def finish(self, clock):
        self.moved = ()
        self.carry(clock)
        return self.moved


def gather_weight(piece):
    return lax.all_gather(piece, ("zh", "y"), axis=0)


class Gather:
    def __init__(self, clock, a, label, halves=False):
        self.a, self.label, self.halves = clock.at(a), label, halves
        self.x = swap(self.a, "x", label + "_x")
        self.z = swap(self.a, "zl", label + "_z")
        self.c = swap(self.a, "tensor", label + "_c")
        self.first = (self.x, self.z, self.c)

    def second(self, clock):
        half, label = self.a.shape[0] // 2, self.label
        ax, az = clock.at_all((self.x, self.z))
        if self.halves:
            self.diag = (swap(az[:half], "x", label + "_dx"), swap(ax[half:], "zl", label + "_dz"))
        else:
            self.diag = (swap(az, "x", label + "_dx"),)
        self.pieces = [self.a, self.c]
        self.pieces += [ax, swap(ax, "tensor", label + "_c"), az, swap(az, "tensor", label + "_c")]
        self.held = (*self.pieces, *self.diag)

    def finish(self, clock):
        diag = clock.at_all(self.diag)
        return [*self.pieces, *diag, *(swap(d, "tensor", self.label + "_c") for d in diag)]


class Scatter:
    def __init__(self, send_rest, send_diag, keep, label, clock):
        self.label, self.keep = label, keep
        send_rest, send_diag = clock.at_all((send_rest, send_diag))
        self.diag = add(keep[3], swap(send_diag, "tensor", label + "_cd"))
        self.rest = swap(send_rest, "tensor", label + "_cr")

    def relay(self, clock, whole=False):
        half = self.diag.shape[0] // 2
        diag = clock.at(self.diag)
        self.whole = whole
        if whole:
            self.through_x = swap(diag, "x", self.label + "_dx")
            self.second = (self.through_x, self.rest)
            return
        self.through_x = swap(diag[:half], "x", self.label + "_dx")
        self.through_z = swap(diag[half:], "zl", self.label + "_dz")
        self.second = (self.through_x, self.through_z, self.rest)

    def send(self, clock):
        *through, rest = (v.astype(f32) for v in clock.at_all(self.second))
        self.own, xmate, zmate = (self.keep[r].astype(f32) + rest[r] for r in range(3))
        if self.whole:
            self.x = swap(xmate.astype(bf16), "x", self.label + "_x")
            self.z = swap((zmate + through[0]).astype(bf16), "zl", self.label + "_z")
            self.last = (self.x, self.z)
            return
        through_x, through_z = through
        half = through_x.shape[0]
        zmate = jnp.concatenate([zmate[:half] + through_x, zmate[half:]]).astype(bf16)
        xmate = jnp.concatenate([xmate[:half], xmate[half:] + through_z]).astype(bf16)
        self.x = swap(xmate, "x", self.label + "_x")
        self.z = swap(zmate, "zl", self.label + "_z")
        self.last = (self.x, self.z)

    def finish(self, clock):
        x, z = clock.at_all(self.last)
        return self.own + x.astype(f32) + z.astype(f32)


VMEM_LIMIT = 60 * 2**20
WHOLE = tuple((i // 2, i, 0, 1) for i in range(8))
HALVES = WHOLE[:6] + tuple((3, slot, part, 2) for slot in (6, 7) for part in (0, 1))
ANY = pl.BlockSpec(memory_space=pl.ANY)
SMEM = pl.BlockSpec(memory_space=pltpu.SMEM)


class Loader:
    def __init__(self, sems):
        self.sems, self.used = sems, 0

    def copy(self, src, dst):
        self.used += 1
        return pltpu.make_async_copy(src, dst, self.sems.at[self.used - 1])

    def tokens(self, refs, held, coord):
        rows = held.shape[1]
        chips = [[], [], [], []]
        if len(refs) == 1:
            for slot in range(8):
                other = 2 * ((slot // 2) ^ coord[2]) + ((slot % 2) ^ coord[3])
                chips[slot // 2].append(self.copy(refs[0].at[other], held.at[slot]))
            return chips
        for ref, (chip, slot, part, parts) in zip(refs, HALVES if len(refs) == 10 else WHOLE):
            size = rows // parts
            chips[chip].append(self.copy(ref, held.at[slot, pl.ds(part * size, size)]))
        return chips

    def weight(self, refs, plan, held, coord):
        copies = []
        columns = pl.ds(plan.column, plan.width)
        if len(refs) == 4:
            for i, ref in enumerate(refs):
                zh, y = coord[0] ^ (i // 2), coord[1] ^ (i % 2)
                for zl in range(2):
                    block = ref.at[pl.ds(2 * zl, 2), :, columns]
                    row = ((zh * 2 + zl) * 2 + y) * 2
                    copies.append(self.copy(block, held.at[pl.ds(row, 2)]))
            return copies
        for i in range(refs[0].shape[0]):
            for zl in range(2):
                block = refs[0].at[i, pl.ds(2 * zl, 2), :, columns]
                row = ((i // 2 * 2 + zl) * 2 + i % 2) * 2
                copies.append(self.copy(block, held.at[pl.ds(row, 2)]))
        return copies


def start(*copies):
    for c in copies:
        c.start()


def wait(*copies):
    for c in copies:
        c.wait()


def at_chip(r, chips):
    for i, copies in enumerate(chips):
        pl.when(r == i)(functools.partial(wait, *copies))


def rows_of(held, r):
    pair = held[pl.ds(2 * r, 2)]
    return pair.reshape(2 * pair.shape[1], pair.shape[2])


def flat(w):
    value = w[...]
    return value.reshape(value.shape[0] * value.shape[1], value.shape[2])


def by_chip(shape):
    return pl.BlockSpec((1,) + shape, lambda r: (r,) + (0,) * len(shape))


def chip_kernel(body, operands, specs, outs, out_specs, scratch, copies, flops):
    moved = sum(a.size * a.dtype.itemsize for a in operands) + sum(
        o.size * jnp.dtype(o.dtype).itemsize for o in outs
    )
    return pl.pallas_call(
        body,
        grid=(4,),
        in_specs=specs,
        out_specs=out_specs,
        out_shape=outs,
        scratch_shapes=scratch + [pltpu.SemaphoreType.DMA((copies,))],
        compiler_params=pltpu.CompilerParams(
            dimension_semantics=("arbitrary",), vmem_limit_bytes=VMEM_LIMIT
        ),
        cost_estimate=pl.CostEstimate(flops=flops, bytes_accessed=moved, transcendentals=0),
    )(*operands)


def held_tokens(pieces):
    return pltpu.VMEM((8,) + pieces[0].shape[-2:], bf16)


def held_weight(w):
    devices = 16 if w.plan.count == 4 else 4 * w.arrays[0].shape[0]
    return pltpu.VMEM((devices, w.plan.rows, w.plan.width), bf16)


def arrays(*weights):
    return [a for w in weights for a in w.arrays]


def copies_of(*weights):
    return sum(8 if w.plan.count == 4 else 2 * w.arrays[0].shape[0] for w in weights)


def struct(shape, dtype):
    return jax.ShapeDtypeStruct(shape, dtype)


def partial_rows(grads, helds, r, keep, store):
    rows, blocks = keep.shape[1], helds[0].shape[0] // 4
    size = blocks * helds[0].shape[1]
    for j in range(4):
        parts = [
            dot(g, h[j * blocks : (j + 1) * blocks].reshape(size, h.shape[2]), NT)
            for g, h in zip(grads, helds)
        ]
        out = sum(parts[1:], parts[0]).astype(bf16)
        keep[0, :, j * size : (j + 1) * size] = out[:rows]
        store[r, :, j * size : (j + 1) * size] = out[rows:]


def send_copies(load, store, rest, diag):
    return [load.copy(store.at[i], rest.at[i]) for i in range(3)] + [load.copy(store.at[3], diag)]


def at_chip_start(r, copies):
    for i, c in enumerate(copies):
        pl.when(r == i)(c.start)

    @pl.when(r == 3)
    def _():
        wait(*copies)


def partial_outs(rows, model):
    outs = [
        struct((3, rows, model), bf16),
        struct((rows, model), bf16),
        struct((4, rows, model), bf16),
    ]
    return outs, [ANY, ANY, by_chip((rows, model))]


def attend_body(tokens, f_qk, f_v, coord, mask, *refs):
    acts, refs = refs[:tokens], refs[tokens:]
    wqk, refs = refs[: f_qk.count], refs[f_qk.count :]
    wv, refs = refs[: f_v.count], refs[f_v.count :]
    q_out, k_out, v_out, score_out, hat_out, scale_out, held, held_qk, held_v, sems = refs
    load, r = Loader(sems), pl.program_id(0)
    w1 = load.weight(wqk, f_qk, held_qk, coord)
    chips = load.tokens(acts, held, coord)
    w2 = load.weight(wv, f_v, held_v, coord)

    @pl.when(r == 0)
    def _():
        start(*w1, *chips[0], *w2, *chips[1], *chips[2], *chips[3])
        wait(*w1)

    at_chip(r, chips)
    x = rows_of(held, r)
    qk = dot(x, flat(held_qk), NN).astype(bf16)
    size = qk.shape[1] // 2
    q, k = qk[:, :size], qk[:, size:]
    q_out[0], k_out[0] = q, k
    scores = (dot(q, k, NT) * mask[0]).astype(bf16)
    score_out[0] = scores

    @pl.when(r == 0)
    def _():
        wait(*w2)

    v = dot(x, flat(held_v), NN).astype(bf16)
    v_out[0] = v
    hat_out[0] = dot(scores, v, NN)
    rows, step = hat_out.shape[1], 32

    def chunk(i, carry):
        at = pl.ds(pl.multiple_of(i * step, step), step)
        part = hat_out[0, at, :]
        part = part - jnp.mean(part, axis=-1, keepdims=True)
        scale = lax.rsqrt(jnp.mean(part * part, axis=-1, keepdims=True) + epsilon)
        hat_out[0, at, :] = part * scale
        scale_out[0, at, :] = jnp.broadcast_to(scale, (step, 128))
        return carry

    lax.fori_loop(0, rows // step, chunk, 0, unroll=4)


def attend(coord, mask, acts, wqk, wv, key_size):
    length, n = mask.shape[1], wv.plan.width
    model = acts[0].shape[-1]
    outs = [
        struct((4, length, key_size), bf16),
        struct((4, length, key_size), bf16),
        struct((4, length, n), bf16),
        struct((4, length, length), bf16),
        struct((4, length, n), f32),
        struct((4, length, 128), f32),
    ]
    return chip_kernel(
        functools.partial(attend_body, len(acts), wqk.plan, wv.plan),
        [coord, mask, *acts, *arrays(wqk, wv)],
        [SMEM, by_chip((length, length))] + [ANY] * (len(acts) + len(arrays(wqk, wv))),
        outs,
        [by_chip(o.shape[1:]) for o in outs],
        [held_tokens(acts), held_weight(wqk), held_weight(wv)],
        10 + copies_of(wqk, wv),
        16 * length * model * n,
    )


def branch_body(tokens, f_s, f_o, coord, hat, *refs):
    acts, refs = refs[:tokens], refs[tokens:]
    ws, refs = refs[: f_s.count], refs[f_s.count :]
    wo, refs = refs[: f_o.count], refs[f_o.count :]
    s_out, gated_out, rest, diag, keep, held, held_s, held_o, store, sems = refs
    load, r = Loader(sems), pl.program_id(0)
    w1 = load.weight(ws, f_s, held_s, coord)
    chips = load.tokens(acts, held, coord)
    w2 = load.weight(wo, f_o, held_o, coord)
    sends = send_copies(load, store, rest, diag)

    @pl.when(r == 0)
    def _():
        start(*w1, *chips[0], *w2, *chips[1], *chips[2], *chips[3])
        wait(*w1)

    at_chip(r, chips)
    s_out[0] = dot(rows_of(held, r), flat(held_s), NN)
    rows, step = s_out.shape[1], 32

    def chunk(i, carry):
        at = pl.ds(pl.multiple_of(i * step, step), step)
        s = s_out[0, at, :]
        gated_out[0, at, :] = (s / (1.0 + jnp.exp(-s)) * hat[0, at, :]).astype(bf16)
        return carry

    lax.fori_loop(0, rows // step, chunk, 0, unroll=4)

    @pl.when(r == 0)
    def _():
        wait(*w2)

    partial_rows([gated_out[0]], [held_o], r, keep, store)
    at_chip_start(r, sends)


def branch(coord, hat, acts, ws, wo):
    length, n = hat.shape[1:]
    rows, model = acts[0].shape[-2:]
    outs, out_specs = partial_outs(rows, model)
    outs = [struct((4, length, n), f32), struct((4, length, n), bf16)] + outs
    return chip_kernel(
        functools.partial(branch_body, len(acts), ws.plan, wo.plan),
        [coord, hat, *acts, *arrays(ws, wo)],
        [SMEM, by_chip((length, n))] + [ANY] * (len(acts) + len(arrays(ws, wo))),
        outs,
        [by_chip((length, n)), by_chip((length, n))] + out_specs,
        [held_tokens(acts), held_weight(ws), held_weight(wo), pltpu.VMEM((4, rows, model), bf16)],
        14 + copies_of(ws, wo),
        16 * length * model * n,
    )


def project_body(tokens, f_d, coord, *refs):
    acts, refs = refs[:tokens], refs[tokens:]
    wd, refs = refs[: f_d.count], refs[f_d.count :]
    out, held, held_d, sems = refs
    load, r = Loader(sems), pl.program_id(0)
    w1 = load.weight(wd, f_d, held_d, coord)
    chips = load.tokens(acts, held, coord)

    @pl.when(r == 0)
    def _():
        start(*w1, *chips[0], *chips[1], *chips[2], *chips[3])
        wait(*w1)

    at_chip(r, chips)
    out[0] = dot(rows_of(held, r), flat(held_d), NN)


def project(coord, acts, wd):
    rows, model = acts[0].shape[-2:]
    shape = (2 * rows, wd.plan.width)
    return chip_kernel(
        functools.partial(project_body, len(acts), wd.plan),
        [coord, *acts, *arrays(wd)],
        [SMEM] + [ANY] * (len(acts) + len(arrays(wd))),
        [struct((4,) + shape, f32)],
        [by_chip(shape)],
        [held_tokens(acts), held_weight(wd)],
        10 + copies_of(wd),
        16 * rows * model * wd.plan.width,
    )[0]


def feed_body(tokens, f_u, f_g, coord, gh, *refs):
    acts, refs = refs[:tokens], refs[tokens:]
    wu, refs = refs[: f_u.count], refs[f_u.count :]
    wg, refs = refs[: f_g.count], refs[f_g.count :]
    hidden_out, up_out, gate_out, rest, diag, keep = refs[:6]
    held, held_u, held_g, store, up, gate, sems = refs[6:]
    load, r = Loader(sems), pl.program_id(0)
    w1 = load.weight(wu, f_u, held_u, coord)
    w2 = load.weight(wg, f_g, held_g, coord)
    chips = load.tokens(acts, held, coord)
    sends = send_copies(load, store, rest, diag)

    @pl.when(r == 0)
    def _():
        start(*w1, *chips[0], *w2)
        for i in range(1, 4):
            start(*chips[i])
        wait(*w1)

    at_chip(r, chips)
    x = rows_of(held, r)
    up[...] = dot(x, flat(held_u), NN)

    @pl.when(r == 0)
    def _():
        wait(*w2)

    gate[...] = dot(x, flat(held_g), NN)
    step = 16

    def chunk(i, carry):
        at = pl.ds(pl.multiple_of(i * step, step), step)
        u, g, e = up[at, :], gate[at, :], gh[0, at, :]
        c = 0.7978845608028654
        square = g * g
        t = jnp.tanh(c * g * (1.0 + 0.044715 * square))
        half = 0.5 * (1.0 + t)
        gelu = g * half
        slope = half + (0.5 * c) * g * (1.0 - t * t) * (1.0 + (3 * 0.044715) * square)
        hidden_out[0, at, :] = (gelu * u).astype(bf16)
        up_out[0, at, :] = (e * gelu).astype(bf16)
        gate_out[0, at, :] = (e * u * slope).astype(bf16)
        return carry

    lax.fori_loop(0, up.shape[0] // step, chunk, 0, unroll=4)
    partial_rows([up_out[0], gate_out[0]], [held_u, held_g], r, keep, store)
    at_chip_start(r, sends)


def feed_forward(coord, gh, acts, wu, wg):
    rows, model = acts[0].shape[-2:]
    n = wu.plan.width
    outs, out_specs = partial_outs(rows, model)
    outs = [struct((4, 2 * rows, n), bf16)] * 3 + outs
    return chip_kernel(
        functools.partial(feed_body, len(acts), wu.plan, wg.plan),
        [coord, gh, *acts, *arrays(wu, wg)],
        [SMEM, by_chip((2 * rows, n))] + [ANY] * (len(acts) + len(arrays(wu, wg))),
        outs,
        [by_chip((2 * rows, n))] * 3 + out_specs,
        [
            held_tokens(acts),
            held_weight(wu),
            held_weight(wg),
            pltpu.VMEM((4, rows, model), bf16),
        ]
        + [pltpu.VMEM((2 * rows, n), f32)] * 2,
        14 + copies_of(wu, wg),
        64 * rows * model * n,
    )


def back_body(plans, whole, coord, *refs):
    count = len(plans)
    weights = []
    grads, refs = refs[:count], refs[count:]
    for plan in plans:
        weights.append(refs[: plan.count])
        refs = refs[plan.count :]
    load, r = Loader(refs[-1]), pl.program_id(0)
    if whole:
        result, helds, keep, store = refs[0], refs[1 : 1 + count], refs[-3], refs[-2]
    else:
        rest, diag, keep, helds, store = *refs[:3], refs[3 : 3 + count], refs[-2]
    copies = [load.weight(w, p, h, coord) for w, p, h in zip(weights, plans, helds)]

    @pl.when(r == 0)
    def _():
        for c in copies:
            start(*c)
        for c in copies:
            wait(*c)

    if not whole:
        sends = send_copies(load, store, rest, diag)
        partial_rows([g[0] for g in grads], helds, r, keep, store)
        at_chip_start(r, sends)
        return
    sends = []
    for i in range(4):
        at = 2 * (i ^ coord[2])
        sends.append(
            (
                load.copy(keep.at[i], result.at[at + coord[3]]),
                load.copy(store.at[i], result.at[at + (1 ^ coord[3])]),
            )
        )
    partial_rows([g[0] for g in grads], helds, r, keep.at[pl.ds(r, 1)], store)
    for i in range(4):
        pl.when(r == i)(functools.partial(start, *sends[i]))

    @pl.when(r == 3)
    def _():
        for c in sends:
            wait(*c)


def back(coord, grads, weights, whole=False):
    length = grads[0].shape[1]
    rows = length // 2
    held = held_weight(weights[0])
    model = held.shape[0] * held.shape[1]
    outs, out_specs = partial_outs(rows, model)
    store = pltpu.VMEM((4, rows, model), bf16)
    if whole:
        outs, out_specs = [struct((8, rows, model), bf16)], [ANY]
    return chip_kernel(
        functools.partial(back_body, tuple(w.plan for w in weights), whole),
        [coord, *grads, *arrays(*weights)],
        [SMEM] + [by_chip(g.shape[1:]) for g in grads] + [ANY] * len(arrays(*weights)),
        outs,
        out_specs,
        [held_weight(w) for w in weights] + [store] * (2 if whole else 1),
        8 + copies_of(*weights),
        8 * length * model * sum(g.shape[2] for g in grads),
    )


def attend_back_body(tokens, f_o, coord, mask, s, hat, scale, scores, q, k, v, *refs):
    acts, refs = refs[:tokens], refs[tokens:]
    wo, refs = refs[: f_o.count], refs[f_o.count :]
    gqk_out, gv_out, gs_out, held, held_o, dg, gr, sems = refs
    load, r = Loader(sems), pl.program_id(0)
    w1 = load.weight(wo, f_o, held_o, coord)
    chips = load.tokens(acts, held, coord)

    @pl.when(r == 0)
    def _():
        start(*w1, *chips[0], *chips[1], *chips[2], *chips[3])
        wait(*w1)

    at_chip(r, chips)
    dg[...] = dot(rows_of(held, r), flat(held_o), NN)
    rows, step = dg.shape[0], 16

    def chunk(i, carry):
        at = pl.ds(pl.multiple_of(i * step, step), step)
        e, x, v_s = dg[at, :], hat[0, at, :], s[0, at, :]
        gate = 1.0 / (1.0 + jnp.exp(-v_s))
        silu = v_s * gate
        gs_out[0, at, :] = (e * x * (gate + silu * (1.0 - gate))).astype(bf16)
        f = e * silu
        f = f - jnp.mean(f, axis=-1, keepdims=True) - x * jnp.mean(f * x, axis=-1, keepdims=True)
        gr[at, :] = (f * scale[0, at, :1]).astype(bf16)
        return carry

    lax.fori_loop(0, rows // step, chunk, 0, unroll=4)
    grad_retained = gr[...]
    gv_out[0] = dot(scores[0], grad_retained, TN).astype(bf16)
    raw = (dot(grad_retained, v[0], NT) * mask[0]).astype(bf16)
    size = q.shape[2]
    gqk_out[0, :, :size] = dot(raw, k[0], NN).astype(bf16)
    gqk_out[0, :, size:] = dot(raw, q[0], TN).astype(bf16)


def attend_back(coord, mask, s, hat, scale, scores, q, k, v, acts, wo):
    length, n = s.shape[1:]
    model = acts[0].shape[-1]
    blocks = [mask, s, hat, scale, scores, q, k, v]
    outs = [struct((4, length, 2 * q.shape[2]), bf16)] + [struct((4, length, n), bf16)] * 2
    return chip_kernel(
        functools.partial(attend_back_body, len(acts), wo.plan),
        [coord, *blocks, *acts, *arrays(wo)],
        [SMEM] + [by_chip(b.shape[1:]) for b in blocks] + [ANY] * (len(acts) + len(arrays(wo))),
        outs,
        [by_chip(o.shape[1:]) for o in outs],
        [
            held_tokens(acts),
            held_weight(wo),
            pltpu.VMEM((length, n), f32),
            pltpu.VMEM((length, n), bf16),
        ],
        10 + copies_of(wo),
        12 * length * model * n,
    )


def weight_grad_body(count, tokens, whole, coord, *refs):
    grads, refs = refs[:count], refs[count:]
    acts, refs = refs[:tokens], refs[tokens:]
    outs, held, sems = refs[:-2], refs[-2], refs[-1]
    load, i = Loader(sems), pl.program_id(0)
    chips = load.tokens(acts, held, coord)

    @pl.when(i == 0)
    def _():
        for c in chips:
            start(*c)
        for c in chips:
            wait(*c)

    width = held.shape[2] // 8
    j = i % 4
    if whole:
        column = ((i // 4 * 2 + i % 2) * 2 + i // 2 % 2) * width
    else:
        y = coord[1] ^ jnp.where(i < 4, 1, 0)
        zh = coord[0] ^ jnp.where(j < 2, 1, 0)
        column = ((zh * 2 + j % 2) * 2 + y) * width
    x = held[:, :, pl.ds(pl.multiple_of(column, width), width)]
    x = x.reshape(x.shape[0] * x.shape[1], width).T
    for n in range(count):
        g = grads[n][...]
        size = g.shape[2]
        out = dot(x, g.reshape(g.shape[0] * g.shape[1], size), NN).astype(bf16)
        if whole:
            outs[0][0, :, n * size : (n + 1) * size] = out
            continue
        pl.when(i < 4)(functools.partial(store_block, outs[2 * n], out))
        pl.when(i >= 4)(functools.partial(store_block, outs[2 * n + 1], out))


def store_block(ref, value):
    ref[0] = value


def weight_grads(coord, acts, grads, whole=False):
    rows, model = acts[0].shape[-2:]
    outs, out_specs = [], []
    width = sum(g.shape[2] for g in grads)
    for g in grads:
        shape = (4, model // 8, g.shape[2])
        outs += [struct(shape, bf16)] * 2
        out_specs += [
            pl.BlockSpec((1,) + shape[1:], lambda i: (jnp.minimum(i, 3), 0, 0)),
            pl.BlockSpec((1,) + shape[1:], lambda i: (jnp.maximum(i - 4, 0), 0, 0)),
        ]
    if whole:
        outs = [struct((8, model // 8, width), bf16)]
        out_specs = [pl.BlockSpec((1, model // 8, width), lambda i: (i, 0, 0))]
    moved = sum(a.size * 2 for a in acts) + sum(g.size * 2 for g in grads) + 2 * model * width
    got = pl.pallas_call(
        functools.partial(weight_grad_body, len(grads), len(acts), whole),
        grid=(8,),
        in_specs=[SMEM] + [pl.BlockSpec(memory_space=pltpu.VMEM)] * len(grads) + [ANY] * len(acts),
        out_specs=out_specs,
        out_shape=outs,
        scratch_shapes=[held_tokens(acts), pltpu.SemaphoreType.DMA((10,))],
        compiler_params=pltpu.CompilerParams(
            dimension_semantics=("arbitrary",), vmem_limit_bytes=VMEM_LIMIT
        ),
        cost_estimate=pl.CostEstimate(
            flops=16 * rows * model * width, bytes_accessed=moved, transcendentals=0
        ),
    )(coord, *grads, *acts)
    if whole:
        return got[0]
    return [(got[2 * i], got[2 * i + 1]) for i in range(len(grads))]


def place_body(parts, g, *outs):
    column = 0
    for (width, way), out in zip(parts, outs):
        value = g[0, :, column : column + width].astype(f32)
        out[...] = value.T if way == "r" else value
        column += width


def place(g, parts):
    rows = g.shape[1]
    outs, specs = [], []
    for width, way in parts:
        if way == "r":
            outs.append(struct((4 * width, rows), f32))
            specs.append(pl.BlockSpec((width, rows), lambda q: (q, 0)))
        else:
            outs.append(struct((rows, 4 * width), f32))
            specs.append(pl.BlockSpec((rows, width), lambda q: (0, q)))
    return pl.pallas_call(
        functools.partial(place_body, parts),
        grid=(4,),
        in_specs=[by_chip(g.shape[1:])],
        out_specs=specs,
        out_shape=outs,
        compiler_params=pltpu.CompilerParams(dimension_semantics=("arbitrary",)),
        cost_estimate=pl.CostEstimate(flops=0, bytes_accessed=6 * g.size, transcendentals=0),
    )(g)


def scatter_whole(g):
    zh, n = lax.axis_size("zh"), g.shape[2]
    if zh == 2:
        g = g.reshape(4, 4, -1, n)
    else:
        g = g.reshape(2, 2, 2, -1, n).transpose(0, 2, 1, 3, 4).reshape(zh, 2, 2, 2, -1, n)
        g = g.transpose(0, 2, 1, 3, 4, 5).reshape(2 * zh, 4, -1, n)
    g = lax.psum_scatter(g, ("zh", "y"), scatter_dimension=0, tiled=True)
    return g.reshape(4, -1, n)


def sum_everywhere(a):
    for axis in ("tensor",) + SPREAD:
        if lax.axis_size(axis) == 2:
            a = a + swap(a, axis)
        else:
            a = lax.psum(a, axis)
    return a


def local(
    tokens,
    segments,
    decay,
    norm1_gain,
    w_query,
    w_key,
    w_value,
    w_swish,
    w_out,
    norm2_gain,
    w_up,
    w_gate,
    w_down,
    cotangent,
):
    rows_q, width = w_query.shape[0], w_value.shape[1] // 4
    quarter = 2 * lax.axis_index("zl") + lax.axis_index("x")
    core = lax.axis_index("tensor")
    length = segments.shape[0]
    rows_each = tokens.shape[0]
    key_size = w_query.shape[1] // 4
    value_size = w_value.shape[1] // 4
    rate = take(decay, quarter, 0)

    ids = [jnp.zeros((), jnp.int32)] * 2
    if lax.axis_size("zh") == 2:
        ids = [lax.axis_index("zh"), lax.axis_index("y")]
    coord = jnp.stack(ids + [quarter, core]).astype(jnp.int32)
    clock, free = Clock(), Clock()
    at = clock.at
    rows_local = tokens.astype(f32)
    everyone = ("zl", "x", "tensor")

    pipe = WeightPipe()
    seg_x, seg_z = swap(segments, "x", "seg"), swap(segments, "zl", "seg")
    with jax.named_scope("seg"):
        seg_d = lax.ppermute(segments, GROUP, [(i, 3 - i) for i in range(4)])
    parts = (by_quarter(w) for w in (w_query, w_key, w_value))
    piece = group_exchange(beside(*parts))
    parts = beside(by_quarter(w_swish), by_quarter(w_out.T))

    clock.done(piece, parts)
    unit_qkv = pipe.step(clock, piece, "qkv")
    piece = group_exchange(at(parts))
    normed_local = layer_norm(rows_local, norm1_gain).astype(bf16)
    normed = [lax.all_gather(at(normed_local), everyone, axis=0)]
    segs = jnp.stack([segments, seg_x, seg_z, seg_d])
    segs = jnp.where(core == 0, segs, jnp.roll(segs, length // 2, 1))
    position = (jnp.arange(length, dtype=jnp.int32) + core * rows_each) % length
    offset = position[:, None] - position[None, :]
    allowed = (offset >= 0)[None] & (segs[:, :, None] == segs[:, None, :])
    distance = jnp.maximum(offset, 0).astype(f32)
    decay_mask = jnp.where(allowed, jnp.exp(-rate * distance)[None], 0.0)
    parts = beside(by_quarter(at(w_up)), by_quarter(at(w_gate)), by_quarter(at(w_down).T))

    clock.done(piece, parts, decay_mask, *pipe.moved)
    unit_so = pipe.step(clock, piece, "so")
    piece = group_exchange(at(parts))
    full_qk, full_value = unit_qkv.weight(0, width), unit_qkv.weight(width, width)
    query, key, values, scores, hat, scale = attend(
        at(coord), decay_mask, normed, full_qk, full_value, key_size
    )

    clock.done(query, piece, *pipe.moved)
    grad_rows = [lax.all_gather(at(cotangent), everyone, axis=0)]
    unit_ug = pipe.step(clock, piece[:, :, : 2 * width], "ug")
    full_swish, full_out = unit_so.weight(0, width), unit_so.weight(width, width)
    swish_in, gated, *partial = branch(at(coord), hat, normed, full_swish, full_out)
    clock.done(*pipe.moved, *partial)
    unit_d = pipe.step(clock, piece[:, :, 2 * width :], "d")
    scatter = Scatter(*partial, "branch", clock)
    scatter.relay(free)
    clock.done(*scatter.second)
    scatter.send(clock)
    clock.done(*scatter.last, *pipe.moved)
    middle = rows_local + scatter.finish(clock)
    normed_two_local = layer_norm(middle, norm2_gain).astype(bf16)
    gather = Gather(clock, normed_two_local, "two", True)
    far_y = pipe.finish(clock)
    clock.done(*far_y, *gather.first)
    gather.second(clock)
    full_up, full_gate = unit_ug.weight(0, width), unit_ug.weight(width, width)
    full_down = unit_d.weight(0, width)
    grad_hidden = project(at(coord), grad_rows, full_down)
    clock.done(grad_hidden, *gather.held)
    normed_two = gather.finish(clock)
    hidden, grad_up_rows, grad_gate_rows, *partial = feed_forward(
        at(coord), grad_hidden, normed_two, full_up, full_gate
    )

    scatter = Scatter(*partial, "back_two", free)
    clock.done(scatter.diag)
    scatter.relay(clock)
    (g_down,) = weight_grads(at(coord), grad_rows, [hidden])
    g_down = WeightGrad(g_down, "down")
    clock.done(g_down.send, *scatter.second)
    scatter.send(clock)
    g_down.to_y(clock)
    g_up, g_gate = weight_grads(at(coord), normed_two, [grad_up_rows, grad_gate_rows])
    g_up, g_gate = WeightGrad(g_up, "up"), WeightGrad(g_gate, "gate")
    clock.done(g_up.send, g_down.y, *scatter.last)
    back_two_local = scatter.finish(clock)
    _, norm_two_pull = jax.vjp(layer_norm, middle, norm2_gain)
    grad_mid_norm, grad_norm2_local = norm_two_pull(back_two_local)
    grad_middle = cotangent.astype(f32) + grad_mid_norm
    grad_branch_local = grad_middle.astype(bf16)

    clock.done(grad_branch_local)
    gather = Gather(clock, grad_branch_local, "gb", True)
    g_down.to_zh(clock)
    g_up.to_y(clock)
    clock.done(g_down.zh, g_up.y, *gather.first)
    gather.second(clock)
    g_gate.to_y(clock)
    (feed,) = back(at(coord), [hidden], [full_down], True)
    clock.done(feed, *gather.held)
    grad_branch = gather.finish(clock)
    feed = lax.psum_scatter(at(feed), everyone, scatter_dimension=0, tiled=True)
    g_up.to_zh(clock)
    grad_qk, grad_values, grad_swish_in = attend_back(
        at(coord),
        decay_mask,
        swish_in,
        hat,
        scale,
        scores,
        query,
        key,
        values,
        grad_branch,
        full_out,
    )
    clock.done(grad_qk, g_up.zh, g_gate.y)
    g_gate.to_zh(clock)
    (g_out,) = weight_grads(at(coord), grad_branch, [gated])
    g_out = WeightGrad(g_out, "out")
    clock.done(g_out.send)
    g_out.to_y(clock)
    (g_swish,) = weight_grads(at(coord), normed, [grad_swish_in])
    g_swish = WeightGrad(g_swish, "swish")
    clock.done(g_swish.send, g_gate.zh)
    g_value, g_qk = weight_grads(at(coord), normed, [grad_values, grad_qk])
    g_value, g_qk = WeightGrad(g_value, "value"), WeightGrad(g_qk, "qk")
    clock.done(g_value.send, g_out.y)
    g_out.to_zh(clock)
    g_swish.to_y(clock)
    partial = back(
        at(coord), [grad_qk, grad_values, grad_swish_in], [full_qk, full_value, full_swish]
    )
    clock.done(g_out.zh, g_swish.y, *partial)
    g_swish.to_zh(clock)
    g_value.to_y(clock)
    scatter = Scatter(*partial, "back_one", clock)
    clock.done(scatter.diag)
    scatter.relay(clock, True)
    clock.done(*scatter.second)
    scatter.send(clock)
    clock.done(g_swish.zh, g_value.y)
    g_value.to_zh(clock)
    g_qk.to_y(clock)
    grad_ff = group_exchange(beside(g_up.sum(clock), g_gate.sum(clock), g_down.sum(clock)))
    clock.done(g_value.zh, g_qk.y)
    g_qk.to_zh(clock)
    clock.done(*scatter.last)
    back_one_local = scatter.finish(clock)
    grad_os = group_exchange(after(beside(g_out.sum(clock), g_swish.sum(clock)), grad_ff))
    grad_up, grad_gate, grad_down = place(at(grad_ff), ((width, "c"), (width, "c"), (width, "r")))
    mixed = (middle + feed.reshape(middle.shape).astype(f32)).astype(bf16)
    _, norm_one_pull = jax.vjp(layer_norm, rows_local, norm1_gain)
    grad_tok_norm, grad_norm1_local = norm_one_pull(back_one_local)
    grad_tokens = grad_middle + grad_tok_norm
    grad_norm1, grad_norm2 = sum_everywhere(
        after(jnp.stack([grad_norm1_local, grad_norm2_local]), g_qk.zh)
    )
    clock.done(g_qk.zh, grad_os, grad_up, mixed, grad_norm1, grad_tokens)
    grad_qkv = group_exchange(beside(g_qk.sum(clock), g_value.sum(clock)))
    grad_out, grad_swish = place(at(grad_os), ((width, "r"), (width, "c")))
    parts = ((key_size, "c"), (key_size, "c"), (width, "c"))
    grad_query, grad_key, grad_value = place(grad_qkv, parts)

    return (
        mixed,
        grad_tokens,
        grad_norm1,
        grad_query,
        grad_key,
        grad_value,
        grad_swish,
        grad_out,
        grad_norm2,
        grad_up,
        grad_gate,
        grad_down,
    )


def solution(mesh):
    dp, tensor = mesh.shape["dp"], mesh.shape["tensor"]
    grid = Mesh(mesh.devices.reshape(dp // 8, 2, 2, 2, tensor), SPREAD + ("tensor",))
    rows = P(SPREAD + ("tensor",), None)
    rows_split = P(SPREAD, "tensor")
    columns_split = P("tensor", SPREAD)
    return jax.shard_map(
        local,
        mesh=grid,
        in_specs=(
            rows,
            P(SPREAD),
            P("tensor"),
            P(),
            rows_split,
            rows_split,
            rows_split,
            rows_split,
            columns_split,
            P(),
            rows_split,
            rows_split,
            columns_split,
            rows,
        ),
        out_specs=(
            rows,
            rows,
            P(),
            rows_split,
            rows_split,
            rows_split,
            rows_split,
            columns_split,
            P(),
            rows_split,
            rows_split,
            columns_split,
        ),
        check_vma=False,
    )
```

```python
import functools
import jax
import jax.numpy as jnp
from jax import lax
from jax.experimental import pallas as pl
from jax.experimental.pallas import tpu as pltpu
from jax.sharding import Mesh, PartitionSpec as P

epsilon = 1e-05
bf16 = jnp.bfloat16
f32 = jnp.float32
SPREAD = ("zh", "zl", "y", "x")
GROUP = ("zl", "x")


def normalize(values):
    centred = values - jnp.mean(values, axis=-1, keepdims=True)
    variance = jnp.mean(centred * centred, axis=-1, keepdims=True)
    return centred * lax.rsqrt(variance + epsilon)


def layer_norm(rows, gain):
    return normalize(rows) * gain


def dot(left, right, dims):
    return lax.dot_general(left, right, (dims, ((), ())), preferred_element_type=f32)


NN = ((1,), (0,))
NT = ((1,), (1,))
TN = ((0,), (0,))


def swap(a, axis, label="move"):
    with jax.named_scope(label):
        return lax.ppermute(a, axis, [(0, 1), (1, 0)])


def after(value, *others):
    return lax.optimization_barrier((value,) + others)[0]


def ordered(own, other, axis, dim):
    first = lax.axis_index(axis) == 0
    return jnp.stack([jnp.where(first, own, other), jnp.where(first, other, own)], dim)


def by_quarter(w):
    rows, cols = w.shape
    return w.reshape(rows, 4, cols // 4).transpose(1, 0, 2)


def beside(*parts):
    return jnp.concatenate(parts, 2)


def group_exchange(parts):
    return lax.all_to_all(parts, GROUP, 0, 0, tiled=True)


def take(a, index, dim):
    return lax.dynamic_index_in_dim(a, index, dim, keepdims=False)


def add(a, b):
    return (a.astype(f32) + b.astype(f32)).astype(bf16)


def scatter_y(keep, got):
    n = got.shape[-1]
    if lax.axis_size("zh") == 2:
        return add(keep[:2], got[:2]), add(keep[2:], got[2:])
    flip = lambda g: jnp.flip(g.reshape(2, 2, 1, -1, n), 0)
    g = jnp.concatenate([flip(keep), flip(got)], 2).reshape(lax.axis_size("zh"), 2, 2, 2, -1, n)
    y = lax.axis_index("y")
    return add(take(g, y, 2), swap(take(g, 1 - y, 2), "y")), None


def send_y(send, label):
    return swap(send, "y", label) if lax.axis_size("zh") == 2 else send


def send_zh(send, label):
    return swap(send, "zh", label) if lax.axis_size("zh") == 2 else send


def scatter_zh(keep, got):
    if lax.axis_size("zh") == 2:
        g = add(keep, got)
    else:
        g = lax.psum_scatter(got, "zh", scatter_dimension=0)
    return g.reshape(4, -1, g.shape[-1])


class WeightGrad:
    def __init__(self, pair, label):
        self.send, self.keep, self.label = *pair, label

    def to_y(self, clock):
        self.y = send_y(clock.at(self.send), "y_" + self.label)

    def to_zh(self, clock):
        send, self.keep = scatter_y(self.keep, clock.at(self.y))
        self.zh = send_zh(send, "zh_g" + self.label)

    def sum(self, clock):
        return scatter_zh(self.keep, clock.at(self.zh))


class Clock:
    def __init__(self):
        self.now = ()

    def done(self, *values):
        self.now = values

    def at(self, value):
        return after(value, *self.now)

    def at_all(self, values):
        return lax.optimization_barrier(tuple(values) + self.now)[: len(values)]


class Plan:
    def __init__(self, count, rows, width, column):
        self.count, self.rows, self.width, self.column = count, rows, width, column


class Weight:
    def __init__(self, arrays, plan):
        self.arrays, self.plan = arrays, plan


class Unit:
    def __init__(self, arrays, rows):
        self.arrays, self.rows = arrays, rows

    def weight(self, column, width):
        return Weight(self.arrays, Plan(len(self.arrays), self.rows, width, column))


class WeightPipe:
    def __init__(self):
        self.last = None

    def step(self, clock, piece, label):
        piece = clock.at(piece)
        if lax.axis_size("zh") != 2:
            whole = gather_weight(piece)
            self.moved = (whole,)
            return Unit([whole], piece.shape[1])
        far, near = swap(piece, "zh", "zh_" + label), swap(piece, "y", "ny_" + label)
        self.moved = (far, near)
        self.carry(clock)
        self.last = Unit([piece, near, far], piece.shape[1])
        self.label = label
        return self.last

    def carry(self, clock):
        if self.last is not None:
            far_y = swap(clock.at(self.last.arrays[2]), "y", "fy_" + self.label)
            self.last.arrays.append(far_y)
            self.moved += (far_y,)

    def finish(self, clock):
        self.moved = ()
        self.carry(clock)
        return self.moved


def gather_weight(piece):
    return lax.all_gather(piece, ("zh", "y"), axis=0)


class Gather:
    def __init__(self, clock, a, label, halves=False):
        self.a, self.label, self.halves = clock.at(a), label, halves
        self.x = swap(self.a, "x", label + "_x")
        self.z = swap(self.a, "zl", label + "_z")
        self.c = swap(self.a, "tensor", label + "_c")
        self.first = (self.x, self.z, self.c)

    def second(self, clock):
        half, label = self.a.shape[0] // 2, self.label
        ax, az = clock.at_all((self.x, self.z))
        if self.halves:
            self.diag = (swap(az[:half], "x", label + "_dx"), swap(ax[half:], "zl", label + "_dz"))
        else:
            self.diag = (swap(az, "x", label + "_dx"),)
        self.pieces = [self.a, self.c]
        self.pieces += [ax, swap(ax, "tensor", label + "_c"), az, swap(az, "tensor", label + "_c")]
        self.held = (*self.pieces, *self.diag)

    def finish(self, clock):
        diag = clock.at_all(self.diag)
        return [*self.pieces, *diag, *(swap(d, "tensor", self.label + "_c") for d in diag)]


class Scatter:
    def __init__(self, send_rest, send_diag, keep, label, clock):
        self.label, self.keep = label, keep
        send_rest, send_diag = clock.at_all((send_rest, send_diag))
        self.diag = add(keep[3], swap(send_diag, "tensor", label + "_cd"))
        self.rest = swap(send_rest, "tensor", label + "_cr")

    def relay(self, clock, whole=False):
        half = self.diag.shape[0] // 2
        diag = clock.at(self.diag)
        self.whole = whole
        if whole:
            self.through_x = swap(diag, "x", self.label + "_dx")
            self.second = (self.through_x, self.rest)
            return
        self.through_x = swap(diag[:half], "x", self.label + "_dx")
        self.through_z = swap(diag[half:], "zl", self.label + "_dz")
        self.second = (self.through_x, self.through_z, self.rest)

    def send(self, clock):
        *through, rest = (v.astype(f32) for v in clock.at_all(self.second))
        xmate, zmate = (self.keep[r].astype(f32) + rest[r] for r in (1, 2))
        if self.whole:
            self.x = swap(xmate.astype(bf16), "x", self.label + "_x")
            self.z = swap((zmate + through[0]).astype(bf16), "zl", self.label + "_z")
            self.last = (self.x, self.z)
            return
        through_x, through_z = through
        half = through_x.shape[0]
        zmate = jnp.concatenate([zmate[:half] + through_x, zmate[half:]]).astype(bf16)
        xmate = jnp.concatenate([xmate[:half], xmate[half:] + through_z]).astype(bf16)
        self.x = swap(xmate, "x", self.label + "_x")
        self.z = swap(zmate, "zl", self.label + "_z")
        self.last = (self.x, self.z)

    def finish(self, clock):
        x, z = clock.at_all(self.last)
        own = self.keep[0].astype(f32) + self.rest[0].astype(f32)
        return own + x.astype(f32) + z.astype(f32)


VMEM_LIMIT = 60 * 2**20
WHOLE = tuple((i // 2, i, 0, 1) for i in range(8))
HALVES = WHOLE[:6] + tuple((3, slot, part, 2) for slot in (6, 7) for part in (0, 1))
ANY = pl.BlockSpec(memory_space=pl.ANY)
SMEM = pl.BlockSpec(memory_space=pltpu.SMEM)


class Loader:
    def __init__(self, sems):
        self.sems, self.used = sems, 0

    def copy(self, src, dst):
        self.used += 1
        return pltpu.make_async_copy(src, dst, self.sems.at[self.used - 1])

    def tokens(self, refs, held, coord):
        rows = held.shape[1]
        chips = [[], [], [], []]
        if len(refs) == 1:
            for slot in range(8):
                other = 2 * ((slot // 2) ^ coord[2]) + ((slot % 2) ^ coord[3])
                chips[slot // 2].append(self.copy(refs[0].at[other], held.at[slot]))
            return chips
        for ref, (chip, slot, part, parts) in zip(refs, HALVES if len(refs) == 10 else WHOLE):
            size = rows // parts
            chips[chip].append(self.copy(ref, held.at[slot, pl.ds(part * size, size)]))
        return chips

    def weight(self, refs, plan, held, coord):
        copies = []
        columns = pl.ds(plan.column, plan.width)
        if len(refs) == 4:
            for i, ref in enumerate(refs):
                zh, y = coord[0] ^ (i // 2), coord[1] ^ (i % 2)
                for zl in range(2):
                    block = ref.at[pl.ds(2 * zl, 2), :, columns]
                    row = ((zh * 2 + zl) * 2 + y) * 2
                    copies.append(self.copy(block, held.at[pl.ds(row, 2)]))
            return copies
        for i in range(refs[0].shape[0]):
            for zl in range(2):
                block = refs[0].at[i, pl.ds(2 * zl, 2), :, columns]
                row = ((i // 2 * 2 + zl) * 2 + i % 2) * 2
                copies.append(self.copy(block, held.at[pl.ds(row, 2)]))
        return copies


def start(*copies):
    for c in copies:
        c.start()


def wait(*copies):
    for c in copies:
        c.wait()


def at_chip(r, chips):
    for i, copies in enumerate(chips):
        pl.when(r == i)(functools.partial(wait, *copies))


def rows_of(held, r):
    pair = held[pl.ds(2 * r, 2)]
    return pair.reshape(2 * pair.shape[1], pair.shape[2])


def flat(w):
    value = w[...]
    return value.reshape(value.shape[0] * value.shape[1], value.shape[2])


def by_chip(shape):
    return pl.BlockSpec((1,) + shape, lambda r: (r,) + (0,) * len(shape))


def chip_kernel(body, operands, specs, outs, out_specs, scratch, copies, flops):
    moved = sum(a.size * a.dtype.itemsize for a in operands) + sum(
        o.size * jnp.dtype(o.dtype).itemsize for o in outs
    )
    return pl.pallas_call(
        body,
        grid=(4,),
        in_specs=specs,
        out_specs=out_specs,
        out_shape=outs,
        scratch_shapes=scratch + [pltpu.SemaphoreType.DMA((copies,))],
        compiler_params=pltpu.CompilerParams(
            dimension_semantics=("arbitrary",), vmem_limit_bytes=VMEM_LIMIT
        ),
        cost_estimate=pl.CostEstimate(flops=flops, bytes_accessed=moved, transcendentals=0),
    )(*operands)


def held_tokens(pieces):
    return pltpu.VMEM((8,) + pieces[0].shape[-2:], bf16)


def held_weight(w):
    devices = 16 if w.plan.count == 4 else 4 * w.arrays[0].shape[0]
    return pltpu.VMEM((devices, w.plan.rows, w.plan.width), bf16)


def arrays(*weights):
    return [a for w in weights for a in w.arrays]


def copies_of(*weights):
    return sum(8 if w.plan.count == 4 else 2 * w.arrays[0].shape[0] for w in weights)


def struct(shape, dtype):
    return jax.ShapeDtypeStruct(shape, dtype)


def partial_rows(grads, helds, r, keep, store):
    rows, blocks = keep.shape[1], helds[0].shape[0] // 4
    size = blocks * helds[0].shape[1]
    for j in range(4):
        parts = [
            dot(g, h[j * blocks : (j + 1) * blocks].reshape(size, h.shape[2]), NT)
            for g, h in zip(grads, helds)
        ]
        out = sum(parts[1:], parts[0]).astype(bf16)
        keep[0, :, j * size : (j + 1) * size] = out[:rows]
        store[r, :, j * size : (j + 1) * size] = out[rows:]


def send_copies(load, store, rest, diag):
    return [load.copy(store.at[i], rest.at[i]) for i in range(3)] + [load.copy(store.at[3], diag)]


def at_chip_start(r, copies):
    for i, c in enumerate(copies):
        pl.when(r == i)(c.start)

    @pl.when(r == 3)
    def _():
        wait(*copies)


def partial_outs(rows, model):
    outs = [
        struct((3, rows, model), bf16),
        struct((rows, model), bf16),
        struct((4, rows, model), bf16),
    ]
    return outs, [ANY, ANY, by_chip((rows, model))]


def attend_body(tokens, f_qk, f_v, coord, mask, *refs):
    acts, refs = refs[:tokens], refs[tokens:]
    wqk, refs = refs[: f_qk.count], refs[f_qk.count :]
    wv, refs = refs[: f_v.count], refs[f_v.count :]
    q_out, k_out, v_out, score_out, hat_out, scale_out, held, held_qk, held_v, sems = refs
    load, r = Loader(sems), pl.program_id(0)
    w1 = load.weight(wqk, f_qk, held_qk, coord)
    chips = load.tokens(acts, held, coord)
    w2 = load.weight(wv, f_v, held_v, coord)

    @pl.when(r == 0)
    def _():
        start(*w1, *chips[0], *w2, *chips[1], *chips[2], *chips[3])
        wait(*w1)

    at_chip(r, chips)
    x = rows_of(held, r)
    qk = dot(x, flat(held_qk), NN).astype(bf16)
    size = qk.shape[1] // 2
    q, k = qk[:, :size], qk[:, size:]
    q_out[0], k_out[0] = q, k
    scores = (dot(q, k, NT) * mask[0]).astype(bf16)
    score_out[0] = scores

    @pl.when(r == 0)
    def _():
        wait(*w2)

    v = dot(x, flat(held_v), NN).astype(bf16)
    v_out[0] = v
    hat_out[0] = dot(scores, v, NN)
    rows, step = hat_out.shape[1], 32

    def chunk(i, carry):
        at = pl.ds(pl.multiple_of(i * step, step), step)
        part = hat_out[0, at, :]
        part = part - jnp.mean(part, axis=-1, keepdims=True)
        scale = lax.rsqrt(jnp.mean(part * part, axis=-1, keepdims=True) + epsilon)
        hat_out[0, at, :] = part * scale
        scale_out[0, at, :] = jnp.broadcast_to(scale, (step, 128))
        return carry

    lax.fori_loop(0, rows // step, chunk, 0, unroll=4)


def attend(coord, mask, acts, wqk, wv, key_size):
    length, n = mask.shape[1], wv.plan.width
    model = acts[0].shape[-1]
    outs = [
        struct((4, length, key_size), bf16),
        struct((4, length, key_size), bf16),
        struct((4, length, n), bf16),
        struct((4, length, length), bf16),
        struct((4, length, n), f32),
        struct((4, length, 128), f32),
    ]
    return chip_kernel(
        functools.partial(attend_body, len(acts), wqk.plan, wv.plan),
        [coord, mask, *acts, *arrays(wqk, wv)],
        [SMEM, by_chip((length, length))] + [ANY] * (len(acts) + len(arrays(wqk, wv))),
        outs,
        [by_chip(o.shape[1:]) for o in outs],
        [held_tokens(acts), held_weight(wqk), held_weight(wv)],
        10 + copies_of(wqk, wv),
        16 * length * model * n,
    )


def branch_body(tokens, f_s, f_o, coord, hat, *refs):
    acts, refs = refs[:tokens], refs[tokens:]
    ws, refs = refs[: f_s.count], refs[f_s.count :]
    wo, refs = refs[: f_o.count], refs[f_o.count :]
    s_out, gated_out, rest, diag, keep, held, held_s, held_o, store, sems = refs
    load, r = Loader(sems), pl.program_id(0)
    w1 = load.weight(ws, f_s, held_s, coord)
    chips = load.tokens(acts, held, coord)
    w2 = load.weight(wo, f_o, held_o, coord)
    sends = send_copies(load, store, rest, diag)

    @pl.when(r == 0)
    def _():
        start(*w1, *chips[0], *w2, *chips[1], *chips[2], *chips[3])
        wait(*w1)

    at_chip(r, chips)
    s_out[0] = dot(rows_of(held, r), flat(held_s), NN)
    rows, step = s_out.shape[1], 32

    def chunk(i, carry):
        at = pl.ds(pl.multiple_of(i * step, step), step)
        s = s_out[0, at, :]
        gated_out[0, at, :] = (s / (1.0 + jnp.exp(-s)) * hat[0, at, :]).astype(bf16)
        return carry

    lax.fori_loop(0, rows // step, chunk, 0, unroll=4)

    @pl.when(r == 0)
    def _():
        wait(*w2)

    partial_rows([gated_out[0]], [held_o], r, keep, store)
    at_chip_start(r, sends)


def branch(coord, hat, acts, ws, wo):
    length, n = hat.shape[1:]
    rows, model = acts[0].shape[-2:]
    outs, out_specs = partial_outs(rows, model)
    outs = [struct((4, length, n), f32), struct((4, length, n), bf16)] + outs
    return chip_kernel(
        functools.partial(branch_body, len(acts), ws.plan, wo.plan),
        [coord, hat, *acts, *arrays(ws, wo)],
        [SMEM, by_chip((length, n))] + [ANY] * (len(acts) + len(arrays(ws, wo))),
        outs,
        [by_chip((length, n)), by_chip((length, n))] + out_specs,
        [held_tokens(acts), held_weight(ws), held_weight(wo), pltpu.VMEM((4, rows, model), bf16)],
        14 + copies_of(ws, wo),
        16 * length * model * n,
    )


def project_body(tokens, f_d, coord, *refs):
    acts, refs = refs[:tokens], refs[tokens:]
    wd, refs = refs[: f_d.count], refs[f_d.count :]
    out, held, held_d, sems = refs
    load, r = Loader(sems), pl.program_id(0)
    w1 = load.weight(wd, f_d, held_d, coord)
    chips = load.tokens(acts, held, coord)

    @pl.when(r == 0)
    def _():
        start(*w1, *chips[0], *chips[1], *chips[2], *chips[3])
        wait(*w1)

    at_chip(r, chips)
    out[0] = dot(rows_of(held, r), flat(held_d), NN)


def project(coord, acts, wd):
    rows, model = acts[0].shape[-2:]
    shape = (2 * rows, wd.plan.width)
    return chip_kernel(
        functools.partial(project_body, len(acts), wd.plan),
        [coord, *acts, *arrays(wd)],
        [SMEM] + [ANY] * (len(acts) + len(arrays(wd))),
        [struct((4,) + shape, f32)],
        [by_chip(shape)],
        [held_tokens(acts), held_weight(wd)],
        10 + copies_of(wd),
        16 * rows * model * wd.plan.width,
    )[0]


def feed_body(tokens, f_u, f_g, coord, gh, *refs):
    acts, refs = refs[:tokens], refs[tokens:]
    wu, refs = refs[: f_u.count], refs[f_u.count :]
    wg, refs = refs[: f_g.count], refs[f_g.count :]
    hidden_out, up_out, gate_out, rest, diag, keep = refs[:6]
    held, held_u, held_g, store, up, gate, sems = refs[6:]
    load, r = Loader(sems), pl.program_id(0)
    w1 = load.weight(wu, f_u, held_u, coord)
    w2 = load.weight(wg, f_g, held_g, coord)
    chips = load.tokens(acts, held, coord)
    sends = send_copies(load, store, rest, diag)

    @pl.when(r == 0)
    def _():
        start(*w1, *chips[0], *w2)
        for i in range(1, 4):
            start(*chips[i])
        wait(*w1)

    at_chip(r, chips)
    x = rows_of(held, r)
    up[...] = dot(x, flat(held_u), NN)

    @pl.when(r == 0)
    def _():
        wait(*w2)

    gate[...] = dot(x, flat(held_g), NN)
    step = 16

    def chunk(i, carry):
        at = pl.ds(pl.multiple_of(i * step, step), step)
        u, g, e = up[at, :], gate[at, :], gh[0, at, :]
        c = 0.7978845608028654
        square = g * g
        t = jnp.tanh(c * g * (1.0 + 0.044715 * square))
        half = 0.5 * (1.0 + t)
        gelu = g * half
        slope = half + (0.5 * c) * g * (1.0 - t * t) * (1.0 + (3 * 0.044715) * square)
        hidden_out[0, at, :] = (gelu * u).astype(bf16)
        up_out[0, at, :] = (e * gelu).astype(bf16)
        gate_out[0, at, :] = (e * u * slope).astype(bf16)
        return carry

    lax.fori_loop(0, up.shape[0] // step, chunk, 0, unroll=4)
    partial_rows([up_out[0], gate_out[0]], [held_u, held_g], r, keep, store)
    at_chip_start(r, sends)


def feed_forward(coord, gh, acts, wu, wg):
    rows, model = acts[0].shape[-2:]
    n = wu.plan.width
    outs, out_specs = partial_outs(rows, model)
    outs = [struct((4, 2 * rows, n), bf16)] * 3 + outs
    return chip_kernel(
        functools.partial(feed_body, len(acts), wu.plan, wg.plan),
        [coord, gh, *acts, *arrays(wu, wg)],
        [SMEM, by_chip((2 * rows, n))] + [ANY] * (len(acts) + len(arrays(wu, wg))),
        outs,
        [by_chip((2 * rows, n))] * 3 + out_specs,
        [
            held_tokens(acts),
            held_weight(wu),
            held_weight(wg),
            pltpu.VMEM((4, rows, model), bf16),
        ]
        + [pltpu.VMEM((2 * rows, n), f32)] * 2,
        14 + copies_of(wu, wg),
        64 * rows * model * n,
    )


def back_body(plans, whole, coord, *refs):
    count = len(plans)
    weights = []
    grads, refs = refs[:count], refs[count:]
    for plan in plans:
        weights.append(refs[: plan.count])
        refs = refs[plan.count :]
    load, r = Loader(refs[-1]), pl.program_id(0)
    if whole:
        result, helds, keep, store = refs[0], refs[1 : 1 + count], refs[-3], refs[-2]
    else:
        rest, diag, keep, helds, store = *refs[:3], refs[3 : 3 + count], refs[-2]
    copies = [load.weight(w, p, h, coord) for w, p, h in zip(weights, plans, helds)]

    @pl.when(r == 0)
    def _():
        for c in copies:
            start(*c)
        for c in copies:
            wait(*c)

    if not whole:
        sends = send_copies(load, store, rest, diag)
        partial_rows([g[0] for g in grads], helds, r, keep, store)
        at_chip_start(r, sends)
        return
    sends = []
    for i in range(4):
        at = 2 * (i ^ coord[2])
        sends.append(
            (
                load.copy(keep.at[i], result.at[at + coord[3]]),
                load.copy(store.at[i], result.at[at + (1 ^ coord[3])]),
            )
        )
    partial_rows([g[0] for g in grads], helds, r, keep.at[pl.ds(r, 1)], store)
    for i in range(4):
        pl.when(r == i)(functools.partial(start, *sends[i]))

    @pl.when(r == 3)
    def _():
        for c in sends:
            wait(*c)


def back(coord, grads, weights, whole=False):
    length = grads[0].shape[1]
    rows = length // 2
    held = held_weight(weights[0])
    model = held.shape[0] * held.shape[1]
    outs, out_specs = partial_outs(rows, model)
    store = pltpu.VMEM((4, rows, model), bf16)
    if whole:
        outs, out_specs = [struct((8, rows, model), bf16)], [ANY]
    return chip_kernel(
        functools.partial(back_body, tuple(w.plan for w in weights), whole),
        [coord, *grads, *arrays(*weights)],
        [SMEM] + [by_chip(g.shape[1:]) for g in grads] + [ANY] * len(arrays(*weights)),
        outs,
        out_specs,
        [held_weight(w) for w in weights] + [store] * (2 if whole else 1),
        8 + copies_of(*weights),
        8 * length * model * sum(g.shape[2] for g in grads),
    )


def attend_back_body(tokens, f_o, coord, mask, s, hat, scale, scores, q, k, v, *refs):
    acts, refs = refs[:tokens], refs[tokens:]
    wo, refs = refs[: f_o.count], refs[f_o.count :]
    gqk_out, gv_out, gs_out, held, held_o, dg, gr, sems = refs
    load, r = Loader(sems), pl.program_id(0)
    w1 = load.weight(wo, f_o, held_o, coord)
    chips = load.tokens(acts, held, coord)

    @pl.when(r == 0)
    def _():
        start(*w1, *chips[0], *chips[1], *chips[2], *chips[3])
        wait(*w1)

    at_chip(r, chips)
    dg[...] = dot(rows_of(held, r), flat(held_o), NN)
    rows, step = dg.shape[0], 16

    def chunk(i, carry):
        at = pl.ds(pl.multiple_of(i * step, step), step)
        e, x, v_s = dg[at, :], hat[0, at, :], s[0, at, :]
        gate = 1.0 / (1.0 + jnp.exp(-v_s))
        silu = v_s * gate
        gs_out[0, at, :] = (e * x * (gate + silu * (1.0 - gate))).astype(bf16)
        f = e * silu
        f = f - jnp.mean(f, axis=-1, keepdims=True) - x * jnp.mean(f * x, axis=-1, keepdims=True)
        gr[at, :] = (f * scale[0, at, :1]).astype(bf16)
        return carry

    lax.fori_loop(0, rows // step, chunk, 0, unroll=4)
    grad_retained = gr[...]
    gv_out[0] = dot(scores[0], grad_retained, TN).astype(bf16)
    raw = (dot(grad_retained, v[0], NT) * mask[0]).astype(bf16)
    size = q.shape[2]
    gqk_out[0, :, :size] = dot(raw, k[0], NN).astype(bf16)
    gqk_out[0, :, size:] = dot(raw, q[0], TN).astype(bf16)


def attend_back(coord, mask, s, hat, scale, scores, q, k, v, acts, wo):
    length, n = s.shape[1:]
    model = acts[0].shape[-1]
    blocks = [mask, s, hat, scale, scores, q, k, v]
    outs = [struct((4, length, 2 * q.shape[2]), bf16)] + [struct((4, length, n), bf16)] * 2
    return chip_kernel(
        functools.partial(attend_back_body, len(acts), wo.plan),
        [coord, *blocks, *acts, *arrays(wo)],
        [SMEM] + [by_chip(b.shape[1:]) for b in blocks] + [ANY] * (len(acts) + len(arrays(wo))),
        outs,
        [by_chip(o.shape[1:]) for o in outs],
        [
            held_tokens(acts),
            held_weight(wo),
            pltpu.VMEM((length, n), f32),
            pltpu.VMEM((length, n), bf16),
        ],
        10 + copies_of(wo),
        12 * length * model * n,
    )


def weight_grad_body(count, tokens, whole, coord, *refs):
    grads, refs = refs[:count], refs[count:]
    acts, refs = refs[:tokens], refs[tokens:]
    outs, held, sems = refs[:-2], refs[-2], refs[-1]
    load, i = Loader(sems), pl.program_id(0)
    chips = load.tokens(acts, held, coord)

    @pl.when(i == 0)
    def _():
        for c in chips:
            start(*c)
        for c in chips:
            wait(*c)

    width = held.shape[2] // 8
    j = i % 4
    if whole:
        column = ((i // 4 * 2 + i % 2) * 2 + i // 2 % 2) * width
    else:
        y = coord[1] ^ jnp.where(i < 4, 1, 0)
        zh = coord[0] ^ jnp.where(j < 2, 1, 0)
        column = ((zh * 2 + j % 2) * 2 + y) * width
    x = held[:, :, pl.ds(pl.multiple_of(column, width), width)]
    x = x.reshape(x.shape[0] * x.shape[1], width).T
    for n in range(count):
        g = grads[n][...]
        size = g.shape[2]
        out = dot(x, g.reshape(g.shape[0] * g.shape[1], size), NN).astype(bf16)
        if whole:
            outs[0][0, :, n * size : (n + 1) * size] = out
            continue
        pl.when(i < 4)(functools.partial(store_block, outs[2 * n], out))
        pl.when(i >= 4)(functools.partial(store_block, outs[2 * n + 1], out))


def store_block(ref, value):
    ref[0] = value


def weight_grads(coord, acts, grads, whole=False):
    rows, model = acts[0].shape[-2:]
    outs, out_specs = [], []
    width = sum(g.shape[2] for g in grads)
    for g in grads:
        shape = (4, model // 8, g.shape[2])
        outs += [struct(shape, bf16)] * 2
        out_specs += [
            pl.BlockSpec((1,) + shape[1:], lambda i: (jnp.minimum(i, 3), 0, 0)),
            pl.BlockSpec((1,) + shape[1:], lambda i: (jnp.maximum(i - 4, 0), 0, 0)),
        ]
    if whole:
        outs = [struct((8, model // 8, width), bf16)]
        out_specs = [pl.BlockSpec((1, model // 8, width), lambda i: (i, 0, 0))]
    moved = sum(a.size * 2 for a in acts) + sum(g.size * 2 for g in grads) + 2 * model * width
    got = pl.pallas_call(
        functools.partial(weight_grad_body, len(grads), len(acts), whole),
        grid=(8,),
        in_specs=[SMEM] + [pl.BlockSpec(memory_space=pltpu.VMEM)] * len(grads) + [ANY] * len(acts),
        out_specs=out_specs,
        out_shape=outs,
        scratch_shapes=[held_tokens(acts), pltpu.SemaphoreType.DMA((10,))],
        compiler_params=pltpu.CompilerParams(
            dimension_semantics=("arbitrary",), vmem_limit_bytes=VMEM_LIMIT
        ),
        cost_estimate=pl.CostEstimate(
            flops=16 * rows * model * width, bytes_accessed=moved, transcendentals=0
        ),
    )(coord, *grads, *acts)
    if whole:
        return got[0]
    return [(got[2 * i], got[2 * i + 1]) for i in range(len(grads))]


def place_body(parts, g, *outs):
    column = 0
    for (width, way), out in zip(parts, outs):
        value = g[0, :, column : column + width].astype(f32)
        out[...] = value.T if way == "r" else value
        column += width


def place(g, parts):
    rows = g.shape[1]
    outs, specs = [], []
    for width, way in parts:
        if way == "r":
            outs.append(struct((4 * width, rows), f32))
            specs.append(pl.BlockSpec((width, rows), lambda q: (q, 0)))
        else:
            outs.append(struct((rows, 4 * width), f32))
            specs.append(pl.BlockSpec((rows, width), lambda q: (0, q)))
    return pl.pallas_call(
        functools.partial(place_body, parts),
        grid=(4,),
        in_specs=[by_chip(g.shape[1:])],
        out_specs=specs,
        out_shape=outs,
        compiler_params=pltpu.CompilerParams(dimension_semantics=("arbitrary",)),
        cost_estimate=pl.CostEstimate(flops=0, bytes_accessed=6 * g.size, transcendentals=0),
    )(g)


def scatter_whole(g):
    zh, n = lax.axis_size("zh"), g.shape[2]
    if zh == 2:
        g = g.reshape(4, 4, -1, n)
    else:
        g = g.reshape(2, 2, 2, -1, n).transpose(0, 2, 1, 3, 4).reshape(zh, 2, 2, 2, -1, n)
        g = g.transpose(0, 2, 1, 3, 4, 5).reshape(2 * zh, 4, -1, n)
    g = lax.psum_scatter(g, ("zh", "y"), scatter_dimension=0, tiled=True)
    return g.reshape(4, -1, n)


def sum_everywhere(a):
    for axis in ("tensor",) + SPREAD:
        if lax.axis_size(axis) == 2:
            a = a + swap(a, axis)
        else:
            a = lax.psum(a, axis)
    return a


def local(
    tokens,
    segments,
    decay,
    norm1_gain,
    w_query,
    w_key,
    w_value,
    w_swish,
    w_out,
    norm2_gain,
    w_up,
    w_gate,
    w_down,
    cotangent,
):
    rows_q, width = w_query.shape[0], w_value.shape[1] // 4
    quarter = 2 * lax.axis_index("zl") + lax.axis_index("x")
    core = lax.axis_index("tensor")
    length = segments.shape[0]
    rows_each = tokens.shape[0]
    key_size = w_query.shape[1] // 4
    value_size = w_value.shape[1] // 4
    rate = take(decay, quarter, 0)

    ids = [jnp.zeros((), jnp.int32)] * 2
    if lax.axis_size("zh") == 2:
        ids = [lax.axis_index("zh"), lax.axis_index("y")]
    coord = jnp.stack(ids + [quarter, core]).astype(jnp.int32)
    clock, free = Clock(), Clock()
    at = clock.at
    rows_local = tokens.astype(f32)
    everyone = ("zl", "x", "tensor")

    pipe = WeightPipe()
    seg_x, seg_z = swap(segments, "x", "seg"), swap(segments, "zl", "seg")
    with jax.named_scope("seg"):
        seg_d = lax.ppermute(segments, GROUP, [(i, 3 - i) for i in range(4)])
    parts = (by_quarter(w) for w in (w_query, w_key, w_value))
    piece = group_exchange(beside(*parts))
    parts = beside(by_quarter(w_swish), by_quarter(w_out.T))

    clock.done(piece, parts)
    unit_qkv = pipe.step(clock, piece, "qkv")
    piece = group_exchange(at(parts))
    normed_local = layer_norm(rows_local, norm1_gain).astype(bf16)
    normed = [lax.all_gather(at(normed_local), everyone, axis=0)]
    segs = jnp.stack([segments, seg_x, seg_z, seg_d])
    segs = jnp.where(core == 0, segs, jnp.roll(segs, length // 2, 1))
    position = (jnp.arange(length, dtype=jnp.int32) + core * rows_each) % length
    offset = position[:, None] - position[None, :]
    allowed = (offset >= 0)[None] & (segs[:, :, None] == segs[:, None, :])
    distance = jnp.maximum(offset, 0).astype(f32)
    decay_mask = jnp.where(allowed, jnp.exp(-rate * distance)[None], 0.0)
    parts = beside(by_quarter(at(w_up)), by_quarter(at(w_gate)), by_quarter(at(w_down).T))

    clock.done(piece, parts, decay_mask, *pipe.moved)
    unit_so = pipe.step(clock, piece, "so")
    piece = group_exchange(at(parts))
    full_qk, full_value = unit_qkv.weight(0, width), unit_qkv.weight(width, width)
    query, key, values, scores, hat, scale = attend(
        at(coord), decay_mask, normed, full_qk, full_value, key_size
    )

    clock.done(query, piece, *pipe.moved)
    grad_rows = [lax.all_gather(at(cotangent), everyone, axis=0)]
    unit_ug = pipe.step(clock, piece[:, :, : 2 * width], "ug")
    full_swish, full_out = unit_so.weight(0, width), unit_so.weight(width, width)
    swish_in, gated, *partial = branch(at(coord), hat, normed, full_swish, full_out)
    clock.done(*pipe.moved, *partial)
    unit_d = pipe.step(clock, piece[:, :, 2 * width :], "d")
    scatter = Scatter(*partial, "branch", clock)
    scatter.relay(free)
    clock.done(*scatter.second)
    scatter.send(clock)
    clock.done(*scatter.last, *pipe.moved)
    middle = rows_local + scatter.finish(clock)
    normed_two_local = layer_norm(middle, norm2_gain).astype(bf16)
    gather = Gather(clock, normed_two_local, "two", True)
    far_y = pipe.finish(clock)
    clock.done(*far_y, *gather.first)
    gather.second(clock)
    full_up, full_gate = unit_ug.weight(0, width), unit_ug.weight(width, width)
    full_down = unit_d.weight(0, width)
    grad_hidden = project(at(coord), grad_rows, full_down)
    clock.done(grad_hidden, *gather.held)
    normed_two = gather.finish(clock)
    hidden, grad_up_rows, grad_gate_rows, *partial = feed_forward(
        at(coord), grad_hidden, normed_two, full_up, full_gate
    )

    scatter = Scatter(*partial, "back_two", free)
    clock.done(scatter.diag)
    scatter.relay(clock)
    (g_down,) = weight_grads(at(coord), grad_rows, [hidden])
    g_down = WeightGrad(g_down, "down")
    clock.done(g_down.send, *scatter.second)
    scatter.send(clock)
    g_down.to_y(clock)
    g_up, g_gate = weight_grads(at(coord), normed_two, [grad_up_rows, grad_gate_rows])
    g_up, g_gate = WeightGrad(g_up, "up"), WeightGrad(g_gate, "gate")
    clock.done(g_up.send, g_down.y, *scatter.last)
    back_two_local = scatter.finish(clock)
    _, norm_two_pull = jax.vjp(layer_norm, middle, norm2_gain)
    grad_mid_norm, grad_norm2_local = norm_two_pull(back_two_local)
    grad_middle = cotangent.astype(f32) + grad_mid_norm
    grad_branch_local = grad_middle.astype(bf16)

    clock.done(grad_branch_local)
    gather = Gather(clock, grad_branch_local, "gb", True)
    g_down.to_zh(clock)
    g_up.to_y(clock)
    clock.done(g_down.zh, g_up.y, *gather.first)
    gather.second(clock)
    g_gate.to_y(clock)
    (feed,) = back(at(coord), [hidden], [full_down], True)
    clock.done(feed, *gather.held)
    grad_branch = gather.finish(clock)
    feed = lax.psum_scatter(at(feed), everyone, scatter_dimension=0, tiled=True)
    g_up.to_zh(clock)
    grad_qk, grad_values, grad_swish_in = attend_back(
        at(coord),
        decay_mask,
        swish_in,
        hat,
        scale,
        scores,
        query,
        key,
        values,
        grad_branch,
        full_out,
    )
    clock.done(grad_qk, g_up.zh, g_gate.y)
    g_gate.to_zh(clock)
    (g_out,) = weight_grads(at(coord), grad_branch, [gated])
    g_out = WeightGrad(g_out, "out")
    clock.done(g_out.send)
    g_out.to_y(clock)
    (g_swish,) = weight_grads(at(coord), normed, [grad_swish_in])
    g_swish = WeightGrad(g_swish, "swish")
    clock.done(g_swish.send, g_gate.zh)
    g_value, g_qk = weight_grads(at(coord), normed, [grad_values, grad_qk])
    g_value, g_qk = WeightGrad(g_value, "value"), WeightGrad(g_qk, "qk")
    clock.done(g_value.send, g_out.y)
    g_out.to_zh(clock)
    g_swish.to_y(clock)
    partial = back(
        at(coord), [grad_qk, grad_values, grad_swish_in], [full_qk, full_value, full_swish]
    )
    clock.done(g_out.zh, g_swish.y, *partial)
    g_swish.to_zh(clock)
    g_value.to_y(clock)
    scatter = Scatter(*partial, "back_one", clock)
    clock.done(scatter.diag)
    scatter.relay(clock, True)
    clock.done(*scatter.second)
    scatter.send(clock)
    clock.done(g_swish.zh, g_value.y)
    g_value.to_zh(clock)
    g_qk.to_y(clock)
    grad_ff = group_exchange(beside(g_up.sum(clock), g_gate.sum(clock), g_down.sum(clock)))
    clock.done(g_value.zh, g_qk.y)
    g_qk.to_zh(clock)
    clock.done(*scatter.last)
    back_one_local = scatter.finish(clock)
    grad_os = group_exchange(after(beside(g_out.sum(clock), g_swish.sum(clock)), grad_ff))
    grad_up, grad_gate, grad_down = place(at(grad_ff), ((width, "c"), (width, "c"), (width, "r")))
    mixed = (middle + feed.reshape(middle.shape).astype(f32)).astype(bf16)
    _, norm_one_pull = jax.vjp(layer_norm, rows_local, norm1_gain)
    grad_tok_norm, grad_norm1_local = norm_one_pull(back_one_local)
    grad_tokens = grad_middle + grad_tok_norm
    grad_norm1, grad_norm2 = sum_everywhere(
        after(jnp.stack([grad_norm1_local, grad_norm2_local]), g_qk.zh)
    )
    clock.done(g_qk.zh, grad_os, grad_up, mixed, grad_norm1, grad_tokens)
    grad_qkv = group_exchange(beside(g_qk.sum(clock), g_value.sum(clock)))
    grad_out, grad_swish = place(at(grad_os), ((width, "r"), (width, "c")))
    parts = ((key_size, "c"), (key_size, "c"), (width, "c"))
    grad_query, grad_key, grad_value = place(grad_qkv, parts)

    return (
        mixed,
        grad_tokens,
        grad_norm1,
        grad_query,
        grad_key,
        grad_value,
        grad_swish,
        grad_out,
        grad_norm2,
        grad_up,
        grad_gate,
        grad_down,
    )


def solution(mesh):
    dp, tensor = mesh.shape["dp"], mesh.shape["tensor"]
    grid = Mesh(mesh.devices.reshape(dp // 8, 2, 2, 2, tensor), SPREAD + ("tensor",))
    rows = P(SPREAD + ("tensor",), None)
    rows_split = P(SPREAD, "tensor")
    columns_split = P("tensor", SPREAD)
    return jax.shard_map(
        local,
        mesh=grid,
        in_specs=(
            rows,
            P(SPREAD),
            P("tensor"),
            P(),
            rows_split,
            rows_split,
            rows_split,
            rows_split,
            columns_split,
            P(),
            rows_split,
            rows_split,
            columns_split,
            rows,
        ),
        out_specs=(
            rows,
            rows,
            P(),
            rows_split,
            rows_split,
            rows_split,
            rows_split,
            columns_split,
            P(),
            rows_split,
            rows_split,
            columns_split,
        ),
        check_vma=False,
    )
```
